32 devices in a mesh: dp: 8 (over z, x), tensor: 4 (over y, core).
Axes of the slice: x: 2, y: 2, z: 4, core: 2. Of those that a mesh axis runs over, the one named last changes fastest.
Arguments:
- tokens: bfloat16 [16384, 2048], P('dp'), may hold values from -43 to 43
- cotangent: bfloat16 [16384, 2048], P('dp'), may hold values from -12 to 12
- doc_ids: int32 [16, 1024], P('dp'), may hold values from 0 to 7, never falling along the last dimension, each value on 1 to 512 neighbouring positions
- tile_slots: int32 [4, 384], P('tensor'), may hold values from 0 to 383, each once within a row
- matrix_tiles: float32 [4, 384, 128, 128], P('tensor', 'dp'), may hold values from -0.125 to 0.125
- left_stats: float32 [4, 384, 128, 128], P('tensor', 'dp'), may hold values from -2097152 to 4194304
- right_stats: float32 [4, 384, 128, 128], P('tensor', 'dp'), may hold values from -2097152 to 4194304
- left_roots: float32 [4, 384, 128, 128], P('tensor', 'dp'), may hold values from -1 to 2
- right_roots: float32 [4, 384, 128, 128], P('tensor', 'dp'), may hold values from -1 to 2
- side_weight: float32 [2048, 320], P('dp'), may hold values from -0.125 to 0.125
- side_moment: float32 [2048, 320], P('dp'), may hold values from -24 to 24
- side_second: float32 [2048, 320], P('dp'), may hold values from 81.92 to 327.68
- vector_params: float32 [4, 7024], P('tensor'), may hold values from -7 to 5
- vector_moment: float32 [4, 7024], P('tensor'), may hold values from -40 to 40
- vector_second: float32 [4, 7024], P('tensor'), may hold values from 212.992 to 851.968
Outputs:
- mixed: bfloat16 [16384, 2048], P('dp')
- input_grad: float32 [16384, 2048], P('dp')
- tile_grads: float32 [4, 384, 128, 128], P('tensor', 'dp')
- left_new: float32 [4, 384, 128, 128], P('tensor', 'dp')
- right_new: float32 [4, 384, 128, 128], P('tensor', 'dp')
- tiles_new: float32 [4, 384, 128, 128], P('tensor', 'dp')
- tiles_copy: bfloat16 [4, 384, 128, 128], P('tensor', 'dp')
- side_moment_new: float32 [2048, 320], P('dp')
- side_second_new: float32 [2048, 320], P('dp')
- side_new: float32 [2048, 320], P('dp')
- vector_moment_new: float32 [4, 7024], P('tensor')
- vector_second_new: float32 [4, 7024], P('tensor')
- vector_new: float32 [4, 7024], P('tensor')
The draws below stay inside these ranges and needn't reach their ends.
Inputs may be any that keep to these rules, and one draw needn't show every extreme that they name: `doc_ids`: within each sequence the document number starts at 0, never falls and rises by one where a document starts; no document is longer than 512 positions. For each tensor index t, a permutation: tile k of t is kept in slot tile_slots[t, k] of matrix_tiles, of the statistics, of the roots and of the tile outputs.
All inputs are finite; a program needn't handle non-finite values.
Results may differ from the reference program's by a relative error of at most 0.0045.
The reference program's roundings to bfloat16 on the way count: a program that leaves them out, or rounds other values in their place, can miss the bound.
Values may be sent and summed in bfloat16 or wider, within the bound.
No kernel may reach another device: no remote copies, remote signals or barrier semaphores. Data moves between devices by JAX's collectives and lax.ppermute only.
A program may use at most 320 MiB of HBM per device.

```python
import math
import jax
import jax.numpy as jnp
import numpy as np
from jax import lax

D = 2048
HEADS = 64
NS = 128
CONV = 4
SSD_BLOCK = 256
SEQ = 1024
DOCS = 8
TILE = 128
STEP = 10
DI = 4096
DI_T = 1024
HEADS_T = 16
D_T = 512
BC_T = 64
SIDE = 320
NT = 384
RV = 7024
NSEQ = 16
TOKENS = 16384
N_TENSOR = 4


def rising_rows(count, top):
    return 1.0 + (top - 1.0) * jnp.arange(count, dtype=jnp.float32) / (count - 1)


def draw_tokens(key, part):
    key = jax.random.fold_in(key, 3)
    key_base, key_col, key_row = jax.random.split(key, 3)
    columns = jnp.exp(jax.random.uniform(key_col, (D,), minval=math.log(0.4), maxval=math.log(2.5)))
    jitter = jnp.exp(jax.random.uniform(key_row, (TOKENS, 1), minval=-0.35, maxval=0.35))
    base = jnp.clip(jax.random.normal(key_base, (TOKENS, D)), -4.0, 4.0) * rising_rows(TOKENS, 3.0)[:, None]
    return (base * jitter * columns[None, :]).astype(jnp.bfloat16)


def draw_cotangent(key, part):
    key = jax.random.fold_in(key, 4)
    return (jnp.clip(jax.random.normal(key, (TOKENS, D)), -4.0, 4.0) * rising_rows(TOKENS, 3.0)[:, None]).astype(jnp.bfloat16)


def spd_tiles(key, scale, top):
    key_diag, key_off = jax.random.split(key)
    diagonal = jnp.exp(jax.random.uniform(key_diag, (N_TENSOR, NT, TILE), minval=0.0, maxval=math.log(top)))
    noise = jnp.clip(jax.random.normal(key_off, (N_TENSOR, NT, TILE, TILE)), -4.0, 4.0) * (0.35 / math.sqrt(TILE))
    mirror = (noise + jnp.swapaxes(noise, -1, -2)) * 0.7071
    identity = jnp.eye(TILE, dtype=jnp.float32)
    return scale * (diagonal[..., None] * identity + mirror * (1.0 - identity))


def draw_left_stats(key, part):
    key = jax.random.fold_in(key, 5)
    return spd_tiles(key, 0.25 * TILE * TOKENS, 4.0)


def draw_right_stats(key, part):
    key = jax.random.fold_in(key, 6)
    return spd_tiles(key, 0.25 * TILE * TOKENS, 4.0)


def draw_left_roots(key, part):
    key = jax.random.fold_in(key, 7)
    return spd_tiles(key, (0.5 * TILE * TOKENS) ** (-0.25), 2.0)


def draw_right_roots(key, part):
    key = jax.random.fold_in(key, 8)
    return spd_tiles(key, (0.5 * TILE * TOKENS) ** (-0.25), 2.0)


def draw_vector_params(key, part):
    key = jax.random.fold_in(key, 11)
    keys = jax.random.split(key, 9)
    channel = (jnp.arange(N_TENSOR * DI_T, dtype=jnp.float32) / (N_TENSOR * DI_T - 1)).reshape(N_TENSOR, 1, DI_T)
    kernel = jnp.clip(jax.random.normal(keys[0], (N_TENSOR, CONV, DI_T)), -4.0, 4.0) * 0.35 * (1.0 + 2.0 * channel)
    offset = jax.random.uniform(keys[1], (N_TENSOR, DI_T), minval=-0.5, maxval=0.5)
    gate_gain = jax.random.uniform(keys[2], (N_TENSOR, DI_T), minval=0.5, maxval=1.5)
    log_rate = jax.random.uniform(keys[3], (N_TENSOR, HEADS_T), minval=0.0, maxval=2.77)
    skip_gain = jax.random.uniform(keys[4], (N_TENSOR, HEADS_T), minval=0.5, maxval=1.5)
    dt_offset = jax.random.uniform(keys[5], (N_TENSOR, HEADS_T), minval=-6.9, maxval=-2.3)
    pre_gain = jax.random.uniform(keys[6], (N_TENSOR, D_T), minval=0.5, maxval=1.5)
    bc_kernel = jnp.clip(jax.random.normal(keys[7], (N_TENSOR, CONV * BC_T)), -4.0, 4.0) * 0.5
    bc_offset = jax.random.uniform(keys[8], (N_TENSOR, BC_T), minval=-0.5, maxval=0.5)
    return jnp.concatenate([kernel.reshape(N_TENSOR, CONV * DI_T), offset, gate_gain, log_rate, skip_gain, dt_offset, pre_gain, bc_kernel, bc_offset], axis=1)


def steps_of(rng, dims, shards, low, largest):
    def one(axis_at, shards_of):
        heights = jax.random.uniform(jax.random.fold_in(jax.random.fold_in(rng, 6), axis_at), (shards_of,), jnp.float32, low / len(shards), largest / len(shards))
        return jnp.repeat(jnp.exp(heights), dims[axis_at] // shards_of).reshape((-1,) + (1,) * (len(dims) - axis_at - 1))

    level = one(*shards[0])
    for cut in shards[1:]:
        level = level * one(*cut)
    return level


def profile(count, total, limit, skew):
    portions = [(1 << 20) // math.isqrt(rank ** skew) + 1 for rank in range(2, count + 1)]
    rest, counts = total - limit - (count - 1), [1] * (count - 1)
    while rest > 0:
        movable = [i for i in range(count - 1) if counts[i] < limit]
        mass, remaining = sum([portions[i] for i in movable]), rest
        for i in movable:
            addition = min(limit - counts[i], max(1, remaining * portions[i] // mass), rest)
            counts[i] = counts[i] + addition
            rest = rest - addition
    return np.array([limit] + counts)


def uneven(own_key, count, total, reach, lean):
    if count == 2:
        one = jax.random.randint(own_key, (), max(1, total - reach), min(reach, total - 1) + 1)
        return jnp.stack([one, total - one])
    sizes = jnp.asarray(profile(count, total, reach, lean), jnp.int32)
    twos = (count - 1) // 2
    donor, sink = sizes[1:1 + 2 * twos:2], sizes[2:2 + 2 * twos:2]
    slack = jnp.minimum(donor - 1, reach - sink)
    moved = jax.random.randint(jax.random.fold_in(own_key, 1), (twos,), 0, 1 << 20) % (slack + 1)
    sizes = sizes.at[1:1 + 2 * twos:2].set(donor - moved).at[2:2 + 2 * twos:2].set(sink + moved)
    return sizes[jax.random.permutation(jax.random.fold_in(own_key, 2), count)]


def gaussian(key, dims, deviation, limit, cuts=(), kind=jnp.bfloat16):
    entries = jax.random.normal(key, dims, jnp.float32) * deviation
    if len(cuts) > 0:
        entries = steps_of(key, dims, cuts, -0.22, 0.18) * entries
    return jnp.clip(entries, min=-limit, max=limit).astype(kind)


def setup_inputs(seed: int = 0) -> dict:
    key_of = jax.random.split(jax.random.key(seed), 16)
    return {
        "tokens": draw_tokens(jax.random.fold_in(key_of[15], 71), 0),
        "cotangent": draw_cotangent(jax.random.fold_in(key_of[15], 71), 0),
        "doc_ids": jax.vmap(lambda own: jnp.searchsorted(jnp.cumsum(uneven(own, DOCS, SEQ, SEQ // 2, 2)), jnp.arange(SEQ), side="right"))(jax.random.split(key_of[2], NSEQ)).reshape((NSEQ, SEQ)).astype(jnp.int32),
        "tile_slots": jax.vmap(lambda own: jax.random.permutation(own, NT))(jax.random.split(key_of[3], N_TENSOR)).reshape((N_TENSOR, NT)).astype(jnp.int32),
        "matrix_tiles": gaussian(key_of[4], (N_TENSOR, NT, TILE, TILE), D ** -0.5, 0.125, ((0, 4), (1, 8)), jnp.float32),
        "left_stats": draw_left_stats(jax.random.fold_in(key_of[15], 71), 0),
        "right_stats": draw_right_stats(jax.random.fold_in(key_of[15], 71), 0),
        "left_roots": draw_left_roots(jax.random.fold_in(key_of[15], 71), 0),
        "right_roots": draw_right_roots(jax.random.fold_in(key_of[15], 71), 0),
        "side_weight": gaussian(key_of[9], (D, SIDE), D ** -0.5, 0.125, ((0, 8),), jnp.float32),
        "side_moment": gaussian(key_of[10], (D, SIDE), (0.033 * TOKENS ** 0.5), 24.0, ((0, 8),), jnp.float32),
        "side_second": jnp.clip(jnp.exp(math.log(327.68) - 1.3862944 * jax.random.uniform(key_of[11], (D, SIDE), jnp.float32) ** steps_of(key_of[11], (D, SIDE), ((0, 8),), -0.2, 0.2)), 81.92, 327.68),
        "vector_params": draw_vector_params(jax.random.fold_in(key_of[15], 71), 0),
        "vector_moment": gaussian(key_of[13], (N_TENSOR, RV), (0.055 * TOKENS ** 0.5), 40.0, ((0, 4),), jnp.float32),
        "vector_second": jnp.clip(jnp.exp(math.log(851.968) - 1.3862944 * jax.random.uniform(key_of[14], (N_TENSOR, RV), jnp.float32) ** steps_of(key_of[14], (N_TENSOR, RV), ((0, 4),), -0.2, 0.2)), 212.992, 851.968),
    }


EPS = 1e-05
HIGH = lax.Precision.HIGHEST
STAT_DECAY = 0.5
LR_MAT = 0.25
LR_SIDE = 0.02
LR_VEC = 0.25
BETA_ONE = 0.9
BETA_TWO = 0.95
ADAM_EPS = 1e-08
DECAY_WD = 0.1

@jax.custom_vjp
def low(v):
    return lax.optimization_barrier(v.astype(jnp.bfloat16)).astype(jnp.float32)

@jax.custom_vjp
def low_back(v):
    return v

def low_keep(v):
    return (low(v), None)

def low_pass(kept, grad):
    return (grad,)

def back_keep(v):
    return (v, None)

def back_low(kept, grad):
    return (low(grad),)
low.defvjp(low_keep, low_pass)
low_back.defvjp(back_keep, back_low)

def matmul(left, right):
    return jnp.dot(left, right, precision=HIGH, preferred_element_type=jnp.float32)

def segment_bounds(di_local, heads_local, model_local, bc_local, tap_count):
    widths = [tap_count * di_local, di_local, di_local, heads_local, heads_local, heads_local, model_local, tap_count * bc_local, bc_local]
    bounds = [0]
    for item in widths:
        bounds.append(bounds[-1] + item)
    return bounds

def causal_conv(values, kernel, offsets, documents):
    tap_count = kernel.shape[0]
    seq_len = values.shape[1]
    padded = jnp.pad(values, ((0, 0), (tap_count - 1, 0), (0, 0)))
    doc_pad = jnp.pad(documents, ((0, 0), (tap_count - 1, 0)), constant_values=-1)
    summed = jnp.zeros_like(values) + offsets
    for k in range(tap_count):
        matches = (doc_pad[:, k:k + seq_len] == documents)[:, :, None]
        summed = summed + kernel[k] * jnp.where(matches, padded[:, k:k + seq_len], 0.0)
    return summed

def block_scan(activated, step_sizes, decay_rate, in_states, out_states, segment):
    length = activated.shape[0]
    blocks = length // SSD_BLOCK
    head_count = activated.shape[1]
    x_blocks = activated.reshape(blocks, SSD_BLOCK, head_count, -1)
    dt_blocks = step_sizes.reshape(blocks, SSD_BLOCK, head_count)
    b_blocks = in_states.reshape(blocks, SSD_BLOCK, -1)
    c_blocks = out_states.reshape(blocks, SSD_BLOCK, -1)
    doc_blocks = segment.reshape(blocks, SSD_BLOCK)
    before = jnp.concatenate([jnp.full((1,), -1, jnp.int32), doc_blocks[:-1, -1].astype(jnp.int32)])
    positions = jnp.arange(SSD_BLOCK)
    causal_ok = positions[:, None] >= positions[None, :]

    def advance(carry_state, block):
        span_x, span_dt, span_b, span_c, span_doc, prev_doc = block
        cumulative = jnp.cumsum(span_dt * decay_rate, axis=0)
        allowed = (causal_ok & (span_doc[:, None] == span_doc[None, :]))[:, :, None]
        spread = cumulative[:, None, :] - cumulative[None, :, :]
        decays = jnp.where(allowed, jnp.exp(jnp.where(allowed, spread, 0.0)), 0.0)
        scores = jnp.dot(span_c, span_b.T, precision=HIGH, preferred_element_type=jnp.float32)
        weights = scores[:, :, None] * decays * span_dt[None, :, :]
        output = jnp.einsum('tsh,shp->thp', weights, span_x, precision=HIGH)
        carried = jnp.where((span_doc == prev_doc)[:, None], jnp.exp(cumulative), 0.0)
        output = output + jnp.einsum('tn,hnp->thp', span_c, carry_state, precision=HIGH) * carried[:, :, None]
        last_cum = cumulative[-1]
        tail_ok = (span_doc == span_doc[-1])[:, None]
        tail_decay = jnp.where(tail_ok, jnp.exp(jnp.where(tail_ok, last_cum[None, :] - cumulative, 0.0)), 0.0)
        new_part = jnp.einsum('sn,shp->hnp', span_b, span_x * (tail_decay * span_dt)[:, :, None], precision=HIGH)
        keep_decay = jnp.where(span_doc[-1] == prev_doc, jnp.exp(last_cum), 0.0)
        return (keep_decay[:, None, None] * carry_state + new_part, output)
    initial = jnp.zeros((head_count, in_states.shape[1], activated.shape[2]), jnp.float32)
    _, outputs = lax.scan(jax.checkpoint(advance), initial, (x_blocks, dt_blocks, b_blocks, c_blocks, doc_blocks, before))
    return outputs.reshape(length, head_count, -1)

def one_sequence(items, decay_rate):
    seq_x, seq_dt, seq_states, seq_doc = items
    half_width = seq_states.shape[1] // 2
    head_count = decay_rate.shape[0]
    shaped = seq_x.reshape(seq_x.shape[0], head_count, -1)
    return block_scan(shaped, seq_dt, decay_rate, seq_states[:, :half_width], seq_states[:, half_width:], seq_doc)

def mixer(x_proj, dt_raw, bc_act, conv_kernel, conv_offset, log_rate, skip_gain, dt_offset, documents):
    sequences = documents.shape[0]
    width = x_proj.shape[1]
    row_count = x_proj.shape[0]
    head_count = log_rate.shape[0]
    conv_out = causal_conv(x_proj.reshape(sequences, -1, width), conv_kernel, conv_offset, documents)
    activated = jax.nn.silu(conv_out)
    step_sizes = jax.nn.softplus(dt_raw + dt_offset).reshape(sequences, -1, head_count)
    decay_rate = -jnp.exp(log_rate)
    states = bc_act.reshape(sequences, -1, bc_act.shape[1])
    checked = jax.checkpoint(one_sequence)
    scanned = lax.map(lambda items: checked(items, decay_rate), (activated, step_sizes, states, documents))
    flat_act = activated.reshape(row_count, width)
    return scanned.reshape(row_count, width) + jnp.repeat(skip_gain, width // head_count) * flat_act

def unpack(packed):
    ranks = packed.shape[0]
    bounds = segment_bounds(DI_T, HEADS_T, D_T, BC_T, CONV)

    def segment_of(index):
        return packed[:, bounds[index]:bounds[index + 1]]
    conv_kernel = segment_of(0).reshape(ranks, CONV, DI_T).transpose(1, 0, 2).reshape(CONV, DI)
    bc_kernel = segment_of(7).reshape(ranks, CONV, BC_T).transpose(1, 0, 2).reshape(CONV, 2 * NS)
    return (conv_kernel, segment_of(1).reshape(DI), segment_of(2).reshape(DI), segment_of(3).reshape(HEADS), segment_of(4).reshape(HEADS), segment_of(5).reshape(HEADS), segment_of(6).reshape(D), bc_kernel, segment_of(8).reshape(2 * NS))

def forward(residual, tiles, side, packed, documents):
    copies = low(tiles)
    row_tiles = D // TILE
    col_tiles = DI_T // TILE
    per_block = row_tiles * col_tiles
    ranks = copies.shape[0]
    w_gate = copies[:, :per_block].reshape(ranks, row_tiles, col_tiles, TILE, TILE).transpose(1, 3, 0, 2, 4).reshape(D, DI)
    w_input = copies[:, per_block:2 * per_block].reshape(ranks, row_tiles, col_tiles, TILE, TILE).transpose(1, 3, 0, 2, 4).reshape(D, DI)
    w_output = copies[:, 2 * per_block:].reshape(ranks, col_tiles, row_tiles, TILE, TILE).transpose(0, 1, 3, 2, 4).reshape(DI, D)
    conv_kernel, conv_offset, gate_gain, log_rate, skip_gain, dt_offset, pre_gain, bc_kernel, bc_offset = unpack(packed)
    inverse = lax.rsqrt(lax.optimization_barrier(jnp.mean(residual * residual, axis=1, keepdims=True)) + EPS)
    normed = low(residual * inverse * pre_gain)
    gate_pre = low_back(matmul(normed, w_gate))
    x_proj = low_back(matmul(normed, w_input))
    side_out = low_back(matmul(normed, low(side)))
    sequences = documents.shape[0]
    bc_conv = causal_conv(side_out[:, :2 * NS].reshape(sequences, -1, 2 * NS), bc_kernel, bc_offset, documents)
    bc_act = jax.nn.silu(bc_conv).reshape(-1, 2 * NS)
    ssd = mixer(x_proj, side_out[:, 2 * NS:], bc_act, conv_kernel, conv_offset, log_rate, skip_gain, dt_offset, documents)
    gated = ssd * jax.nn.silu(gate_pre)
    hidden = low(gated * lax.rsqrt(lax.optimization_barrier(jnp.mean(gated * gated, axis=1, keepdims=True)) + EPS) * gate_gain)
    return residual + matmul(hidden, w_output)

def adam_update(weight, moment, second, gradient, learn_rate):
    moment_new = BETA_ONE * moment + (1.0 - BETA_ONE) * gradient
    second_new = BETA_TWO * second + (1.0 - BETA_TWO) * gradient * gradient
    corrected = moment_new / (1.0 - BETA_ONE ** STEP)
    scaled = jnp.sqrt(second_new / (1.0 - BETA_TWO ** STEP)) + ADAM_EPS
    return (moment_new, second_new, weight - learn_rate * (corrected / scaled + DECAY_WD * weight))

def reference(tokens, cotangent, doc_ids, tile_slots, matrix_tiles, left_stats, right_stats, left_roots, right_roots, side_weight, side_moment, side_second, vector_params, vector_moment, vector_second):
    residual = tokens.astype(jnp.float32)
    ordered = jax.vmap(lambda tile_set, slot_map: tile_set[slot_map])(matrix_tiles, tile_slots)

    def forward_pass(res_in, tiles_in, side_in, packed_in):
        return forward(res_in, tiles_in, side_in, packed_in, doc_ids)
    result, pullback = jax.vjp(forward_pass, residual, ordered, side_weight, vector_params)
    input_grad, ordered_grads, side_grad, vector_grad = pullback(cotangent.astype(jnp.float32))
    tile_grads = jax.vmap(lambda grads, slot_map: jnp.zeros_like(grads).at[slot_map].set(grads))(ordered_grads, tile_slots)
    gram_left = jnp.einsum('tkab,tkcb->tkac', tile_grads, tile_grads, precision=HIGH)
    gram_right = jnp.einsum('tkba,tkbc->tkac', tile_grads, tile_grads, precision=HIGH)
    left_new = STAT_DECAY * left_stats + (1.0 - STAT_DECAY) * gram_left
    right_new = STAT_DECAY * right_stats + (1.0 - STAT_DECAY) * gram_right
    shaped = jnp.einsum('tkab,tkbc->tkac', left_roots, tile_grads, precision=HIGH)
    shaped = jnp.einsum('tkab,tkbc->tkac', shaped, right_roots, precision=HIGH)
    tiles_new = matrix_tiles - LR_MAT * shaped
    side_m, side_v, side_new = adam_update(side_weight, side_moment, side_second, side_grad, LR_SIDE)
    vec_m, vec_v, vec_new = adam_update(vector_params, vector_moment, vector_second, vector_grad, LR_VEC)
    return (result.astype(jnp.bfloat16), input_grad, tile_grads, left_new, right_new, tiles_new, tiles_new.astype(jnp.bfloat16), side_m, side_v, side_new, vec_m, vec_v, vec_new)
```

```python
import functools

import jax
import jax.numpy as jnp
from jax import lax
from jax.experimental import pallas as pl
from jax.experimental.pallas import tpu as pltpu
from jax.sharding import PartitionSpec as P

D = 2048
HEADS = 64
NS = 128
CONV = 4
TILE = 128
STEP = 10
DI = 4096
SIDE = 320
BLK = 128
LANES = 128
MID_ROWS = 512
TILES_STEP = 6
COPY_ROWS = 16
SLACK = 2
ONE_PASS = True

EPS = 1e-05
HIGH = lax.Precision.HIGHEST
STAT_DECAY = 0.5
LR_MAT = 0.25
LR_SIDE = 0.02
LR_VEC = 0.25
BETA_ONE = 0.9
BETA_TWO = 0.95
ADAM_EPS = 1e-08
DECAY_WD = 0.1
LOG2E = 1.4426950408889634
FAR = -1e30
VMEM_LIMIT = 60 * 1024 * 1024

F32 = jnp.float32
BF16 = jnp.bfloat16

NN = (((1,), (0,)), ((), ()))
NT = (((1,), (1,)), ((), ()))


def segment_bounds(di_local, heads_local, model_local, bc_local, tap_count):
    widths = [
        tap_count * di_local,
        di_local,
        di_local,
        heads_local,
        heads_local,
        heads_local,
        model_local,
        tap_count * bc_local,
        bc_local,
    ]
    bounds = [0]
    for item in widths:
        bounds.append(bounds[-1] + item)
    return bounds


def adam_update(weight, moment, second, gradient, learn_rate):
    moment_new = BETA_ONE * moment + (1.0 - BETA_ONE) * gradient
    second_new = BETA_TWO * second + (1.0 - BETA_TWO) * gradient * gradient
    corrected = moment_new / (1.0 - BETA_ONE**STEP)
    scaled = jnp.sqrt(second_new / (1.0 - BETA_TWO**STEP)) + ADAM_EPS
    return (moment_new, second_new, weight - learn_rate * (corrected / scaled + DECAY_WD * weight))


def contract_rows(left, right):
    return lax.dot_general(left, right, (((0,), (0,)), ((), ())), preferred_element_type=F32)


def contract_cols(left, right):
    return lax.dot_general(left, right, NT, preferred_element_type=F32)


def swap(value, axis, bit):
    size = lax.axis_size(axis)
    return lax.ppermute(value, axis, [(i, i ^ bit) for i in range(size)])


def sum_over(value, axis):
    bit = 1
    while bit < lax.axis_size(axis):
        value = value + swap(value, axis, bit)
        bit *= 2
    return value


class SharedSums:
    def __init__(self, owned, shared):
        self.owned, self.shared = owned, shared
        self.bit = lax.axis_size("dp") // 2

    def exchange(self):
        if self.bit == 0:
            return
        upper = (lax.axis_index("dp") // self.bit) % 2
        pairs = self.owned.reshape(2, -1, self.owned.shape[1])
        sent = lax.dynamic_index_in_dim(pairs, 1 - upper, 0, keepdims=False)
        kept = lax.dynamic_index_in_dim(pairs, upper, 0, keepdims=False)
        arrived = swap(
            jnp.concatenate([sent.reshape(-1), self.shared])[None], "dp", self.bit
        )[0]
        self.owned = kept + arrived[: kept.size].reshape(kept.shape)
        self.shared = self.shared + arrived[kept.size :]
        self.bit //= 2

    def exchange_rest(self):
        while self.bit > 0:
            self.exchange()


class OwnerSum:
    def __init__(self, grads, groups):
        owners = lax.axis_size("dp")
        self.grads = grads.reshape(owners, -1, TILE)
        self.lined = owners == 8
        if not self.lined:
            return
        me = lax.axis_index("dp")
        x, z = me % 2, me // 2
        self.low = z < 2
        order = [jnp.where(self.low, z + 3 - k, z + 1 + k) % 4 for k in range(4)]
        self.own = [self.part(seg, x) for seg in order]
        self.found = [(i, group.index(k)) for k in range(4) for i, group in enumerate(groups) if k in group]
        self.groups = [
            swap(jnp.concatenate([self.part(order[k], 1 - x) for k in group]), "dp", 1)
            for group in groups
        ]

    def part(self, seg, x):
        return lax.dynamic_index_in_dim(self.grads, seg * 2 + x, 0, keepdims=False)

    def pair_sum(self, k):
        rows = self.own[k].shape[0]
        group, place = self.found[k]
        arrived = self.groups[group][place * rows : (place + 1) * rows]
        return self.own[k].astype(F32) + arrived.astype(F32)

    def hop(self, value, moves):
        pairs = [(2 * a + x, 2 * b + x) for a, b in moves for x in (0, 1)]
        return lax.ppermute(value.astype(BF16), "dp", pairs)


    def first(self, other):
        if self.lined:
            self.groups[0], other = tied(self.groups[0], other)
            self.ahead = self.hop(self.pair_sum(0), [(0, 1), (3, 2)])
        return other

    def second(self, other):
        if self.lined:
            needed = self.found[1][0]
            self.ahead, self.groups[needed], other = tied(self.ahead, self.groups[needed], other)
            value = self.pair_sum(1) + self.ahead.astype(F32)
            self.up = self.hop(value, [(0, 1), (1, 2)])
            self.down = self.hop(value, [(3, 2), (2, 1)])
        return other

    def third(self, other):
        if self.lined:
            self.up, self.down, self.groups[-1], other = tied(
                self.up, self.down, self.groups[-1], other
            )
            near, far = self.pair_sum(2), self.pair_sum(0)
            up = jnp.where(self.low, near, far) + self.up.astype(F32)
            down = jnp.where(self.low, far, near) + self.down.astype(F32)
            self.up = self.hop(up, [(0, 1), (1, 2), (2, 3)])
            self.down = self.hop(down, [(3, 2), (2, 1), (1, 0)])
        return other

    def total(self, other):
        if not self.lined:
            flat = self.grads.reshape(-1, TILE)
            return lax.psum_scatter(flat, "dp", scatter_dimension=0, tiled=True).astype(F32), other
        self.up, self.down, other = tied(self.up, self.down, other)
        return self.pair_sum(3) + (self.up.astype(F32) + self.down.astype(F32)), other


def tied(*values):
    return lax.optimization_barrier(values)


def halves(value):
    high = value.astype(BF16)
    return high, (value - high.astype(F32)).astype(BF16)


def dot(left, right, dims=NN):
    return lax.dot_general(left, right, dims, preferred_element_type=F32)


def product(left, right, dims=NN):
    return dot(left.astype(BF16), right.astype(BF16), dims)


def by_halves(left, right):
    both = dot(left.astype(BF16), jnp.concatenate(halves(right), axis=1))
    return both[:, : right.shape[1]] + both[:, right.shape[1] :]


def careful(left, right, dims=NN):
    left_high, left_low = halves(left)
    right_high, right_low = halves(right)
    return dot(
        jnp.concatenate([left_high, left_low, left_high], axis=1),
        jnp.concatenate([right_high, right_high, right_low], axis=dims[0][1][0]),
        dims,
    )


def summed(mask, value):
    high, rest = halves(value)
    low = (value - high.astype(F32) - rest.astype(F32)).astype(BF16)
    mask = mask.astype(BF16)
    return dot(jnp.concatenate([mask] * 3, axis=1), jnp.concatenate([high, rest, low], axis=0))


def sigmoid(value):
    return 0.5 * jnp.tanh(0.5 * value) + 0.5


def softplus(value):
    return jnp.maximum(value, 0.0) + jnp.log1p(jnp.exp(-jnp.abs(value)))


def taps_of(padded, lanes, masks):
    rows = masks[0].shape[0]
    shifted = [padded[8 : 8 + rows, lanes]]
    for shift in range(1, CONV):
        shifted.append(padded[8 - shift : 8 - shift + rows, lanes] * masks[shift - 1])
    return shifted


def convolve(shifted, params, lanes):
    total = params[CONV : CONV + 1, lanes]
    for shift in range(CONV):
        total = total + params[CONV - 1 - shift : CONV - shift, lanes] * shifted[shift]
    return total


def wide(column, shape):
    return jnp.broadcast_to(column, shape)


def ssd_forward_kernel(
    rest_ref, prev_ref, start_ref, par_ref, bcpar_ref, hp_ref,
    ssd_ref, states_ref, xs, ss, state, tails, keeps,
):
    width = ssd_ref.shape[1]
    pairs = width // LANES
    shape = (BLK, LANES)
    base_i = pl.program_id(1) * BLK
    base = base_i.astype(F32)

    @pl.when(pl.program_id(1) == 0)
    def _():
        state[...] = jnp.zeros_like(state)

    xs[0:8, :] = prev_ref[:, 0:width]
    xs[8 : 8 + BLK, :] = rest_ref[:, 0:width]
    ss[0:8, :] = prev_ref[:, width : width + 2 * NS]
    ss[8 : 8 + BLK, :] = rest_ref[:, width : width + 2 * NS]
    start = start_ref[...]
    row = (lax.broadcasted_iota(jnp.int32, shape, 0) + base_i).astype(F32)
    col = (lax.broadcasted_iota(jnp.int32, shape, 1) + base_i).astype(F32)
    lane = lax.broadcasted_iota(jnp.int32, shape, 1)
    low = lane < LANES // 2
    pos = row - start
    masks = [jnp.where(pos >= float(k), 1.0, 0.0) for k in range(1, CONV)]
    bias = jnp.where((col >= start) & (col <= row), 0.0, FAR)
    carried = start < base
    last_start = start_ref[BLK - 1 : BLK, :]
    tail_ok = row >= last_start
    keep_ok = last_start < base

    acts = []
    for part in range(2):
        lanes = slice(part * NS, (part + 1) * NS)
        raw = convolve(taps_of(ss, lanes, masks), bcpar_ref, lanes)
        acts.append(raw * sigmoid(raw))
    b_act, c_act = acts
    first_step = width + 2 * NS
    steps = softplus(rest_ref[:, first_step : first_step + LANES] + hp_ref[0:1, :])
    lower = jnp.where(col <= row, 1.0, 0.0)
    cum = summed(lower, steps * hp_ref[1:2, :])
    cum_t = cum.T
    scores = careful(c_act, b_act, NT)
    states_ref[0] = state[...]
    from_state = product(c_act, state[...])
    for pair in range(pairs):
        lanes = slice(pair * LANES, (pair + 1) * LANES)
        raw = convolve(taps_of(xs, lanes, masks), par_ref, lanes)
        act = raw * sigmoid(raw)
        col_a = wide(cum[:, 2 * pair : 2 * pair + 1], shape)
        col_b = wide(cum[:, 2 * pair + 1 : 2 * pair + 2], shape)
        both = jnp.where(low, col_a, col_b)
        step_both = jnp.where(
            low,
            wide(steps[:, 2 * pair : 2 * pair + 1], shape),
            wide(steps[:, 2 * pair + 1 : 2 * pair + 2], shape),
        )
        scaled = act * step_both
        weight_a = scores * jnp.exp2(col_a - cum_t[2 * pair : 2 * pair + 1, :] + bias)
        weight_b = scores * jnp.exp2(col_b - cum_t[2 * pair + 1 : 2 * pair + 2, :] + bias)
        inner = by_halves(
            jnp.concatenate([weight_a, weight_b], axis=1),
            jnp.concatenate([jnp.where(low, scaled, 0.0), jnp.where(low, 0.0, scaled)], axis=0),
        )
        carry = jnp.where(carried, jnp.exp2(both), 0.0)
        ssd_ref[:, lanes] = inner + carry * from_state[:, lanes] + par_ref[5:6, lanes] * act
        last = both[BLK - 1 : BLK, :]
        tails[:, lanes] = scaled * jnp.where(tail_ok, jnp.exp2(last - both), 0.0)
        keeps[0:1, lanes] = jnp.where(keep_ok, jnp.exp2(last), 0.0)
    state[...] = keeps[0:1, :] * state[...] + product(b_act.T, tails[...])


def ssd_backward_kernel(
    *refs,
):
    held = max(len(refs) - 27, 0)
    ssd_backward_body(*refs[held:])


def ssd_backward_body(
    place_ref, rest_ref, prev_ref, dy_ref, states_ref, start_ref, end_ref, srow_ref,
    par_ref, bcpar_ref, hp_ref, pick_ref,
    drest_ref, dside_ref, gx_ref, gbc_ref, gh_ref,
    xs, ss, dxs, dbs, dstate, tails, carries, terms, rows_in, keeps,
):
    width = dy_ref.shape[1]
    pairs = width // LANES
    shape = (BLK, LANES)
    blocks = pl.num_programs(0)
    base_i = (blocks - 1 - pl.program_id(0)) * BLK
    base = base_i.astype(F32)

    @pl.when(pl.program_id(0) == 0)
    def _():
        gx_ref[...] = jnp.zeros_like(gx_ref)
        gbc_ref[...] = jnp.zeros_like(gbc_ref)
        gh_ref[...] = jnp.zeros_like(gh_ref)
        rows_in[...] = jnp.zeros_like(rows_in)
        dxs[0:8, :] = jnp.zeros((8, width), F32)
        dbs[0:8, :] = jnp.zeros((8, 2 * NS), F32)
        dstate[...] = jnp.zeros_like(dstate)

    dxs[BLK : BLK + 8, :] = dxs[0:8, :]
    dbs[BLK : BLK + 8, :] = dbs[0:8, :]
    xs[0:8, :] = prev_ref[:, 0:width]
    xs[8 : 8 + BLK, :] = rest_ref[:, 0:width]
    ss[0:8, :] = prev_ref[:, width : width + 2 * NS]
    ss[8 : 8 + BLK, :] = rest_ref[:, width : width + 2 * NS]
    start = start_ref[...]
    row_i = lax.broadcasted_iota(jnp.int32, shape, 0)
    lane = lax.broadcasted_iota(jnp.int32, shape, 1)
    row = (row_i + base_i).astype(F32)
    col = (lane + base_i).astype(F32)
    low = lane < LANES // 2
    pos = row - start
    left = end_ref[...] - row
    masks = [jnp.where(pos >= float(k), 1.0, 0.0) for k in range(1, CONV)]
    after = [jnp.where(left > float(k), 1.0, 0.0) for k in range(1, CONV)]
    bias_t = jnp.where((row >= srow_ref[...]) & (row <= col), 0.0, FAR)
    carried = start < base
    last_start = start_ref[BLK - 1 : BLK, :]
    tail_ok = row >= last_start
    keep_ok = last_start < base

    acts, slopes, bc_taps = [], [], []
    for part in range(2):
        lanes = slice(part * NS, (part + 1) * NS)
        shifted = taps_of(ss, lanes, masks)
        raw = convolve(shifted, bcpar_ref, lanes)
        sig = sigmoid(raw)
        acts.append(raw * sig)
        slopes.append(sig * (1.0 + raw * (1.0 - sig)))
        bc_taps.append(shifted)
    b_act, c_act = acts
    first_step = width + 2 * NS
    raw_steps = rest_ref[:, first_step : first_step + LANES] + hp_ref[0:1, :]
    steps = softplus(raw_steps)
    lower = jnp.where(col <= row, 1.0, 0.0)
    upper = jnp.where(col >= row, 1.0, 0.0)
    cum = summed(lower, steps * hp_ref[1:2, :])
    cum_t = cum.T
    scores_t = careful(b_act, c_act, NT)
    old = states_ref[0]
    from_state = product(c_act, old)
    from_next = product(b_act, dstate[...])
    d_scores = jnp.zeros(shape, F32)
    direct = jnp.zeros(shape, F32)

    def add_rows(ref, first, lanes, value):
        ref[first : first + 8, lanes] += jnp.sum(value.reshape(BLK // 8, 8, value.shape[1]), axis=0)

    for pair in range(pairs):
        lanes = slice(pair * LANES, (pair + 1) * LANES)
        shifted = taps_of(xs, lanes, masks)
        raw = convolve(shifted, par_ref, lanes)
        sig = sigmoid(raw)
        act = raw * sig
        dy = dy_ref[:, lanes]
        cols = [wide(cum[:, h : h + 1], shape) for h in (2 * pair, 2 * pair + 1)]
        step_cols = [wide(steps[:, h : h + 1], shape) for h in (2 * pair, 2 * pair + 1)]
        both = jnp.where(low, cols[0], cols[1])
        step_both = jnp.where(low, step_cols[0], step_cols[1])
        parts = [jnp.where(low, act, 0.0), jnp.where(low, 0.0, act)]
        dy_high, dy_low = halves(dy)
        dy_wide = jnp.concatenate([dy_high, dy_high, dy_low], axis=1)
        high, rest = halves(jnp.concatenate(parts, axis=0))
        inners = dot(jnp.concatenate([high, rest, high], axis=1), dy_wide, NT)
        weights = []
        for which in range(2):
            head = 2 * pair + which
            decay = jnp.exp2(cum_t[head : head + 1, :] - cols[which] + bias_t)
            inner = inners[which * BLK : (which + 1) * BLK, :]
            weight = decay * scores_t
            weights.append(weight)
            d_scores = d_scores + decay * inner * step_cols[which]
            pulled = weight * inner
            direct = jnp.where(lane == head, jnp.sum(pulled, axis=1, keepdims=True), direct)
            rows_in[head : head + 1, :] = jnp.sum(pulled * step_cols[which], axis=0, keepdims=True)
        d_intra = by_halves(
            jnp.concatenate(weights, axis=1),
            jnp.concatenate([jnp.where(low, dy, 0.0), jnp.where(low, 0.0, dy)], axis=0),
        )
        last = both[BLK - 1 : BLK, :]
        tail = jnp.where(tail_ok, jnp.exp2(last - both), 0.0)
        d_tail = tail * from_next[:, lanes]
        terms[0:BLK, lanes] = act * d_tail
        tails[:, lanes] = act * step_both * tail
        carry = dy * jnp.where(carried, jnp.exp2(both), 0.0)
        carries[:, lanes] = carry
        terms[BLK : 2 * BLK, lanes] = carry * from_state[:, lanes]
        keeps[0:1, lanes] = jnp.where(keep_ok, jnp.exp2(last), 0.0)
        d_act = step_both * (d_intra + d_tail) + par_ref[5:6, lanes] * dy
        d_conv = d_act * (sig * (1.0 + raw * (1.0 - sig)))
        dxs[0:BLK, lanes] = d_conv
        for shift in range(CONV):
            add_rows(gx_ref, 8 * (CONV - 1 - shift), lanes, d_conv * shifted[shift])
        add_rows(gx_ref, 8 * CONV, lanes, d_conv)
        add_rows(gx_ref, 8 * (CONV + 1), lanes, dy * act)
        d_in = par_ref[CONV - 1 : CONV, lanes] * d_conv
        for shift in range(1, CONV):
            d_in = d_in + par_ref[CONV - 1 - shift : CONV - shift, lanes] * (
                after[shift - 1] * dxs[shift : shift + BLK, lanes]
            )
        drest_ref[:, lanes] = d_in.astype(BF16)

    stay = keeps[0:1, :] * jnp.sum((old * dstate[...]).reshape(NS // 8, 8, width), axis=0)
    terms[2 * BLK : 2 * BLK + 8, :] = stay
    by_head = dot(terms[...].astype(BF16), pick_ref[...])
    at_heads = by_head[0:BLK, :]
    stay_heads = jnp.sum(by_head[2 * BLK : 2 * BLK + 8, :], axis=0, keepdims=True)
    direct = direct + at_heads
    d_cum = rows_in[...].T + by_head[BLK : 2 * BLK, :] - steps * direct
    at_last = jnp.sum(steps * at_heads, axis=0, keepdims=True) + stay_heads
    through = summed(upper, d_cum) + at_last
    decay_rate = hp_ref[2:3, :]
    d_steps = direct + decay_rate * through
    d_raw = d_steps * sigmoid(raw_steps)
    every = slice(0, LANES)
    add_rows(gh_ref, 0, every, decay_rate * steps * through)
    add_rows(gh_ref, 8, every, d_raw)
    dside_ref[:, 2 * NS :] = pltpu.roll(d_raw, place_ref[0], 1)
    drest_ref[:, first_step : first_step + LANES] = d_raw.astype(BF16)
    drest_ref[:, first_step + LANES :] = jnp.zeros(
        (BLK, drest_ref.shape[1] - first_step - LANES), BF16
    )
    d_b = careful(d_scores, c_act) + product(tails[...], dstate[...], NT)
    d_c = careful(d_scores.T, b_act) + product(carries[...], old, NT)
    for part, value in ((0, d_b), (1, d_c)):
        lanes = slice(part * NS, (part + 1) * NS)
        d_conv = value * slopes[part]
        dbs[0:BLK, lanes] = d_conv
        for shift in range(CONV):
            add_rows(gbc_ref, 8 * (CONV - 1 - shift), lanes, d_conv * bc_taps[part][shift])
        add_rows(gbc_ref, 8 * CONV, lanes, d_conv)
        d_in = bcpar_ref[CONV - 1 : CONV, lanes] * d_conv
        for shift in range(1, CONV):
            d_in = d_in + bcpar_ref[CONV - 1 - shift : CONV - shift, lanes] * (
                after[shift - 1] * dbs[shift : shift + BLK, lanes]
            )
        dside_ref[:, lanes] = d_in
        drest_ref[:, width + part * NS : width + (part + 1) * NS] = d_in.astype(BF16)
    dstate[...] = keeps[0:1, :] * dstate[...] + product(c_act.T, carries[...])


def ssd_forward(rest, starts, par, bcpar, hp, sequences):
    rows, width = rest.shape[0], par.shape[1]
    blocks = rows // sequences // BLK
    here = lambda s, b: (s * blocks + b, 0)
    before = lambda s, b: (jnp.maximum((s * blocks + b) * (BLK // 8) - 1, 0), 0)
    fixed = lambda s, b: (0, 0)
    return pl.pallas_call(
        ssd_forward_kernel,
        grid=(sequences, blocks),
        in_specs=[
            pl.BlockSpec((BLK, rest.shape[1]), here),
            pl.BlockSpec((8, rest.shape[1]), before),
            pl.BlockSpec((BLK, LANES), here),
            pl.BlockSpec(par.shape, fixed),
            pl.BlockSpec(bcpar.shape, fixed),
            pl.BlockSpec(hp.shape, fixed),
        ],
        out_specs=[
            pl.BlockSpec((BLK, width), here),
            pl.BlockSpec((1, NS, width), lambda s, b: (s * blocks + b, 0, 0)),
        ],
        out_shape=[
            jax.ShapeDtypeStruct((rows, width), F32),
            jax.ShapeDtypeStruct((sequences * blocks, NS, width), F32),
        ],
        scratch_shapes=[
            pltpu.VMEM((BLK + 8, width), F32),
            pltpu.VMEM((BLK + 8, 2 * NS), F32),
            pltpu.VMEM((NS, width), F32),
            pltpu.VMEM((BLK, width), F32),
            pltpu.VMEM((8, width), F32),
        ],
        compiler_params=pltpu.CompilerParams(vmem_limit_bytes=VMEM_LIMIT),
        cost_estimate=pl.CostEstimate(
            flops=40 * rows * BLK * width, bytes_accessed=20 * rows * width, transcendentals=0
        ),
        name="ssd_forward",
    )(rest, rest, starts, par, bcpar, hp)


def ssd_backward(
    sequence, before_it, place, rest, d_ssd, states, starts, ends, start_row, par, bcpar, hp, pick, sequences
):
    rows, width = d_ssd.shape
    rest_width = rest.shape[1]
    blocks = rows // sequences // BLK
    at = lambda b: sequence * blocks + blocks - 1 - b
    here = lambda b: (at(b), 0)
    before = lambda b: (jnp.maximum(at(b) * (BLK // 8) - 1, 0), 0)
    fixed = lambda b: (0, 0)
    return pl.pallas_call(
        ssd_backward_kernel,
        grid=(blocks,),
        in_specs=[pl.BlockSpec(memory_space=pl.ANY)] * len(before_it)
        + [
            pl.BlockSpec(memory_space=pltpu.SMEM),
            pl.BlockSpec((BLK, rest_width), here),
            pl.BlockSpec((8, rest_width), before),
            pl.BlockSpec((BLK, width), here),
            pl.BlockSpec((1, NS, width), lambda b: (at(b), 0, 0)),
            pl.BlockSpec((BLK, LANES), here),
            pl.BlockSpec((BLK, LANES), here),
            pl.BlockSpec((1, BLK), lambda b: (0, at(b))),
            pl.BlockSpec(par.shape, fixed),
            pl.BlockSpec(bcpar.shape, fixed),
            pl.BlockSpec(hp.shape, fixed),
            pl.BlockSpec(pick.shape, fixed),
        ],
        out_specs=[
            pl.BlockSpec((BLK, rest_width), here),
            pl.BlockSpec((BLK, 2 * NS + LANES), lambda b: (blocks - 1 - b, 0)),
            pl.BlockSpec((8 * (CONV + 2), width), fixed),
            pl.BlockSpec((8 * (CONV + 1), 2 * NS), fixed),
            pl.BlockSpec((16, LANES), fixed),
        ],
        out_shape=[
            jax.ShapeDtypeStruct((rows, rest_width), BF16),
            jax.ShapeDtypeStruct((rows // sequences, 2 * NS + LANES), F32),
            jax.ShapeDtypeStruct((8 * (CONV + 2), width), F32),
            jax.ShapeDtypeStruct((8 * (CONV + 1), 2 * NS), F32),
            jax.ShapeDtypeStruct((16, LANES), F32),
        ],
        scratch_shapes=[
            pltpu.VMEM((BLK + 8, width), F32),
            pltpu.VMEM((BLK + 8, 2 * NS), F32),
            pltpu.VMEM((BLK + 8, width), F32),
            pltpu.VMEM((BLK + 8, 2 * NS), F32),
            pltpu.VMEM((NS, width), F32),
            pltpu.VMEM((BLK, width), F32),
            pltpu.VMEM((BLK, width), F32),
            pltpu.VMEM((2 * BLK + 8, width), F32),
            pltpu.VMEM((LANES, BLK), F32),
            pltpu.VMEM((8, width), F32),
        ],
        input_output_aliases={i: i for i in range(len(before_it))},
        compiler_params=pltpu.CompilerParams(vmem_limit_bytes=VMEM_LIMIT),
        cost_estimate=pl.CostEstimate(
            flops=100 * rows * BLK * width // sequences,
            bytes_accessed=4 * rows * 5 * width // sequences,
            transcendentals=0,
        ),
        name="ssd_backward",
    )(*before_it, place, rest, rest, d_ssd, states, starts, ends, start_row, par, bcpar, hp, pick)


def resident(array):
    return pl.BlockSpec(
        array.shape, lambda *i: (0,) * array.ndim, pipeline_mode=pl.Buffered(buffer_count=1)
    )


def matmul_kernel(left_ref, right_ref, out_ref):
    out_ref[...] = dot(left_ref[...], right_ref[...])


def project(normed, weights):
    rows = normed.shape[0]
    step = min(MID_ROWS, rows)
    width = weights.shape[1]
    here = lambda i: (i, 0)
    return pl.pallas_call(
        matmul_kernel,
        grid=(rows // step,),
        in_specs=[pl.BlockSpec((step, D), here), resident(weights)],
        out_specs=pl.BlockSpec((step, width), here),
        out_shape=jax.ShapeDtypeStruct((rows, width), F32),
        compiler_params=pltpu.CompilerParams(vmem_limit_bytes=VMEM_LIMIT),
        cost_estimate=pl.CostEstimate(
            flops=2 * rows * D * width,
            bytes_accessed=4 * rows * width + 2 * D * (rows + width),
            transcendentals=0,
        ),
        name="project",
    )(normed, weights)


def gate_kernel(normed_ref, cot_ref, wgate_ref, wout_ref, ssd_ref, gain_ref, gate_ref, dh_ref, sums_ref):
    gate_ref[...] = dot(normed_ref[...], wgate_ref[...])
    dh_ref[...] = dot(cot_ref[...], wout_ref[...], NT)
    rows, width = ssd_ref.shape
    for first in range(0, rows, LANES):
        at = slice(first, first + LANES)
        squares = jnp.zeros((LANES, LANES), F32)
        inners = jnp.zeros((LANES, LANES), F32)
        for piece in range(width // LANES):
            lanes = slice(piece * LANES, (piece + 1) * LANES)
            gate = gate_ref[at, lanes]
            gated = ssd_ref[at, lanes] * (gate * sigmoid(gate))
            squares = squares + gated * gated
            inners = inners + dh_ref[at, lanes] * gain_ref[0:1, lanes] * gated
        sums_ref[0:1, at] = jnp.sum(squares.T, axis=0, keepdims=True)
        sums_ref[1:2, at] = jnp.sum(inners.T, axis=0, keepdims=True)
    sums_ref[2:8, :] = jnp.zeros((6, rows), F32)


def gate_project(normed, cotangent, w_gate, w_output, ssd, gain):
    rows, width = ssd.shape
    step = min(MID_ROWS, rows)
    here = lambda i: (i, 0)
    return pl.pallas_call(
        gate_kernel,
        grid=(rows // step,),
        in_specs=[
            pl.BlockSpec((step, D), here),
            pl.BlockSpec((step, D), here),
            resident(w_gate),
            resident(w_output),
            pl.BlockSpec((step, width), here),
            pl.BlockSpec((1, width), lambda i: (0, 0)),
        ],
        out_specs=[
            pl.BlockSpec((step, width), here),
            pl.BlockSpec((step, width), here),
            pl.BlockSpec((8, step), lambda i: (0, i)),
        ],
        out_shape=[
            jax.ShapeDtypeStruct((rows, width), F32),
            jax.ShapeDtypeStruct((rows, width), F32),
            jax.ShapeDtypeStruct((8, rows), F32),
        ],
        compiler_params=pltpu.CompilerParams(vmem_limit_bytes=VMEM_LIMIT),
        cost_estimate=pl.CostEstimate(
            flops=4 * rows * D * width, bytes_accessed=16 * rows * width, transcendentals=0
        ),
        name="gate_project",
    )(normed, cotangent, w_gate, w_output, ssd, gain)


def gated_kernel(
    core_ref, ssd_ref, gate_ref, dh_ref, sums_ref, gain_ref, wout_ref,
    hidden_ref, dgate_ref, dssd_ref, gain_out, sent_ref, kept_ref,
):
    @pl.when(pl.program_id(0) == 0)
    def _():
        gain_out[...] = jnp.zeros_like(gain_out)

    width = ssd_ref.shape[1]
    rows = ssd_ref.shape[0]
    scale = lax.rsqrt(sums_ref[0:1, :] / DI + EPS)
    shift = scale * scale * scale * (sums_ref[1:2, :] / DI)
    turned = jnp.concatenate([scale] * 8 + [shift] * 8 + [jnp.zeros((LANES - 16, rows), F32)], axis=0).T
    chunk = min(64, rows)
    for first in range(0, rows, chunk):
        at = slice(first, first + chunk)
        scales = wide(turned[at, 0:1], (chunk, LANES))
        shifts = wide(turned[at, 8:9], (chunk, LANES))
        for piece in range(width // LANES):
            lanes = slice(piece * LANES, (piece + 1) * LANES)
            gate = gate_ref[at, lanes]
            ssd = ssd_ref[at, lanes]
            d_hidden = dh_ref[at, lanes]
            gain = gain_ref[0:1, lanes]
            sig = sigmoid(gate)
            act = gate * sig
            gated = ssd * act
            unit = gated * scales
            hidden_ref[at, lanes] = (unit * gain).astype(BF16)
            gain_out[:, lanes] += jnp.sum((d_hidden * unit).reshape(chunk // 8, 8, LANES), axis=0)
            d_gated = scales * (d_hidden * gain) - gated * shifts
            dssd_ref[at, lanes] = d_gated * act
            dgate_ref[at, lanes] = (
                d_gated * ssd * (sig * (1.0 + gate * (1.0 - sig)))
            ).astype(BF16)
    mixed = dot(hidden_ref[...], wout_ref[...]).astype(BF16)
    steps = pl.num_programs(0) // 2

    @pl.when(pl.program_id(0) < steps)
    def _():
        sent_ref[...] = mixed

    @pl.when(pl.program_id(0) >= steps)
    def _():
        kept_ref[...] = mixed


def gated_pass(core, ssd, gate, d_hidden, sums, gain, w_output):
    rows, width = ssd.shape
    step = min(MID_ROWS, rows // 2)
    steps = rows // step // 2

    def at(i, core):
        half = jnp.where(i < steps, 1 - core[0], core[0])
        return half * steps + i % steps

    here = lambda i, core: (at(i, core), 0)
    fixed = lambda i, core: (0, 0)
    return pl.pallas_call(
        gated_kernel,
        grid_spec=pltpu.PrefetchScalarGridSpec(
            num_scalar_prefetch=1,
            grid=(2 * steps,),
            in_specs=[
                pl.BlockSpec((step, width), here),
                pl.BlockSpec((step, width), here),
                pl.BlockSpec((step, width), here),
                pl.BlockSpec((8, step), lambda i, core: (0, at(i, core))),
                pl.BlockSpec((1, width), fixed),
                resident(w_output),
            ],
            out_specs=[
                pl.BlockSpec((step, width), here),
                pl.BlockSpec((step, width), here),
                pl.BlockSpec((step, width), here),
                pl.BlockSpec((8, width), fixed),
                pl.BlockSpec((step, D), lambda i, core: (jnp.minimum(i, steps - 1), 0)),
                pl.BlockSpec((step, D), lambda i, core: (jnp.maximum(i - steps, 0), 0)),
            ],
        ),
        out_shape=[
            jax.ShapeDtypeStruct((rows, width), BF16),
            jax.ShapeDtypeStruct((rows, width), BF16),
            jax.ShapeDtypeStruct((rows, width), F32),
            jax.ShapeDtypeStruct((8, width), F32),
            jax.ShapeDtypeStruct((rows // 2, D), BF16),
            jax.ShapeDtypeStruct((rows // 2, D), BF16),
        ],
        compiler_params=pltpu.CompilerParams(vmem_limit_bytes=VMEM_LIMIT),
        cost_estimate=pl.CostEstimate(
            flops=2 * rows * width * D, bytes_accessed=20 * rows * width, transcendentals=0
        ),
        name="gated_pass",
    )(core, ssd, gate, d_hidden, sums, gain, w_output)


def unit_rows(tokens_ref):
    rows = tokens_ref[...].astype(F32)
    inverse = lax.rsqrt(jnp.mean(rows * rows, axis=1, keepdims=True) + EPS)
    return rows, inverse


def normed_grad_kernel(half_ref, dgate_ref, drest_ref, tokens_ref, wgate_ref, wrest_ref, out_ref, gain_out):
    @pl.when(pl.program_id(0) == 0)
    def _():
        gain_out[...] = jnp.zeros_like(gain_out)

    total = dot(dgate_ref[...], wgate_ref[...], NT) + dot(drest_ref[...], wrest_ref[...], NT)
    out_ref[...] = total.astype(BF16)
    rows, inverse = unit_rows(tokens_ref)
    weighted = total * (rows * inverse)
    gain_out[...] += jnp.sum(weighted.reshape(-1, 8, D), axis=0)


def normed_grad(half, weight, d_gate, d_rest, tokens, w_gate, w_rest):
    rows = tokens.shape[0]
    step = min(MID_ROWS, rows // 2)
    steps = rows // step // 2
    here = lambda i, half: (half[0] * steps + i, 0)
    return pl.pallas_call(
        normed_grad_kernel,
        grid_spec=pltpu.PrefetchScalarGridSpec(
            num_scalar_prefetch=1,
            grid=(steps,),
            in_specs=[
                pl.BlockSpec((step, d_gate.shape[1]), here),
                pl.BlockSpec((step, d_rest.shape[1]), here),
                pl.BlockSpec((step, D), here),
                resident(w_gate),
                resident(w_rest),
            ],
            out_specs=[
                pl.BlockSpec((step, D), lambda i, half: (i, 0)),
                pl.BlockSpec((8, D), lambda i, half: (0, 0)),
            ],
        ),
        out_shape=[
            jax.ShapeDtypeStruct((rows // 2, D), BF16),
            jax.ShapeDtypeStruct((8, D), F32),
        ],
        compiler_params=pltpu.CompilerParams(vmem_limit_bytes=VMEM_LIMIT),
        cost_estimate=pl.CostEstimate(
            flops=weight * rows * D * (d_gate.shape[1] + d_rest.shape[1]),
            bytes_accessed=weight * 6 * rows * D,
            transcendentals=0,
        ),
        name="normed_grad",
    )(half, d_gate, d_rest, tokens, w_gate, w_rest)


def input_grad_kernel(core_ref, own_ref, other_ref, tokens_ref, cot_ref, gain_ref, out_ref, terms):
    steps = pl.num_programs(0) // 2
    mine = pl.program_id(0) // steps == core_ref[0]

    @pl.when(mine)
    def _():
        terms[...] = own_ref[...].astype(F32)

    @pl.when(jnp.logical_not(mine))
    def _():
        terms[...] = other_ref[...].astype(F32)

    rows, inverse = unit_rows(tokens_ref)
    weighted = terms[...] * gain_ref[0:1, :]
    inner = jnp.mean(weighted * rows, axis=1, keepdims=True)
    out_ref[...] = (
        cot_ref[...].astype(F32) + inverse * weighted - rows * (inverse * inverse * inverse * inner)
    )


def input_grads(core, own, other, tokens, cotangent, gain):
    rows = tokens.shape[0]
    step = min(MID_ROWS, rows // 2)
    steps = rows // step // 2
    here = lambda i, core: (i, 0)

    def part_at(is_own):
        def index(i, core):
            wanted = (i // steps == core[0]) == is_own
            parked = jnp.where((core[0] == 0) == is_own, steps - 1, 0)
            return (jnp.where(wanted, i % steps, parked), 0)

        return index

    return pl.pallas_call(
        input_grad_kernel,
        grid_spec=pltpu.PrefetchScalarGridSpec(
            num_scalar_prefetch=1,
            grid=(2 * steps,),
            in_specs=[
                pl.BlockSpec((step, D), part_at(True)),
                pl.BlockSpec((step, D), part_at(False)),
                pl.BlockSpec((step, D), here),
                pl.BlockSpec((step, D), here),
                pl.BlockSpec((1, D), lambda i, core: (0, 0)),
            ],
            out_specs=pl.BlockSpec((step, D), here),
            scratch_shapes=[pltpu.VMEM((step, D), F32)],
        ),
        out_shape=jax.ShapeDtypeStruct((rows, D), F32),
        compiler_params=pltpu.CompilerParams(vmem_limit_bytes=VMEM_LIMIT),
        cost_estimate=pl.CostEstimate(
            flops=0, bytes_accessed=10 * rows * D, transcendentals=0
        ),
        name="input_grads",
    )(core, own, other, tokens, cotangent, gain)


def held_rows(first):
    return (pl.ds(pl.multiple_of(first, COPY_ROWS), TILE), slice(None))


def band_tiles(ref):
    columns = ref.shape[1] // TILE
    for tile in range(columns * (ref.shape[0] // TILE)):
        down, across = tile // columns, tile % columns
        yield tile, (
            slice(down * TILE, (down + 1) * TILE),
            slice(across * TILE, (across + 1) * TILE),
        )


def copied(first, helds, ref, at):
    past = 0
    for held_ref in helds:
        size = held_ref.shape[0]
        if len(helds) == 1:
            ref[at] = held_ref[held_rows(first)]
        else:

            @pl.when((first >= past) & (first < past + size))
            def _(held_ref=held_ref, past=past):
                ref[at] = held_ref[held_rows(first - past)]

        past += size


def assemble_kernel(parts, width, rows_ref, *refs):
    helds = refs[:parts]
    band = pl.program_id(0)
    outs = refs[parts:]
    if width:
        outs[1][:, width:] = outs[0][...]
        outs = (outs[1].at[:, 0:width],)
    base = 0
    for ref in outs:
        count = (ref.shape[0] // TILE) * (ref.shape[1] // TILE)
        for tile, at in band_tiles(ref):
            copied(rows_ref[base + band * count + tile], helds, ref, at)
        base += count * pl.num_programs(0)


def assemble(rows, helds, side_cols, shapes):
    bands = min(shape[0] for shape in shapes) // TILE
    bands = min(bands, 8)
    here = lambda i: (i, 0)
    width = shapes[0][1] - side_cols[0].shape[1] if side_cols else 0
    return pl.pallas_call(
        functools.partial(assemble_kernel, len(helds), width),
        grid=(bands,),
        in_specs=[pl.BlockSpec(memory_space=pltpu.SMEM)]
        + [resident(held) for held in helds]
        + [pl.BlockSpec((side.shape[0] // bands, side.shape[1]), here) for side in side_cols],
        out_specs=[pl.BlockSpec((shape[0] // bands, shape[1]), here) for shape in shapes],
        out_shape=[jax.ShapeDtypeStruct(shape, BF16) for shape in shapes],
        compiler_params=pltpu.CompilerParams(vmem_limit_bytes=VMEM_LIMIT),
        cost_estimate=pl.CostEstimate(
            flops=0, bytes_accessed=4 * sum(held.size for held in helds), transcendentals=0
        ),
        name="assemble",
    )(rows, *helds, *side_cols)


def spread_kernel(rows_ref, *refs):
    out_ref = refs[-1]
    band = pl.program_id(0)
    base = 0
    for ref in refs[:-1]:
        count = (ref.shape[0] // TILE) * (ref.shape[1] // TILE)
        for tile, place in band_tiles(ref):
            first = rows_ref[base + band * count + tile]

            @pl.when(first >= 0)
            def _(first=first, place=place, ref=ref):
                out_ref[held_rows(first)] = ref[place]

        base += count * pl.num_programs(0)


def spread(grad_rows, grads, total_rows):
    bands = min(grad.shape[0] for grad in grads) // TILE
    return pl.pallas_call(
        spread_kernel,
        grid=(bands,),
        in_specs=[pl.BlockSpec(memory_space=pltpu.SMEM)]
        + [pl.BlockSpec((grad.shape[0] // bands, grad.shape[1]), lambda i: (i, 0)) for grad in grads],
        out_specs=pl.BlockSpec((total_rows, TILE), lambda i: (0, 0)),
        out_shape=jax.ShapeDtypeStruct((total_rows, TILE), BF16),
        compiler_params=pltpu.CompilerParams(vmem_limit_bytes=VMEM_LIMIT),
        cost_estimate=pl.CostEstimate(
            flops=0,
            bytes_accessed=2 * total_rows * TILE + sum(2 * grad.size for grad in grads),
            transcendentals=0,
        ),
        name="spread",
    )(grad_rows, *grads)


def update_kernel(
    rows_ref, early_ref, late_ref, repair_ref, tiles_ref, lstat_ref, rstat_ref, lroot_ref, rroot_ref,
    grads_out, left_out, right_out, tiles_out, copy_out, grad_tile,
):
    dot = functools.partial(lax.dot_general, dimension_numbers=NN, preferred_element_type=F32)
    step = tiles_ref.shape[0]
    for tile in range(step):
        first = rows_ref[pl.program_id(0) * step + tile]
        past = 0
        for source in (early_ref, late_ref, repair_ref):
            size = source.shape[0]

            @pl.when((first >= past) & (first < past + size))
            def _(source=source, past=past, tile=tile):
                grad_tile[tile] = source[held_rows(first - past)]

            past += size
    for tile in range(step):
        exact_grad = grad_tile[tile]
        grad = exact_grad.astype(BF16)
        turned = exact_grad.T.astype(BF16)
        grads_out[tile] = exact_grad
        left_out[tile] = STAT_DECAY * lstat_ref[tile] + (1.0 - STAT_DECAY) * dot(grad, turned)
        right_out[tile] = STAT_DECAY * rstat_ref[tile] + (1.0 - STAT_DECAY) * dot(turned, grad)
        shaped = careful(careful(lroot_ref[tile], exact_grad), rroot_ref[tile])
        updated = tiles_ref[tile] - LR_MAT * shaped
        tiles_out[tile] = updated
        copy_out[tile] = updated.astype(BF16)


def update_tiles(rows, early, late, repair, tiles, left_stats, right_stats, left_roots, right_roots):
    count = tiles.shape[0]
    step = TILES_STEP if count % TILES_STEP == 0 else 1
    spec = pl.BlockSpec((step, TILE, TILE), lambda i, rows: (i, 0, 0))
    sources = [pl.BlockSpec(part.shape, lambda i, rows: (0, 0)) for part in (early, late, repair)]
    whole = jax.ShapeDtypeStruct(tiles.shape, F32)
    return pl.pallas_call(
        update_kernel,
        grid_spec=pltpu.PrefetchScalarGridSpec(
            num_scalar_prefetch=1,
            grid=(count // step,),
            in_specs=sources + [spec] * 5,
            out_specs=[spec] * 5,
            scratch_shapes=[pltpu.VMEM((step, TILE, TILE), F32)],
        ),
        out_shape=[whole] * 4 + [jax.ShapeDtypeStruct(tiles.shape, BF16)],
        compiler_params=pltpu.CompilerParams(vmem_limit_bytes=VMEM_LIMIT),
        cost_estimate=pl.CostEstimate(
            flops=18 * count * TILE**3, bytes_accessed=42 * count * TILE**2, transcendentals=0
        ),
        name="update_tiles",
    )(rows, early, late, repair, tiles, left_stats, right_stats, left_roots, right_roots)


def fetch_plan(slot_map, own_tiles, side_rows):
    count = slot_map.shape[0]
    tiles = jnp.arange(count, dtype=jnp.int32)
    waits = tiles // (count // 3) != 1
    key = tiles + waits * count
    owner = slot_map // own_tiles
    together = owner[:, None] == owner[None, :]
    place = jnp.sum(together & (key[None, :] < key[:, None]), axis=1, dtype=jnp.int32)
    first = max(1, own_tiles * 13 // 24)
    first_rows, second_rows = first * TILE + side_rows, (own_tiles - first) * TILE
    early = place < first
    owners = count // own_tiles
    rows = jnp.where(
        early,
        owner * first_rows + place * TILE,
        owners * first_rows + owner * second_rows + (place - first) * TILE,
    )
    rank = lax.axis_index("dp")
    places = jnp.arange(own_tiles, dtype=jnp.int32)
    order = jnp.sum(
        jnp.where(
            (owner == rank)[None, :] & (place[None, :] == places[:, None]),
            slot_map[None, :] - rank * own_tiles,
            0,
        ),
        axis=1,
        dtype=jnp.int32,
    )
    return rows, order, first, jnp.any(~waits & ~early)


def tile_plan(slot_map, own_tiles):
    count = slot_map.shape[0]
    tiles = jnp.arange(count, dtype=jnp.int32)
    kind = tiles // (count // 3)
    waits = kind == 1
    key = tiles + waits * count
    owner = slot_map // own_tiles
    together = owner[:, None] == owner[None, :]
    first = own_tiles // 2
    last = min(own_tiles, own_tiles - first + SLACK)
    place = jnp.sum(together & (key[None, :] < key[:, None]), axis=1, dtype=jnp.int32)
    early = (place < first) & ~waits
    behind = jnp.sum(
        together & ~early[None, :] & (key[None, :] < key[:, None]), axis=1, dtype=jnp.int32
    )
    late = ~early & (behind < last)
    repair = ~early & ~late

    def rows_where(chosen, position, rows):
        return jnp.where(chosen, owner * rows + position * TILE, -1)

    early_rows, late_rows = first * TILE, last * TILE
    plans = (
        (rows_where(early, place, early_rows), early_rows),
        (rows_where(late, behind, late_rows), late_rows),
        (rows_where(repair, behind - last, early_rows), early_rows),
    )
    in_owner = jnp.where(early, place, first + behind) * TILE
    rank = lax.axis_index("dp")
    slots = rank * own_tiles + jnp.arange(own_tiles, dtype=jnp.int32)
    own_rows = jnp.sum(
        jnp.where(slot_map[None, :] == slots[:, None], in_owner[None, :], 0), axis=1, dtype=jnp.int32
    )
    return plans, own_rows, jnp.any(repair).astype(F32)


def on_device(
    tokens,
    cotangent,
    doc_ids,
    tile_slots,
    matrix_tiles,
    left_stats,
    right_stats,
    left_roots,
    right_roots,
    side_weight,
    side_moment,
    side_second,
    vector_params,
    vector_moment,
    vector_second,
):
    n_tensor = lax.axis_size("tensor")
    n_dp = lax.axis_size("dp")
    tensor_rank = lax.axis_index("tensor")
    core = tensor_rank % 2
    di_local = DI // n_tensor
    heads_local = HEADS // n_tensor
    model_local = D // n_tensor
    bc_local = 2 * NS // n_tensor
    rows = tokens.shape[0]
    half = rows // 2
    sequences, seq_len = doc_ids.shape
    slot_map = tile_slots[0]
    own_tiles = matrix_tiles.shape[1]
    side_rows = side_weight.shape[0] * SIDE // TILE
    fetch_rows, order, first_tiles, misfetch = fetch_plan(
        slot_map, own_tiles, side_rows
    )
    plans, own_rows, misfit = tile_plan(slot_map, own_tiles)
    misfits = sum_over(jnp.full((8, LANES), misfit), "tensor")
    vector = vector_params[0]
    bounds = segment_bounds(di_local, heads_local, model_local, bc_local, CONV)

    def segment_of(index):
        return vector[bounds[index] : bounds[index + 1]]

    conv_kernel = segment_of(0).reshape(CONV, di_local)
    conv_offset = segment_of(1)
    gate_gain = segment_of(2)
    log_rate = segment_of(3)
    skip_gain = segment_of(4)
    dt_offset = segment_of(5)

    mine = matrix_tiles[0].astype(BF16)[order].reshape(own_tiles * TILE, TILE)
    cut = first_tiles * TILE
    first_share = jnp.concatenate(
        [mine[:cut], side_weight.astype(BF16).reshape(side_rows, TILE)], axis=0
    )
    first_held = lax.all_gather(first_share, "dp", axis=0, tiled=True)
    second_held = lax.all_gather(mine[cut:], "dp", axis=0, tiled=True)
    shared = lax.all_gather(vector[bounds[6] :][None, :], "tensor", axis=0, tiled=True)
    pre_gain = shared[:, :model_local].reshape(D)
    bc_kernel = (
        shared[:, model_local : model_local + CONV * bc_local]
        .reshape(n_tensor, CONV, bc_local)
        .transpose(1, 0, 2)
        .reshape(CONV, 2 * NS)
    )
    bc_offset = shared[:, model_local + CONV * bc_local :].reshape(2 * NS)
    par = jnp.concatenate(
        [
            conv_kernel,
            conv_offset[None],
            jnp.repeat(skip_gain, di_local // heads_local)[None],
            gate_gain[None],
            jnp.zeros((1, di_local), F32),
        ],
        axis=0,
    )
    bcpar = jnp.concatenate([bc_kernel, bc_offset[None], jnp.zeros((3, 2 * NS), F32)], axis=0)
    decay_rate = -jnp.exp(log_rate)
    hp = jnp.pad(
        jnp.stack([dt_offset, decay_rate * LOG2E, decay_rate]), ((0, 5), (0, LANES - heads_local))
    )
    pick = (
        jnp.arange(di_local)[:, None] // (di_local // heads_local) == jnp.arange(LANES)[None, :]
    ).astype(BF16)
    starts = jnp.sum(doc_ids[:, None, :] < doc_ids[:, :, None], axis=2).astype(F32).reshape(rows)
    ends = jnp.sum(doc_ids[:, None, :] <= doc_ids[:, :, None], axis=2).astype(F32).reshape(rows)
    start_row = starts[None, :]
    start_wide = jnp.broadcast_to(starts[:, None], (rows, LANES))
    end_wide = jnp.broadcast_to(ends[:, None], (rows, LANES))

    residual = tokens.astype(F32)
    inverse = lax.rsqrt(jnp.mean(residual * residual, axis=1, keepdims=True) + EPS)
    normed = (residual * inverse * pre_gain).astype(BF16)
    normed, misfits = tied(normed, misfits)
    misfit = misfits[0, 0] > 0.0

    side_copy = first_held.reshape(n_dp, -1, TILE)[:, cut:].reshape(D, SIDE)
    side_cols = jnp.concatenate(
        [
            side_copy[:, : 2 * NS],
            lax.dynamic_slice_in_dim(side_copy, 2 * NS + tensor_rank * heads_local, heads_local, 1),
            jnp.zeros((D, 2 * NS - heads_local), BF16),
        ],
        axis=1,
    )
    per_block = (D // TILE) * (di_local // TILE)
    rest_shape = ((D, di_local + side_cols.shape[1]),)

    rest_rows = fetch_rows[per_block : 2 * per_block]

    def forward_with(rows, helds):
        weights = assemble(rows, helds, (side_cols,), rest_shape)[0]
        projected = project(normed, weights)
        scanned = ssd_forward(projected, start_wide, par, bcpar, hp, sequences)
        return (weights, projected, *scanned)

    tried = forward_with(
        jnp.minimum(rest_rows, first_held.shape[0] - TILE), (first_held,)
    )
    tried, second_held = tied(tried, second_held)
    w_rest, rest, ssd, states = lax.while_loop(
        lambda carry: carry[0],
        lambda carry: (False, forward_with(rest_rows, (first_held, second_held))),
        (misfetch, tried),
    )[1]
    w_gate, w_output = assemble(
        jnp.concatenate([fetch_rows[:per_block], fetch_rows[2 * per_block :]]),
        (first_held, second_held),
        (),
        ((D, di_local), (di_local, D)),
    )
    gate, d_hidden, sums = gate_project(
        normed, cotangent, w_gate, w_output, ssd, gate_gain[None, :]
    )
    sums = sum_over(sums, "tensor")
    core_at = core[None].astype(jnp.int32)
    hidden, d_gate, d_ssd, gain_sums, out_sent, out_kept = gated_pass(
        core_at, ssd, gate, d_hidden, sums, gate_gain[None, :], w_output
    )

    def chip_sum(kept, sent):
        return (kept.astype(F32) + swap(sent, "tensor", 1).astype(F32)).astype(BF16)

    out_chip = chip_sum(out_kept, out_sent)
    grad_output = contract_rows(hidden, cotangent).astype(BF16)
    out_chip, normed_now = tied(out_chip, normed)
    out_others = [swap(part, "tensor", 2) for part in jnp.split(out_chip, 2)]
    grad_gate = contract_rows(normed_now, d_gate).astype(BF16)
    early_grads = spread(
        jnp.concatenate([plans[0][0][:per_block], plans[0][0][2 * per_block :]]),
        (grad_gate, grad_output),
        n_dp * plans[0][1],
    )
    d_ssd, early_grads = tied(d_ssd, early_grads)
    early = OwnerSum(early_grads, ((0, 1), (2, 3)))
    given = (states, start_wide, end_wide, start_row, par, bcpar, hp, pick, sequences)
    place = (tensor_rank * heads_local).astype(jnp.int32)[None]
    back, parts, side_parts = (), [], []
    for sequence in range(sequences):
        d_rest, d_side, *sums_here = ssd_backward(sequence, back, place, rest, d_ssd, *given)
        parts.append(sums_here)
        if sequence == 0:
            d_rest, out_others[0] = early.first((d_rest, out_others[0]))
        else:
            d_rest, side_parts[-1] = tied(d_rest, side_parts[-1])
        side_parts.append((d_side, swap(d_side, "tensor", 1)))
        back = (d_rest,)
    gx, gbc, gh = (sum(terms) for terms in zip(*parts))
    d_rest, out_others[1] = early.second((back[0], out_others[1]))

    split_side = sequences // 2
    side_chips = [
        jnp.concatenate([(own + other).astype(BF16) for own, other in part], axis=0)
        for part in (side_parts[:split_side], side_parts[split_side:])
    ]
    d_rest, side_chips[0] = tied(d_rest, side_chips[0])
    side_others = [swap(side_chips[0], "tensor", 2)]
    grad_input = contract_rows(normed, d_rest[:, :di_local]).astype(BF16)
    late_grads = spread(plans[1][0], (grad_gate, grad_input, grad_output), n_dp * plans[1][1])
    late_grads, side_chips[1], side_others[0], d_rest = early.third(
        (late_grads, side_chips[1], side_others[0], d_rest)
    )
    side_others.append(swap(side_chips[1], "tensor", 2))
    late = OwnerSum(late_grads, ((0,), (1,), (2, 3)))
    d_sent, pre_sent = normed_grad(1 - core_at, 16, d_gate, d_rest, tokens, w_gate, w_rest)
    early_share, (d_sent, d_rest) = early.total((d_sent, d_rest))
    d_sent, d_rest = late.first((d_sent, d_rest))
    d_kept, pre_kept = normed_grad(core_at, 0, d_gate, d_rest, tokens, w_gate, w_rest)
    d_kept, side_others[1] = late.second((d_kept, side_others[1]))
    grad_pre = jnp.sum(pre_sent + pre_kept, axis=0)
    d_chip = chip_sum(d_kept, d_sent)
    d_others = [swap(part, "tensor", 2) for part in jnp.split(d_chip, 4)]
    d_others[0], early_share = late.third((d_others[0], early_share))

    side_total = jnp.concatenate(
        [
            (own.astype(F32) + other.astype(F32)).astype(BF16)
            for own, other in zip(side_chips, side_others)
        ],
        axis=0,
    )
    side_total, d_others[0] = tied(side_total, d_others[0])
    grad_side = lax.dynamic_index_in_dim(
        contract_rows(normed, side_total).reshape(n_dp, n_tensor, -1, side_total.shape[1]),
        tensor_rank,
        1,
        keepdims=False,
    )[:, :, :SIDE]
    gx_sums = jnp.sum(gx.reshape(CONV + 2, 8, di_local), axis=1)
    gbc_sums = jnp.sum(gbc.reshape(CONV + 1, 8, 2 * NS), axis=1)
    gh_sums = jnp.sum(gh.reshape(2, 8, LANES), axis=1)[:, :heads_local]
    own_vector = jnp.concatenate(
        [
            gx_sums[: CONV + 1].reshape(-1),
            jnp.sum(gain_sums, axis=0),
            gh_sums[0],
            jnp.sum(gx_sums[CONV + 1].reshape(heads_local, -1), axis=1),
            gh_sums[1],
        ]
    )
    small_sums = SharedSums(
        grad_side.reshape(n_dp, -1), jnp.concatenate([own_vector, grad_pre, gbc_sums.reshape(-1)])
    )
    small_sums.exchange()
    late_share, (small_sums.owned, d_others[1]) = late.total((small_sums.owned, d_others[1]))
    small_sums.exchange_rest()
    late_share, misfit = tied(late_share, misfit)

    def repaired(grads):
        again = spread(plans[2][0], grads, n_dp * plans[2][1])
        return lax.psum_scatter(again, "dp", scatter_dimension=0, tiled=True).astype(F32)

    repair_share = lax.cond(
        misfit,
        repaired,
        lambda grads: jnp.zeros((plans[2][1], TILE), F32),
        (grad_gate, grad_input, grad_output),
    )

    tile_share, left_new, right_new, tiles_new, tiles_copy = update_tiles(
        own_rows,
        early_share,
        late_share,
        repair_share,
        matrix_tiles[0],
        left_stats[0],
        right_stats[0],
        left_roots[0],
        right_roots[0],
    )
    tiles_copy, d_others[2] = tied(tiles_copy, d_others[2])
    split_at = own_vector.shape[0]
    side_own, all_vector = small_sums.owned, small_sums.shared
    quarters = jnp.where(
        (jnp.arange(n_tensor) == tensor_rank)[:, None], side_own, jnp.zeros((), F32)
    )
    common = sum_over(
        jnp.concatenate([quarters.reshape(-1), all_vector[split_at:]])[None], "tensor"
    )[0]
    side_share = common[: side_weight.size].reshape(side_weight.shape)
    common = common[side_weight.size :]
    quarter = half // 2
    mixed_own = [
        (
            lax.dynamic_slice_in_dim(tokens, core * half + i * quarter, quarter, 0).astype(F32)
            + (out_chip[i * quarter : (i + 1) * quarter].astype(F32) + out_others[i].astype(F32))
        ).astype(BF16)
        for i in range(2)
    ]
    mixed_other = [swap(part, "tensor", 1) for part in mixed_own]
    lower_half = core == 0
    mixed = jnp.concatenate(
        [jnp.where(lower_half, own, other) for own, other in zip(mixed_own, mixed_other)]
        + [jnp.where(lower_half, other, own) for own, other in zip(mixed_own, mixed_other)],
        axis=0,
    )

    d_half = (d_chip.astype(F32) + jnp.concatenate(d_others).astype(F32)).astype(BF16)
    d_half_other = swap(d_half, "tensor", 1)
    input_grad = input_grads(core_at, d_half, d_half_other, tokens, cotangent, pre_gain[None, :])

    pre_share = lax.dynamic_slice_in_dim(common[:D], tensor_rank * model_local, model_local, 0)
    bc_share = lax.dynamic_slice_in_dim(
        common[D:].reshape(CONV + 1, 2 * NS), tensor_rank * bc_local, bc_local, 1
    )
    vector_total = jnp.concatenate([all_vector[:split_at], pre_share, bc_share.reshape(-1)])[None]

    side_m, side_v, side_new = adam_update(
        side_weight, side_moment, side_second, side_share, LR_SIDE
    )
    vec_m, vec_v, vec_new = adam_update(
        vector_params, vector_moment, vector_second, vector_total, LR_VEC
    )
    return (
        mixed,
        input_grad,
        tile_share[None],
        left_new[None],
        right_new[None],
        tiles_new[None],
        tiles_copy[None],
        side_m,
        side_v,
        side_new,
        vec_m,
        vec_v,
        vec_new,
    )


def solution(mesh):
    by_dp = P("dp", None)
    by_tensor = P("tensor", None)
    by_tile = P("tensor", "dp", None, None)
    return jax.shard_map(
        on_device,
        mesh=mesh,
        in_specs=(by_dp,) * 3
        + (by_tensor,)
        + (by_tile,) * 5
        + (by_dp,) * 3
        + (by_tensor,) * 3,
        out_specs=(by_dp,) * 2 + (by_tile,) * 5 + (by_dp,) * 3 + (by_tensor,) * 3,
        check_vma=False,
    )
```

```python
import functools

import jax
import jax.numpy as jnp
from jax import lax
from jax.experimental import pallas as pl
from jax.experimental.pallas import tpu as pltpu
from jax.sharding import PartitionSpec as P

D = 2048
HEADS = 64
NS = 128
CONV = 4
TILE = 128
STEP = 10
DI = 4096
SIDE = 320
BLK = 128
LANES = 128
MID_ROWS = 512
TILES_STEP = 6
COPY_ROWS = 16
SLACK = 2
ONE_PASS = True

EPS = 1e-05
HIGH = lax.Precision.HIGHEST
STAT_DECAY = 0.5
LR_MAT = 0.25
LR_SIDE = 0.02
LR_VEC = 0.25
BETA_ONE = 0.9
BETA_TWO = 0.95
ADAM_EPS = 1e-08
DECAY_WD = 0.1
LOG2E = 1.4426950408889634
FAR = -1e30
VMEM_LIMIT = 60 * 1024 * 1024

F32 = jnp.float32
BF16 = jnp.bfloat16

NN = (((1,), (0,)), ((), ()))
NT = (((1,), (1,)), ((), ()))


def segment_bounds(di_local, heads_local, model_local, bc_local, tap_count):
    widths = [
        tap_count * di_local,
        di_local,
        di_local,
        heads_local,
        heads_local,
        heads_local,
        model_local,
        tap_count * bc_local,
        bc_local,
    ]
    bounds = [0]
    for item in widths:
        bounds.append(bounds[-1] + item)
    return bounds


def adam_update(weight, moment, second, gradient, learn_rate):
    moment_new = BETA_ONE * moment + (1.0 - BETA_ONE) * gradient
    second_new = BETA_TWO * second + (1.0 - BETA_TWO) * gradient * gradient
    corrected = moment_new / (1.0 - BETA_ONE**STEP)
    scaled = jnp.sqrt(second_new / (1.0 - BETA_TWO**STEP)) + ADAM_EPS
    return (moment_new, second_new, weight - learn_rate * (corrected / scaled + DECAY_WD * weight))


def contract_rows(left, right):
    return lax.dot_general(left, right, (((0,), (0,)), ((), ())), preferred_element_type=F32)


def contract_cols(left, right):
    return lax.dot_general(left, right, NT, preferred_element_type=F32)


def swap(value, axis, bit):
    size = lax.axis_size(axis)
    return lax.ppermute(value, axis, [(i, i ^ bit) for i in range(size)])


def sum_over(value, axis):
    bit = 1
    while bit < lax.axis_size(axis):
        value = value + swap(value, axis, bit)
        bit *= 2
    return value


class SharedSums:
    def __init__(self, owned, shared):
        self.owned, self.shared = owned, shared
        self.bit = lax.axis_size("dp") // 2

    def send(self):
        upper = (lax.axis_index("dp") // self.bit) % 2
        pairs = self.owned.reshape(2, -1, self.owned.shape[1])
        sent = lax.dynamic_index_in_dim(pairs, 1 - upper, 0, keepdims=False)
        self.kept = lax.dynamic_index_in_dim(pairs, upper, 0, keepdims=False)
        return swap(jnp.concatenate([sent.reshape(-1), self.shared])[None], "dp", self.bit)

    def add(self, arrived):
        size = self.kept.size
        self.owned = self.kept + arrived[0, :size].reshape(self.kept.shape)
        self.shared = self.shared + arrived[0, size:]
        self.bit //= 2

    def finish(self):
        while self.bit > 0:
            self.add(self.send())


class OwnerSum:
    def __init__(self, grads, groups):
        owners = lax.axis_size("dp")
        self.grads = grads.reshape(owners, -1, TILE)
        self.lined = owners == 8
        if not self.lined:
            return
        me = lax.axis_index("dp")
        x, z = me % 2, me // 2
        self.low = z < 2
        order = [jnp.where(self.low, z + 3 - k, z + 1 + k) % 4 for k in range(4)]
        self.own = [self.part(seg, x) for seg in order]
        self.found = [(i, group.index(k)) for k in range(4) for i, group in enumerate(groups) if k in group]
        self.groups = [
            swap(jnp.concatenate([self.part(order[k], 1 - x) for k in group]), "dp", 1)
            for group in groups
        ]

    def part(self, seg, x):
        return lax.dynamic_index_in_dim(self.grads, seg * 2 + x, 0, keepdims=False)

    def pair_sum(self, k):
        rows = self.own[k].shape[0]
        group, place = self.found[k]
        arrived = self.groups[group][place * rows : (place + 1) * rows]
        return self.own[k].astype(F32) + arrived.astype(F32)

    def hop(self, value, moves):
        pairs = [(2 * a + x, 2 * b + x) for a, b in moves for x in (0, 1)]
        return lax.ppermute(value.astype(BF16), "dp", pairs)


    def first(self, other):
        if self.lined:
            self.groups[0], other = tied(self.groups[0], other)
            self.ahead = self.hop(self.pair_sum(0), [(0, 1), (3, 2)])
        return other

    def second(self, other):
        if self.lined:
            needed = self.found[1][0]
            self.ahead, self.groups[needed], other = tied(self.ahead, self.groups[needed], other)
            value = self.pair_sum(1) + self.ahead.astype(F32)
            self.up = self.hop(value, [(0, 1), (1, 2)])
            self.down = self.hop(value, [(3, 2), (2, 1)])
        return other

    def third(self, other):
        if self.lined:
            needed = self.found[2][0]
            self.up, self.down, self.groups[needed], other = tied(
                self.up, self.down, self.groups[needed], other
            )
            near, far = self.pair_sum(2), self.pair_sum(0)
            up = jnp.where(self.low, near, far) + self.up.astype(F32)
            down = jnp.where(self.low, far, near) + self.down.astype(F32)
            self.up = self.hop(up, [(0, 1), (1, 2), (2, 3)])
            self.down = self.hop(down, [(3, 2), (2, 1), (1, 0)])
        return other

    def total(self, other):
        if not self.lined:
            flat = self.grads.reshape(-1, TILE)
            return lax.psum_scatter(flat, "dp", scatter_dimension=0, tiled=True).astype(F32), other
        self.up, self.down, self.groups[-1], other = tied(
            self.up, self.down, self.groups[-1], other
        )
        return self.pair_sum(3) + (self.up.astype(F32) + self.down.astype(F32)), other


def tied(*values):
    return lax.optimization_barrier(values)


def halves(value):
    high = value.astype(BF16)
    return high, (value - high.astype(F32)).astype(BF16)


def dot(left, right, dims=NN):
    return lax.dot_general(left, right, dims, preferred_element_type=F32)


def product(left, right, dims=NN):
    return dot(left.astype(BF16), right.astype(BF16), dims)


def by_halves(left, right):
    both = dot(left.astype(BF16), jnp.concatenate(halves(right), axis=1))
    return both[:, : right.shape[1]] + both[:, right.shape[1] :]


def careful(left, right, dims=NN):
    left_high, left_low = halves(left)
    right_high, right_low = halves(right)
    return dot(
        jnp.concatenate([left_high, left_low, left_high], axis=1),
        jnp.concatenate([right_high, right_high, right_low], axis=dims[0][1][0]),
        dims,
    )


def summed(mask, value):
    high, rest = halves(value)
    low = (value - high.astype(F32) - rest.astype(F32)).astype(BF16)
    mask = mask.astype(BF16)
    return dot(jnp.concatenate([mask] * 3, axis=1), jnp.concatenate([high, rest, low], axis=0))


def sigmoid(value):
    return 0.5 * jnp.tanh(0.5 * value) + 0.5


def softplus(value):
    return jnp.maximum(value, 0.0) + jnp.log1p(jnp.exp(-jnp.abs(value)))


def taps_of(padded, lanes, masks):
    rows = masks[0].shape[0]
    shifted = [padded[8 : 8 + rows, lanes]]
    for shift in range(1, CONV):
        shifted.append(padded[8 - shift : 8 - shift + rows, lanes] * masks[shift - 1])
    return shifted


def convolve(shifted, params, lanes):
    total = params[CONV : CONV + 1, lanes]
    for shift in range(CONV):
        total = total + params[CONV - 1 - shift : CONV - shift, lanes] * shifted[shift]
    return total


def wide(column, shape):
    return jnp.broadcast_to(column, shape)


def ssd_forward_kernel(
    rest_ref, prev_ref, start_ref, par_ref, bcpar_ref, hp_ref,
    ssd_ref, states_ref, xs, ss, state, tails, keeps,
):
    width = ssd_ref.shape[1]
    pairs = width // LANES
    shape = (BLK, LANES)
    base_i = pl.program_id(1) * BLK
    base = base_i.astype(F32)

    @pl.when(pl.program_id(1) == 0)
    def _():
        state[...] = jnp.zeros_like(state)

    xs[0:8, :] = prev_ref[:, 0:width]
    xs[8 : 8 + BLK, :] = rest_ref[:, 0:width]
    ss[0:8, :] = prev_ref[:, width : width + 2 * NS]
    ss[8 : 8 + BLK, :] = rest_ref[:, width : width + 2 * NS]
    start = start_ref[...]
    row = (lax.broadcasted_iota(jnp.int32, shape, 0) + base_i).astype(F32)
    col = (lax.broadcasted_iota(jnp.int32, shape, 1) + base_i).astype(F32)
    lane = lax.broadcasted_iota(jnp.int32, shape, 1)
    low = lane < LANES // 2
    pos = row - start
    masks = [jnp.where(pos >= float(k), 1.0, 0.0) for k in range(1, CONV)]
    bias = jnp.where((col >= start) & (col <= row), 0.0, FAR)
    carried = start < base
    last_start = start_ref[BLK - 1 : BLK, :]
    tail_ok = row >= last_start
    keep_ok = last_start < base

    acts = []
    for part in range(2):
        lanes = slice(part * NS, (part + 1) * NS)
        raw = convolve(taps_of(ss, lanes, masks), bcpar_ref, lanes)
        acts.append(raw * sigmoid(raw))
    b_act, c_act = acts
    first_step = width + 2 * NS
    steps = softplus(rest_ref[:, first_step : first_step + LANES] + hp_ref[0:1, :])
    lower = jnp.where(col <= row, 1.0, 0.0)
    cum = summed(lower, steps * hp_ref[1:2, :])
    cum_t = cum.T
    scores = careful(c_act, b_act, NT)
    states_ref[0] = state[...]
    from_state = product(c_act, state[...])
    for pair in range(pairs):
        lanes = slice(pair * LANES, (pair + 1) * LANES)
        raw = convolve(taps_of(xs, lanes, masks), par_ref, lanes)
        act = raw * sigmoid(raw)
        col_a = wide(cum[:, 2 * pair : 2 * pair + 1], shape)
        col_b = wide(cum[:, 2 * pair + 1 : 2 * pair + 2], shape)
        both = jnp.where(low, col_a, col_b)
        step_both = jnp.where(
            low,
            wide(steps[:, 2 * pair : 2 * pair + 1], shape),
            wide(steps[:, 2 * pair + 1 : 2 * pair + 2], shape),
        )
        scaled = act * step_both
        weight_a = scores * jnp.exp2(col_a - cum_t[2 * pair : 2 * pair + 1, :] + bias)
        weight_b = scores * jnp.exp2(col_b - cum_t[2 * pair + 1 : 2 * pair + 2, :] + bias)
        inner = by_halves(
            jnp.concatenate([weight_a, weight_b], axis=1),
            jnp.concatenate([jnp.where(low, scaled, 0.0), jnp.where(low, 0.0, scaled)], axis=0),
        )
        carry = jnp.where(carried, jnp.exp2(both), 0.0)
        ssd_ref[:, lanes] = inner + carry * from_state[:, lanes] + par_ref[5:6, lanes] * act
        last = both[BLK - 1 : BLK, :]
        tails[:, lanes] = scaled * jnp.where(tail_ok, jnp.exp2(last - both), 0.0)
        keeps[0:1, lanes] = jnp.where(keep_ok, jnp.exp2(last), 0.0)
    state[...] = keeps[0:1, :] * state[...] + product(b_act.T, tails[...])


def ssd_backward_kernel(
    *refs,
):
    held = max(len(refs) - 27, 0)
    ssd_backward_body(*refs[held:])


def ssd_backward_body(
    place_ref, rest_ref, prev_ref, dy_ref, states_ref, start_ref, end_ref, srow_ref,
    par_ref, bcpar_ref, hp_ref, pick_ref,
    drest_ref, dside_ref, gx_ref, gbc_ref, gh_ref,
    xs, ss, dxs, dbs, dstate, tails, carries, terms, rows_in, keeps,
):
    width = dy_ref.shape[1]
    pairs = width // LANES
    shape = (BLK, LANES)
    blocks = pl.num_programs(0)
    base_i = (blocks - 1 - pl.program_id(0)) * BLK
    base = base_i.astype(F32)

    @pl.when(pl.program_id(0) == 0)
    def _():
        gx_ref[...] = jnp.zeros_like(gx_ref)
        gbc_ref[...] = jnp.zeros_like(gbc_ref)
        gh_ref[...] = jnp.zeros_like(gh_ref)
        rows_in[...] = jnp.zeros_like(rows_in)
        dxs[0:8, :] = jnp.zeros((8, width), F32)
        dbs[0:8, :] = jnp.zeros((8, 2 * NS), F32)
        dstate[...] = jnp.zeros_like(dstate)

    dxs[BLK : BLK + 8, :] = dxs[0:8, :]
    dbs[BLK : BLK + 8, :] = dbs[0:8, :]
    xs[0:8, :] = prev_ref[:, 0:width]
    xs[8 : 8 + BLK, :] = rest_ref[:, 0:width]
    ss[0:8, :] = prev_ref[:, width : width + 2 * NS]
    ss[8 : 8 + BLK, :] = rest_ref[:, width : width + 2 * NS]
    start = start_ref[...]
    row_i = lax.broadcasted_iota(jnp.int32, shape, 0)
    lane = lax.broadcasted_iota(jnp.int32, shape, 1)
    row = (row_i + base_i).astype(F32)
    col = (lane + base_i).astype(F32)
    low = lane < LANES // 2
    pos = row - start
    left = end_ref[...] - row
    masks = [jnp.where(pos >= float(k), 1.0, 0.0) for k in range(1, CONV)]
    after = [jnp.where(left > float(k), 1.0, 0.0) for k in range(1, CONV)]
    bias_t = jnp.where((row >= srow_ref[...]) & (row <= col), 0.0, FAR)
    carried = start < base
    last_start = start_ref[BLK - 1 : BLK, :]
    tail_ok = row >= last_start
    keep_ok = last_start < base

    acts, slopes, bc_taps = [], [], []
    for part in range(2):
        lanes = slice(part * NS, (part + 1) * NS)
        shifted = taps_of(ss, lanes, masks)
        raw = convolve(shifted, bcpar_ref, lanes)
        sig = sigmoid(raw)
        acts.append(raw * sig)
        slopes.append(sig * (1.0 + raw * (1.0 - sig)))
        bc_taps.append(shifted)
    b_act, c_act = acts
    first_step = width + 2 * NS
    raw_steps = rest_ref[:, first_step : first_step + LANES] + hp_ref[0:1, :]
    steps = softplus(raw_steps)
    lower = jnp.where(col <= row, 1.0, 0.0)
    upper = jnp.where(col >= row, 1.0, 0.0)
    cum = summed(lower, steps * hp_ref[1:2, :])
    cum_t = cum.T
    scores_t = careful(b_act, c_act, NT)
    old = states_ref[0]
    from_state = product(c_act, old)
    from_next = product(b_act, dstate[...])
    d_scores = jnp.zeros(shape, F32)
    direct = jnp.zeros(shape, F32)

    def add_rows(ref, first, lanes, value):
        ref[first : first + 8, lanes] += jnp.sum(value.reshape(BLK // 8, 8, value.shape[1]), axis=0)

    for pair in range(pairs):
        lanes = slice(pair * LANES, (pair + 1) * LANES)
        shifted = taps_of(xs, lanes, masks)
        raw = convolve(shifted, par_ref, lanes)
        sig = sigmoid(raw)
        act = raw * sig
        dy = dy_ref[:, lanes]
        cols = [wide(cum[:, h : h + 1], shape) for h in (2 * pair, 2 * pair + 1)]
        step_cols = [wide(steps[:, h : h + 1], shape) for h in (2 * pair, 2 * pair + 1)]
        both = jnp.where(low, cols[0], cols[1])
        step_both = jnp.where(low, step_cols[0], step_cols[1])
        parts = [jnp.where(low, act, 0.0), jnp.where(low, 0.0, act)]
        dy_high, dy_low = halves(dy)
        dy_wide = jnp.concatenate([dy_high, dy_high, dy_low], axis=1)
        high, rest = halves(jnp.concatenate(parts, axis=0))
        inners = dot(jnp.concatenate([high, rest, high], axis=1), dy_wide, NT)
        weights = []
        for which in range(2):
            head = 2 * pair + which
            decay = jnp.exp2(cum_t[head : head + 1, :] - cols[which] + bias_t)
            inner = inners[which * BLK : (which + 1) * BLK, :]
            weight = decay * scores_t
            weights.append(weight)
            d_scores = d_scores + decay * inner * step_cols[which]
            pulled = weight * inner
            direct = jnp.where(lane == head, jnp.sum(pulled, axis=1, keepdims=True), direct)
            rows_in[head : head + 1, :] = jnp.sum(pulled * step_cols[which], axis=0, keepdims=True)
        d_intra = by_halves(
            jnp.concatenate(weights, axis=1),
            jnp.concatenate([jnp.where(low, dy, 0.0), jnp.where(low, 0.0, dy)], axis=0),
        )
        last = both[BLK - 1 : BLK, :]
        tail = jnp.where(tail_ok, jnp.exp2(last - both), 0.0)
        d_tail = tail * from_next[:, lanes]
        terms[0:BLK, lanes] = act * d_tail
        tails[:, lanes] = act * step_both * tail
        carry = dy * jnp.where(carried, jnp.exp2(both), 0.0)
        carries[:, lanes] = carry
        terms[BLK : 2 * BLK, lanes] = carry * from_state[:, lanes]
        keeps[0:1, lanes] = jnp.where(keep_ok, jnp.exp2(last), 0.0)
        d_act = step_both * (d_intra + d_tail) + par_ref[5:6, lanes] * dy
        d_conv = d_act * (sig * (1.0 + raw * (1.0 - sig)))
        dxs[0:BLK, lanes] = d_conv
        for shift in range(CONV):
            add_rows(gx_ref, 8 * (CONV - 1 - shift), lanes, d_conv * shifted[shift])
        add_rows(gx_ref, 8 * CONV, lanes, d_conv)
        add_rows(gx_ref, 8 * (CONV + 1), lanes, dy * act)
        d_in = par_ref[CONV - 1 : CONV, lanes] * d_conv
        for shift in range(1, CONV):
            d_in = d_in + par_ref[CONV - 1 - shift : CONV - shift, lanes] * (
                after[shift - 1] * dxs[shift : shift + BLK, lanes]
            )
        drest_ref[:, lanes] = d_in.astype(BF16)

    stay = keeps[0:1, :] * jnp.sum((old * dstate[...]).reshape(NS // 8, 8, width), axis=0)
    terms[2 * BLK : 2 * BLK + 8, :] = stay
    by_head = dot(terms[...].astype(BF16), pick_ref[...])
    at_heads = by_head[0:BLK, :]
    stay_heads = jnp.sum(by_head[2 * BLK : 2 * BLK + 8, :], axis=0, keepdims=True)
    direct = direct + at_heads
    d_cum = rows_in[...].T + by_head[BLK : 2 * BLK, :] - steps * direct
    at_last = jnp.sum(steps * at_heads, axis=0, keepdims=True) + stay_heads
    through = summed(upper, d_cum) + at_last
    decay_rate = hp_ref[2:3, :]
    d_steps = direct + decay_rate * through
    d_raw = d_steps * sigmoid(raw_steps)
    every = slice(0, LANES)
    add_rows(gh_ref, 0, every, decay_rate * steps * through)
    add_rows(gh_ref, 8, every, d_raw)
    dside_ref[:, 2 * NS :] = pltpu.roll(d_raw, place_ref[0], 1)
    drest_ref[:, first_step : first_step + LANES] = d_raw.astype(BF16)
    drest_ref[:, first_step + LANES :] = jnp.zeros(
        (BLK, drest_ref.shape[1] - first_step - LANES), BF16
    )
    d_b = careful(d_scores, c_act) + product(tails[...], dstate[...], NT)
    d_c = careful(d_scores.T, b_act) + product(carries[...], old, NT)
    for part, value in ((0, d_b), (1, d_c)):
        lanes = slice(part * NS, (part + 1) * NS)
        d_conv = value * slopes[part]
        dbs[0:BLK, lanes] = d_conv
        for shift in range(CONV):
            add_rows(gbc_ref, 8 * (CONV - 1 - shift), lanes, d_conv * bc_taps[part][shift])
        add_rows(gbc_ref, 8 * CONV, lanes, d_conv)
        d_in = bcpar_ref[CONV - 1 : CONV, lanes] * d_conv
        for shift in range(1, CONV):
            d_in = d_in + bcpar_ref[CONV - 1 - shift : CONV - shift, lanes] * (
                after[shift - 1] * dbs[shift : shift + BLK, lanes]
            )
        dside_ref[:, lanes] = d_in
        drest_ref[:, width + part * NS : width + (part + 1) * NS] = d_in.astype(BF16)
    dstate[...] = keeps[0:1, :] * dstate[...] + product(c_act.T, carries[...])


def ssd_forward(rest, starts, par, bcpar, hp, sequences):
    rows, width = rest.shape[0], par.shape[1]
    blocks = rows // sequences // BLK
    here = lambda s, b: (s * blocks + b, 0)
    before = lambda s, b: (jnp.maximum((s * blocks + b) * (BLK // 8) - 1, 0), 0)
    fixed = lambda s, b: (0, 0)
    return pl.pallas_call(
        ssd_forward_kernel,
        grid=(sequences, blocks),
        in_specs=[
            pl.BlockSpec((BLK, rest.shape[1]), here),
            pl.BlockSpec((8, rest.shape[1]), before),
            pl.BlockSpec((BLK, LANES), here),
            pl.BlockSpec(par.shape, fixed),
            pl.BlockSpec(bcpar.shape, fixed),
            pl.BlockSpec(hp.shape, fixed),
        ],
        out_specs=[
            pl.BlockSpec((BLK, width), here),
            pl.BlockSpec((1, NS, width), lambda s, b: (s * blocks + b, 0, 0)),
        ],
        out_shape=[
            jax.ShapeDtypeStruct((rows, width), F32),
            jax.ShapeDtypeStruct((sequences * blocks, NS, width), F32),
        ],
        scratch_shapes=[
            pltpu.VMEM((BLK + 8, width), F32),
            pltpu.VMEM((BLK + 8, 2 * NS), F32),
            pltpu.VMEM((NS, width), F32),
            pltpu.VMEM((BLK, width), F32),
            pltpu.VMEM((8, width), F32),
        ],
        compiler_params=pltpu.CompilerParams(vmem_limit_bytes=VMEM_LIMIT),
        cost_estimate=pl.CostEstimate(
            flops=40 * rows * BLK * width, bytes_accessed=20 * rows * width, transcendentals=0
        ),
        name="ssd_forward",
    )(rest, rest, starts, par, bcpar, hp)


def ssd_backward(
    sequence, before_it, place, rest, d_ssd, states, starts, ends, start_row, par, bcpar, hp, pick, sequences
):
    rows, width = d_ssd.shape
    rest_width = rest.shape[1]
    blocks = rows // sequences // BLK
    at = lambda b: sequence * blocks + blocks - 1 - b
    here = lambda b: (at(b), 0)
    before = lambda b: (jnp.maximum(at(b) * (BLK // 8) - 1, 0), 0)
    fixed = lambda b: (0, 0)
    return pl.pallas_call(
        ssd_backward_kernel,
        grid=(blocks,),
        in_specs=[pl.BlockSpec(memory_space=pl.ANY)] * len(before_it)
        + [
            pl.BlockSpec(memory_space=pltpu.SMEM),
            pl.BlockSpec((BLK, rest_width), here),
            pl.BlockSpec((8, rest_width), before),
            pl.BlockSpec((BLK, width), here),
            pl.BlockSpec((1, NS, width), lambda b: (at(b), 0, 0)),
            pl.BlockSpec((BLK, LANES), here),
            pl.BlockSpec((BLK, LANES), here),
            pl.BlockSpec((1, BLK), lambda b: (0, at(b))),
            pl.BlockSpec(par.shape, fixed),
            pl.BlockSpec(bcpar.shape, fixed),
            pl.BlockSpec(hp.shape, fixed),
            pl.BlockSpec(pick.shape, fixed),
        ],
        out_specs=[
            pl.BlockSpec((BLK, rest_width), here),
            pl.BlockSpec((BLK, 2 * NS + LANES), lambda b: (blocks - 1 - b, 0)),
            pl.BlockSpec((8 * (CONV + 2), width), fixed),
            pl.BlockSpec((8 * (CONV + 1), 2 * NS), fixed),
            pl.BlockSpec((16, LANES), fixed),
        ],
        out_shape=[
            jax.ShapeDtypeStruct((rows, rest_width), BF16),
            jax.ShapeDtypeStruct((rows // sequences, 2 * NS + LANES), F32),
            jax.ShapeDtypeStruct((8 * (CONV + 2), width), F32),
            jax.ShapeDtypeStruct((8 * (CONV + 1), 2 * NS), F32),
            jax.ShapeDtypeStruct((16, LANES), F32),
        ],
        scratch_shapes=[
            pltpu.VMEM((BLK + 8, width), F32),
            pltpu.VMEM((BLK + 8, 2 * NS), F32),
            pltpu.VMEM((BLK + 8, width), F32),
            pltpu.VMEM((BLK + 8, 2 * NS), F32),
            pltpu.VMEM((NS, width), F32),
            pltpu.VMEM((BLK, width), F32),
            pltpu.VMEM((BLK, width), F32),
            pltpu.VMEM((2 * BLK + 8, width), F32),
            pltpu.VMEM((LANES, BLK), F32),
            pltpu.VMEM((8, width), F32),
        ],
        input_output_aliases={i: i for i in range(len(before_it))},
        compiler_params=pltpu.CompilerParams(vmem_limit_bytes=VMEM_LIMIT),
        cost_estimate=pl.CostEstimate(
            flops=100 * rows * BLK * width // sequences,
            bytes_accessed=4 * rows * 5 * width // sequences,
            transcendentals=0,
        ),
        name="ssd_backward",
    )(*before_it, place, rest, rest, d_ssd, states, starts, ends, start_row, par, bcpar, hp, pick)


def resident(array):
    return pl.BlockSpec(
        array.shape, lambda *i: (0,) * array.ndim, pipeline_mode=pl.Buffered(buffer_count=1)
    )


def matmul_kernel(left_ref, right_ref, out_ref):
    out_ref[...] = dot(left_ref[...], right_ref[...])


def project(normed, weights):
    rows = normed.shape[0]
    step = min(MID_ROWS, rows)
    width = weights.shape[1]
    here = lambda i: (i, 0)
    return pl.pallas_call(
        matmul_kernel,
        grid=(rows // step,),
        in_specs=[pl.BlockSpec((step, D), here), resident(weights)],
        out_specs=pl.BlockSpec((step, width), here),
        out_shape=jax.ShapeDtypeStruct((rows, width), F32),
        compiler_params=pltpu.CompilerParams(vmem_limit_bytes=VMEM_LIMIT),
        cost_estimate=pl.CostEstimate(
            flops=2 * rows * D * width,
            bytes_accessed=4 * rows * width + 2 * D * (rows + width),
            transcendentals=0,
        ),
        name="project",
    )(normed, weights)


def gate_kernel(normed_ref, cot_ref, wgate_ref, wout_ref, ssd_ref, gain_ref, gate_ref, dh_ref, sums_ref):
    gate_ref[...] = dot(normed_ref[...], wgate_ref[...])
    dh_ref[...] = dot(cot_ref[...], wout_ref[...], NT)
    rows, width = ssd_ref.shape
    for first in range(0, rows, LANES):
        at = slice(first, first + LANES)
        squares = jnp.zeros((LANES, LANES), F32)
        inners = jnp.zeros((LANES, LANES), F32)
        for piece in range(width // LANES):
            lanes = slice(piece * LANES, (piece + 1) * LANES)
            gate = gate_ref[at, lanes]
            gated = ssd_ref[at, lanes] * (gate * sigmoid(gate))
            squares = squares + gated * gated
            inners = inners + dh_ref[at, lanes] * gain_ref[0:1, lanes] * gated
        sums_ref[0:1, at] = jnp.sum(squares.T, axis=0, keepdims=True)
        sums_ref[1:2, at] = jnp.sum(inners.T, axis=0, keepdims=True)
    sums_ref[2:8, :] = jnp.zeros((6, rows), F32)


def gate_project(normed, cotangent, w_gate, w_output, ssd, gain):
    rows, width = ssd.shape
    step = min(MID_ROWS, rows)
    here = lambda i: (i, 0)
    return pl.pallas_call(
        gate_kernel,
        grid=(rows // step,),
        in_specs=[
            pl.BlockSpec((step, D), here),
            pl.BlockSpec((step, D), here),
            resident(w_gate),
            resident(w_output),
            pl.BlockSpec((step, width), here),
            pl.BlockSpec((1, width), lambda i: (0, 0)),
        ],
        out_specs=[
            pl.BlockSpec((step, width), here),
            pl.BlockSpec((step, width), here),
            pl.BlockSpec((8, step), lambda i: (0, i)),
        ],
        out_shape=[
            jax.ShapeDtypeStruct((rows, width), F32),
            jax.ShapeDtypeStruct((rows, width), F32),
            jax.ShapeDtypeStruct((8, rows), F32),
        ],
        compiler_params=pltpu.CompilerParams(vmem_limit_bytes=VMEM_LIMIT),
        cost_estimate=pl.CostEstimate(
            flops=4 * rows * D * width, bytes_accessed=16 * rows * width, transcendentals=0
        ),
        name="gate_project",
    )(normed, cotangent, w_gate, w_output, ssd, gain)


def gated_kernel(
    core_ref, ssd_ref, gate_ref, dh_ref, sums_ref, gain_ref, wout_ref,
    hidden_ref, dgate_ref, dssd_ref, gain_out, sent_ref, kept_ref,
):
    @pl.when(pl.program_id(0) == 0)
    def _():
        gain_out[...] = jnp.zeros_like(gain_out)

    width = ssd_ref.shape[1]
    rows = ssd_ref.shape[0]
    scale = lax.rsqrt(sums_ref[0:1, :] / DI + EPS)
    shift = scale * scale * scale * (sums_ref[1:2, :] / DI)
    turned = jnp.concatenate([scale] * 8 + [shift] * 8 + [jnp.zeros((LANES - 16, rows), F32)], axis=0).T
    chunk = min(64, rows)
    for first in range(0, rows, chunk):
        at = slice(first, first + chunk)
        scales = wide(turned[at, 0:1], (chunk, LANES))
        shifts = wide(turned[at, 8:9], (chunk, LANES))
        for piece in range(width // LANES):
            lanes = slice(piece * LANES, (piece + 1) * LANES)
            gate = gate_ref[at, lanes]
            ssd = ssd_ref[at, lanes]
            d_hidden = dh_ref[at, lanes]
            gain = gain_ref[0:1, lanes]
            sig = sigmoid(gate)
            act = gate * sig
            gated = ssd * act
            unit = gated * scales
            hidden_ref[at, lanes] = (unit * gain).astype(BF16)
            gain_out[:, lanes] += jnp.sum((d_hidden * unit).reshape(chunk // 8, 8, LANES), axis=0)
            d_gated = scales * (d_hidden * gain) - gated * shifts
            dssd_ref[at, lanes] = d_gated * act
            dgate_ref[at, lanes] = (
                d_gated * ssd * (sig * (1.0 + gate * (1.0 - sig)))
            ).astype(BF16)
    mixed = dot(hidden_ref[...], wout_ref[...]).astype(BF16)
    steps = pl.num_programs(0) // 2

    @pl.when(pl.program_id(0) < steps)
    def _():
        sent_ref[...] = mixed

    @pl.when(pl.program_id(0) >= steps)
    def _():
        kept_ref[...] = mixed


def gated_pass(core, ssd, gate, d_hidden, sums, gain, w_output):
    rows, width = ssd.shape
    step = min(MID_ROWS, rows // 2)
    steps = rows // step // 2

    def at(i, core):
        half = jnp.where(i < steps, 1 - core[0], core[0])
        return half * steps + i % steps

    here = lambda i, core: (at(i, core), 0)
    fixed = lambda i, core: (0, 0)
    return pl.pallas_call(
        gated_kernel,
        grid_spec=pltpu.PrefetchScalarGridSpec(
            num_scalar_prefetch=1,
            grid=(2 * steps,),
            in_specs=[
                pl.BlockSpec((step, width), here),
                pl.BlockSpec((step, width), here),
                pl.BlockSpec((step, width), here),
                pl.BlockSpec((8, step), lambda i, core: (0, at(i, core))),
                pl.BlockSpec((1, width), fixed),
                resident(w_output),
            ],
            out_specs=[
                pl.BlockSpec((step, width), here),
                pl.BlockSpec((step, width), here),
                pl.BlockSpec((step, width), here),
                pl.BlockSpec((8, width), fixed),
                pl.BlockSpec((step, D), lambda i, core: (jnp.minimum(i, steps - 1), 0)),
                pl.BlockSpec((step, D), lambda i, core: (jnp.maximum(i - steps, 0), 0)),
            ],
        ),
        out_shape=[
            jax.ShapeDtypeStruct((rows, width), BF16),
            jax.ShapeDtypeStruct((rows, width), BF16),
            jax.ShapeDtypeStruct((rows, width), F32),
            jax.ShapeDtypeStruct((8, width), F32),
            jax.ShapeDtypeStruct((rows // 2, D), BF16),
            jax.ShapeDtypeStruct((rows // 2, D), BF16),
        ],
        compiler_params=pltpu.CompilerParams(vmem_limit_bytes=VMEM_LIMIT),
        cost_estimate=pl.CostEstimate(
            flops=2 * rows * width * D, bytes_accessed=20 * rows * width, transcendentals=0
        ),
        name="gated_pass",
    )(core, ssd, gate, d_hidden, sums, gain, w_output)


def unit_rows(tokens_ref):
    rows = tokens_ref[...].astype(F32)
    inverse = lax.rsqrt(jnp.mean(rows * rows, axis=1, keepdims=True) + EPS)
    return rows, inverse


def normed_grad_kernel(half_ref, dgate_ref, drest_ref, tokens_ref, wgate_ref, wrest_ref, out_ref, gain_out):
    @pl.when(pl.program_id(0) == 0)
    def _():
        gain_out[...] = jnp.zeros_like(gain_out)

    total = dot(dgate_ref[...], wgate_ref[...], NT) + dot(drest_ref[...], wrest_ref[...], NT)
    out_ref[...] = total.astype(BF16)
    rows, inverse = unit_rows(tokens_ref)
    weighted = total * (rows * inverse)
    gain_out[...] += jnp.sum(weighted.reshape(-1, 8, D), axis=0)


def normed_grad(half, weight, d_gate, d_rest, tokens, w_gate, w_rest):
    rows = tokens.shape[0]
    step = min(MID_ROWS, rows // 2)
    steps = rows // step // 2
    here = lambda i, half: (half[0] * steps + i, 0)
    return pl.pallas_call(
        normed_grad_kernel,
        grid_spec=pltpu.PrefetchScalarGridSpec(
            num_scalar_prefetch=1,
            grid=(steps,),
            in_specs=[
                pl.BlockSpec((step, d_gate.shape[1]), here),
                pl.BlockSpec((step, d_rest.shape[1]), here),
                pl.BlockSpec((step, D), here),
                resident(w_gate),
                resident(w_rest),
            ],
            out_specs=[
                pl.BlockSpec((step, D), lambda i, half: (i, 0)),
                pl.BlockSpec((8, D), lambda i, half: (0, 0)),
            ],
        ),
        out_shape=[
            jax.ShapeDtypeStruct((rows // 2, D), BF16),
            jax.ShapeDtypeStruct((8, D), F32),
        ],
        compiler_params=pltpu.CompilerParams(vmem_limit_bytes=VMEM_LIMIT),
        cost_estimate=pl.CostEstimate(
            flops=weight * rows * D * (d_gate.shape[1] + d_rest.shape[1]),
            bytes_accessed=weight * 6 * rows * D,
            transcendentals=0,
        ),
        name="normed_grad",
    )(half, d_gate, d_rest, tokens, w_gate, w_rest)


def input_grad_kernel(core_ref, own_ref, other_ref, tokens_ref, cot_ref, gain_ref, out_ref, terms):
    steps = pl.num_programs(0) // 2
    mine = pl.program_id(0) // steps == core_ref[0]

    @pl.when(mine)
    def _():
        terms[...] = own_ref[...].astype(F32)

    @pl.when(jnp.logical_not(mine))
    def _():
        terms[...] = other_ref[...].astype(F32)

    rows, inverse = unit_rows(tokens_ref)
    weighted = terms[...] * gain_ref[0:1, :]
    inner = jnp.mean(weighted * rows, axis=1, keepdims=True)
    out_ref[...] = (
        cot_ref[...].astype(F32) + inverse * weighted - rows * (inverse * inverse * inverse * inner)
    )


def input_grads(core, own, other, tokens, cotangent, gain):
    rows = tokens.shape[0]
    step = min(MID_ROWS, rows // 2)
    steps = rows // step // 2
    here = lambda i, core: (i, 0)

    def part_at(is_own):
        def index(i, core):
            wanted = (i // steps == core[0]) == is_own
            parked = jnp.where((core[0] == 0) == is_own, steps - 1, 0)
            return (jnp.where(wanted, i % steps, parked), 0)

        return index

    return pl.pallas_call(
        input_grad_kernel,
        grid_spec=pltpu.PrefetchScalarGridSpec(
            num_scalar_prefetch=1,
            grid=(2 * steps,),
            in_specs=[
                pl.BlockSpec((step, D), part_at(True)),
                pl.BlockSpec((step, D), part_at(False)),
                pl.BlockSpec((step, D), here),
                pl.BlockSpec((step, D), here),
                pl.BlockSpec((1, D), lambda i, core: (0, 0)),
            ],
            out_specs=pl.BlockSpec((step, D), here),
            scratch_shapes=[pltpu.VMEM((step, D), F32)],
        ),
        out_shape=jax.ShapeDtypeStruct((rows, D), F32),
        compiler_params=pltpu.CompilerParams(vmem_limit_bytes=VMEM_LIMIT),
        cost_estimate=pl.CostEstimate(
            flops=0, bytes_accessed=10 * rows * D, transcendentals=0
        ),
        name="input_grads",
    )(core, own, other, tokens, cotangent, gain)


def held_rows(first):
    return (pl.ds(pl.multiple_of(first, COPY_ROWS), TILE), slice(None))


def band_tiles(ref):
    columns = ref.shape[1] // TILE
    for tile in range(columns * (ref.shape[0] // TILE)):
        down, across = tile // columns, tile % columns
        yield tile, (
            slice(down * TILE, (down + 1) * TILE),
            slice(across * TILE, (across + 1) * TILE),
        )


def copied(first, helds, ref, at):
    past = 0
    for held_ref in helds:
        size = held_ref.shape[0]
        if len(helds) == 1:
            ref[at] = held_ref[held_rows(first)]
        else:

            @pl.when((first >= past) & (first < past + size))
            def _(held_ref=held_ref, past=past):
                ref[at] = held_ref[held_rows(first - past)]

        past += size


def assemble_kernel(parts, width, rows_ref, *refs):
    helds = refs[:parts]
    band = pl.program_id(0)
    outs = refs[parts:]
    if width:
        outs[1][:, width:] = outs[0][...]
        outs = (outs[1].at[:, 0:width],)
    base = 0
    for ref in outs:
        count = (ref.shape[0] // TILE) * (ref.shape[1] // TILE)
        for tile, at in band_tiles(ref):
            copied(rows_ref[base + band * count + tile], helds, ref, at)
        base += count * pl.num_programs(0)


def assemble(rows, helds, side_cols, shapes):
    bands = min(shape[0] for shape in shapes) // TILE
    bands = min(bands, 8)
    here = lambda i: (i, 0)
    width = shapes[0][1] - side_cols[0].shape[1] if side_cols else 0
    return pl.pallas_call(
        functools.partial(assemble_kernel, len(helds), width),
        grid=(bands,),
        in_specs=[pl.BlockSpec(memory_space=pltpu.SMEM)]
        + [resident(held) for held in helds]
        + [pl.BlockSpec((side.shape[0] // bands, side.shape[1]), here) for side in side_cols],
        out_specs=[pl.BlockSpec((shape[0] // bands, shape[1]), here) for shape in shapes],
        out_shape=[jax.ShapeDtypeStruct(shape, BF16) for shape in shapes],
        compiler_params=pltpu.CompilerParams(vmem_limit_bytes=VMEM_LIMIT),
        cost_estimate=pl.CostEstimate(
            flops=0, bytes_accessed=4 * sum(held.size for held in helds), transcendentals=0
        ),
        name="assemble",
    )(rows, *helds, *side_cols)


def spread_kernel(rows_ref, *refs):
    out_ref = refs[-1]
    band = pl.program_id(0)
    base = 0
    for ref in refs[:-1]:
        count = (ref.shape[0] // TILE) * (ref.shape[1] // TILE)
        for tile, place in band_tiles(ref):
            first = rows_ref[base + band * count + tile]

            @pl.when(first >= 0)
            def _(first=first, place=place, ref=ref):
                out_ref[held_rows(first)] = ref[place]

        base += count * pl.num_programs(0)


def spread(grad_rows, grads, total_rows):
    bands = min(grad.shape[0] for grad in grads) // TILE
    return pl.pallas_call(
        spread_kernel,
        grid=(bands,),
        in_specs=[pl.BlockSpec(memory_space=pltpu.SMEM)]
        + [pl.BlockSpec((grad.shape[0] // bands, grad.shape[1]), lambda i: (i, 0)) for grad in grads],
        out_specs=pl.BlockSpec((total_rows, TILE), lambda i: (0, 0)),
        out_shape=jax.ShapeDtypeStruct((total_rows, TILE), BF16),
        compiler_params=pltpu.CompilerParams(vmem_limit_bytes=VMEM_LIMIT),
        cost_estimate=pl.CostEstimate(
            flops=0,
            bytes_accessed=2 * total_rows * TILE + sum(2 * grad.size for grad in grads),
            transcendentals=0,
        ),
        name="spread",
    )(grad_rows, *grads)


def update_kernel(
    rows_ref, early_ref, late_ref, repair_ref, tiles_ref, lstat_ref, rstat_ref, lroot_ref, rroot_ref,
    grads_out, left_out, right_out, tiles_out, copy_out, grad_tile,
):
    dot = functools.partial(lax.dot_general, dimension_numbers=NN, preferred_element_type=F32)
    step = tiles_ref.shape[0]
    for tile in range(step):
        first = rows_ref[pl.program_id(0) * step + tile]
        past = 0
        for source in (early_ref, late_ref, repair_ref):
            size = source.shape[0]

            @pl.when((first >= past) & (first < past + size))
            def _(source=source, past=past, tile=tile):
                grad_tile[tile] = source[held_rows(first - past)]

            past += size
    for tile in range(step):
        exact_grad = grad_tile[tile]
        grad = exact_grad.astype(BF16)
        turned = exact_grad.T.astype(BF16)
        grads_out[tile] = exact_grad
        left_out[tile] = STAT_DECAY * lstat_ref[tile] + (1.0 - STAT_DECAY) * dot(grad, turned)
        right_out[tile] = STAT_DECAY * rstat_ref[tile] + (1.0 - STAT_DECAY) * dot(turned, grad)
        shaped = careful(careful(lroot_ref[tile], exact_grad), rroot_ref[tile])
        updated = tiles_ref[tile] - LR_MAT * shaped
        tiles_out[tile] = updated
        copy_out[tile] = updated.astype(BF16)


def update_tiles(rows, early, late, repair, tiles, left_stats, right_stats, left_roots, right_roots):
    count = tiles.shape[0]
    step = TILES_STEP if count % TILES_STEP == 0 else 1
    spec = pl.BlockSpec((step, TILE, TILE), lambda i, rows: (i, 0, 0))
    sources = [pl.BlockSpec(part.shape, lambda i, rows: (0, 0)) for part in (early, late, repair)]
    whole = jax.ShapeDtypeStruct(tiles.shape, F32)
    return pl.pallas_call(
        update_kernel,
        grid_spec=pltpu.PrefetchScalarGridSpec(
            num_scalar_prefetch=1,
            grid=(count // step,),
            in_specs=sources + [spec] * 5,
            out_specs=[spec] * 5,
            scratch_shapes=[pltpu.VMEM((step, TILE, TILE), F32)],
        ),
        out_shape=[whole] * 4 + [jax.ShapeDtypeStruct(tiles.shape, BF16)],
        compiler_params=pltpu.CompilerParams(vmem_limit_bytes=VMEM_LIMIT),
        cost_estimate=pl.CostEstimate(
            flops=18 * count * TILE**3, bytes_accessed=42 * count * TILE**2, transcendentals=0
        ),
        name="update_tiles",
    )(rows, early, late, repair, tiles, left_stats, right_stats, left_roots, right_roots)


def fetch_plan(slot_map, own_tiles, side_rows):
    count = slot_map.shape[0]
    tiles = jnp.arange(count, dtype=jnp.int32)
    waits = tiles // (count // 3) != 1
    key = tiles + waits * count
    owner = slot_map // own_tiles
    together = owner[:, None] == owner[None, :]
    place = jnp.sum(together & (key[None, :] < key[:, None]), axis=1, dtype=jnp.int32)
    first = max(1, own_tiles * 13 // 24)
    first_rows, second_rows = first * TILE + side_rows, (own_tiles - first) * TILE
    early = place < first
    owners = count // own_tiles
    rows = jnp.where(
        early,
        owner * first_rows + place * TILE,
        owners * first_rows + owner * second_rows + (place - first) * TILE,
    )
    rank = lax.axis_index("dp")
    places = jnp.arange(own_tiles, dtype=jnp.int32)
    order = jnp.sum(
        jnp.where(
            (owner == rank)[None, :] & (place[None, :] == places[:, None]),
            slot_map[None, :] - rank * own_tiles,
            0,
        ),
        axis=1,
        dtype=jnp.int32,
    )
    return rows, order, first, jnp.any(~waits & ~early)


def tile_plan(slot_map, own_tiles):
    count = slot_map.shape[0]
    tiles = jnp.arange(count, dtype=jnp.int32)
    kind = tiles // (count // 3)
    waits = kind == 1
    key = tiles + waits * count
    owner = slot_map // own_tiles
    together = owner[:, None] == owner[None, :]
    first = own_tiles // 2
    last = min(own_tiles, own_tiles - first + SLACK)
    place = jnp.sum(together & (key[None, :] < key[:, None]), axis=1, dtype=jnp.int32)
    early = (place < first) & ~waits
    behind = jnp.sum(
        together & ~early[None, :] & (key[None, :] < key[:, None]), axis=1, dtype=jnp.int32
    )
    late = ~early & (behind < last)
    repair = ~early & ~late

    def rows_where(chosen, position, rows):
        return jnp.where(chosen, owner * rows + position * TILE, -1)

    early_rows, late_rows = first * TILE, last * TILE
    plans = (
        (rows_where(early, place, early_rows), early_rows),
        (rows_where(late, behind, late_rows), late_rows),
        (rows_where(repair, behind - last, early_rows), early_rows),
    )
    in_owner = jnp.where(early, place, first + behind) * TILE
    rank = lax.axis_index("dp")
    slots = rank * own_tiles + jnp.arange(own_tiles, dtype=jnp.int32)
    own_rows = jnp.sum(
        jnp.where(slot_map[None, :] == slots[:, None], in_owner[None, :], 0), axis=1, dtype=jnp.int32
    )
    return plans, own_rows, jnp.any(repair).astype(F32)


def on_device(
    tokens,
    cotangent,
    doc_ids,
    tile_slots,
    matrix_tiles,
    left_stats,
    right_stats,
    left_roots,
    right_roots,
    side_weight,
    side_moment,
    side_second,
    vector_params,
    vector_moment,
    vector_second,
):
    n_tensor = lax.axis_size("tensor")
    n_dp = lax.axis_size("dp")
    tensor_rank = lax.axis_index("tensor")
    core = tensor_rank % 2
    di_local = DI // n_tensor
    heads_local = HEADS // n_tensor
    model_local = D // n_tensor
    bc_local = 2 * NS // n_tensor
    rows = tokens.shape[0]
    half = rows // 2
    sequences, seq_len = doc_ids.shape
    slot_map = tile_slots[0]
    own_tiles = matrix_tiles.shape[1]
    side_rows = side_weight.shape[0] * SIDE // TILE
    fetch_rows, order, first_tiles, misfetch = fetch_plan(
        slot_map, own_tiles, side_rows
    )
    plans, own_rows, misfit = tile_plan(slot_map, own_tiles)
    misfits = sum_over(jnp.full((8, LANES), misfit), "tensor")
    vector = vector_params[0]
    bounds = segment_bounds(di_local, heads_local, model_local, bc_local, CONV)

    def segment_of(index):
        return vector[bounds[index] : bounds[index + 1]]

    conv_kernel = segment_of(0).reshape(CONV, di_local)
    conv_offset = segment_of(1)
    gate_gain = segment_of(2)
    log_rate = segment_of(3)
    skip_gain = segment_of(4)
    dt_offset = segment_of(5)

    mine = matrix_tiles[0].astype(BF16)[order].reshape(own_tiles * TILE, TILE)
    cut = first_tiles * TILE
    first_share = jnp.concatenate(
        [mine[:cut], side_weight.astype(BF16).reshape(side_rows, TILE)], axis=0
    )
    first_held = lax.all_gather(first_share, "dp", axis=0, tiled=True)
    second_held = lax.all_gather(mine[cut:], "dp", axis=0, tiled=True)
    shared = lax.all_gather(vector[bounds[6] :][None, :], "tensor", axis=0, tiled=True)
    pre_gain = shared[:, :model_local].reshape(D)
    bc_kernel = (
        shared[:, model_local : model_local + CONV * bc_local]
        .reshape(n_tensor, CONV, bc_local)
        .transpose(1, 0, 2)
        .reshape(CONV, 2 * NS)
    )
    bc_offset = shared[:, model_local + CONV * bc_local :].reshape(2 * NS)
    par = jnp.concatenate(
        [
            conv_kernel,
            conv_offset[None],
            jnp.repeat(skip_gain, di_local // heads_local)[None],
            gate_gain[None],
            jnp.zeros((1, di_local), F32),
        ],
        axis=0,
    )
    bcpar = jnp.concatenate([bc_kernel, bc_offset[None], jnp.zeros((3, 2 * NS), F32)], axis=0)
    decay_rate = -jnp.exp(log_rate)
    hp = jnp.pad(
        jnp.stack([dt_offset, decay_rate * LOG2E, decay_rate]), ((0, 5), (0, LANES - heads_local))
    )
    pick = (
        jnp.arange(di_local)[:, None] // (di_local // heads_local) == jnp.arange(LANES)[None, :]
    ).astype(BF16)
    starts = jnp.sum(doc_ids[:, None, :] < doc_ids[:, :, None], axis=2).astype(F32).reshape(rows)
    ends = jnp.sum(doc_ids[:, None, :] <= doc_ids[:, :, None], axis=2).astype(F32).reshape(rows)
    start_row = starts[None, :]
    start_wide = jnp.broadcast_to(starts[:, None], (rows, LANES))
    end_wide = jnp.broadcast_to(ends[:, None], (rows, LANES))

    residual = tokens.astype(F32)
    inverse = lax.rsqrt(jnp.mean(residual * residual, axis=1, keepdims=True) + EPS)
    normed = (residual * inverse * pre_gain).astype(BF16)
    normed, misfits = tied(normed, misfits)
    misfit = misfits[0, 0] > 0.0

    side_copy = first_held.reshape(n_dp, -1, TILE)[:, cut:].reshape(D, SIDE)
    side_cols = jnp.concatenate(
        [
            side_copy[:, : 2 * NS],
            lax.dynamic_slice_in_dim(side_copy, 2 * NS + tensor_rank * heads_local, heads_local, 1),
            jnp.zeros((D, 2 * NS - heads_local), BF16),
        ],
        axis=1,
    )
    per_block = (D // TILE) * (di_local // TILE)
    rest_shape = ((D, di_local + side_cols.shape[1]),)

    rest_rows = fetch_rows[per_block : 2 * per_block]

    def forward_with(rows, helds):
        weights = assemble(rows, helds, (side_cols,), rest_shape)[0]
        projected = project(normed, weights)
        scanned = ssd_forward(projected, start_wide, par, bcpar, hp, sequences)
        return (weights, projected, *scanned)

    tried = forward_with(
        jnp.minimum(rest_rows, first_held.shape[0] - TILE), (first_held,)
    )
    tried, second_held = tied(tried, second_held)
    w_rest, rest, ssd, states = lax.while_loop(
        lambda carry: carry[0],
        lambda carry: (False, forward_with(rest_rows, (first_held, second_held))),
        (misfetch, tried),
    )[1]
    w_gate, w_output = assemble(
        jnp.concatenate([fetch_rows[:per_block], fetch_rows[2 * per_block :]]),
        (first_held, second_held),
        (),
        ((D, di_local), (di_local, D)),
    )
    gate, d_hidden, sums = gate_project(
        normed, cotangent, w_gate, w_output, ssd, gate_gain[None, :]
    )
    sums = sum_over(sums, "tensor")
    core_at = core[None].astype(jnp.int32)
    hidden, d_gate, d_ssd, gain_sums, out_sent, out_kept = gated_pass(
        core_at, ssd, gate, d_hidden, sums, gate_gain[None, :], w_output
    )

    def chip_sum(kept, sent):
        return (kept.astype(F32) + swap(sent, "tensor", 1).astype(F32)).astype(BF16)

    out_chip = chip_sum(out_kept, out_sent)
    grad_output = contract_rows(hidden, cotangent).astype(BF16)
    out_chip, normed_now = tied(out_chip, normed)
    out_others = [swap(part, "tensor", 2) for part in jnp.split(out_chip, 2)]
    grad_gate = contract_rows(normed_now, d_gate).astype(BF16)
    early_grads = spread(
        jnp.concatenate([plans[0][0][:per_block], plans[0][0][2 * per_block :]]),
        (grad_gate, grad_output),
        n_dp * plans[0][1],
    )
    d_ssd, early_grads = tied(d_ssd, early_grads)
    early = OwnerSum(early_grads, ((0, 1), (2, 3)))
    given = (states, start_wide, end_wide, start_row, par, bcpar, hp, pick, sequences)
    place = (tensor_rank * heads_local).astype(jnp.int32)[None]
    back, parts, side_parts = (), [], []
    for sequence in range(sequences):
        d_rest, d_side, *sums_here = ssd_backward(sequence, back, place, rest, d_ssd, *given)
        parts.append(sums_here)
        if sequence == 0:
            d_rest, out_others[0] = early.first((d_rest, out_others[0]))
        else:
            d_rest, side_parts[-1] = tied(d_rest, side_parts[-1])
        side_parts.append((d_side, swap(d_side, "tensor", 1)))
        back = (d_rest,)
    gx, gbc, gh = (sum(terms) for terms in zip(*parts))
    d_rest, out_others[1] = early.second((back[0], out_others[1]))

    split_side = sequences // 2
    side_chips = [
        jnp.concatenate([(own + other).astype(BF16) for own, other in part], axis=0)
        for part in (side_parts[:split_side], side_parts[split_side:])
    ]
    d_rest, side_chips[0] = tied(d_rest, side_chips[0])
    side_others = [swap(side_chips[0], "tensor", 2)]
    d_sent, pre_sent = normed_grad(1 - core_at, 16, d_gate, d_rest, tokens, w_gate, w_rest)
    d_sent, side_chips[1], side_others[0], d_rest = early.third(
        (d_sent, side_chips[1], side_others[0], d_rest)
    )
    side_others.append(swap(side_chips[1], "tensor", 2))
    d_kept, pre_kept = normed_grad(core_at, 0, d_gate, d_rest, tokens, w_gate, w_rest)
    early_share, (d_kept, side_others[1]) = early.total((d_kept, side_others[1]))
    grad_pre = jnp.sum(pre_sent + pre_kept, axis=0)
    d_chip, d_rest = tied(chip_sum(d_kept, d_sent), d_rest)
    d_others = [swap(part, "tensor", 2) for part in jnp.split(d_chip, 4)]
    grad_input = contract_rows(normed, d_rest[:, :di_local]).astype(BF16)
    late_grads = spread(plans[1][0], (grad_gate, grad_input, grad_output), n_dp * plans[1][1])
    late_grads, d_others[0] = tied(late_grads, d_others[0])
    late = OwnerSum(late_grads, ((0,), (1,), (2,), (3,)))

    side_total = jnp.concatenate(
        [
            (own.astype(F32) + other.astype(F32)).astype(BF16)
            for own, other in zip(side_chips, side_others)
        ],
        axis=0,
    )
    side_total, d_others[1], out_chip, out_others, early_share, grad_pre = late.first(
        (side_total, d_others[1], out_chip, out_others, early_share, grad_pre)
    )
    grad_side = lax.dynamic_index_in_dim(
        contract_rows(normed, side_total).reshape(n_dp, n_tensor, -1, side_total.shape[1]),
        tensor_rank,
        1,
        keepdims=False,
    )[:, :, :SIDE]
    gx_sums = jnp.sum(gx.reshape(CONV + 2, 8, di_local), axis=1)
    gbc_sums = jnp.sum(gbc.reshape(CONV + 1, 8, 2 * NS), axis=1)
    gh_sums = jnp.sum(gh.reshape(2, 8, LANES), axis=1)[:, :heads_local]
    own_vector = jnp.concatenate(
        [
            gx_sums[: CONV + 1].reshape(-1),
            jnp.sum(gain_sums, axis=0),
            gh_sums[0],
            jnp.sum(gx_sums[CONV + 1].reshape(heads_local, -1), axis=1),
            gh_sums[1],
        ]
    )
    small_sums = SharedSums(
        grad_side.reshape(n_dp, -1), jnp.concatenate([own_vector, grad_pre, gbc_sums.reshape(-1)])
    )
    arrived, d_others[2] = late.second((small_sums.send(), d_others[2]))
    small_sums.add(arrived)
    arrived, d_others[3] = late.third((small_sums.send(), d_others[3]))
    small_sums.add(arrived)
    d_half = (d_chip.astype(F32) + jnp.concatenate(d_others).astype(F32)).astype(BF16)
    input_grad = input_grads(
        core_at, d_half, swap(d_half, "tensor", 1), tokens, cotangent, pre_gain[None, :]
    )
    late_share, (arrived, input_grad, misfit) = late.total(
        (small_sums.send(), input_grad, misfit)
    )
    small_sums.add(arrived)
    small_sums.finish()

    def repaired(grads):
        again = spread(plans[2][0], grads, n_dp * plans[2][1])
        return lax.psum_scatter(again, "dp", scatter_dimension=0, tiled=True).astype(F32)

    repair_share = lax.cond(
        misfit,
        repaired,
        lambda grads: jnp.zeros((plans[2][1], TILE), F32),
        (grad_gate, grad_input, grad_output),
    )

    tile_share, left_new, right_new, tiles_new, tiles_copy = update_tiles(
        own_rows,
        early_share,
        late_share,
        repair_share,
        matrix_tiles[0],
        left_stats[0],
        right_stats[0],
        left_roots[0],
        right_roots[0],
    )
    split_at = own_vector.shape[0]
    side_own, all_vector = small_sums.owned, small_sums.shared
    quarters = jnp.where(
        (jnp.arange(n_tensor) == tensor_rank)[:, None], side_own, jnp.zeros((), F32)
    )
    common = sum_over(
        jnp.concatenate([quarters.reshape(-1), all_vector[split_at:]])[None], "tensor"
    )[0]
    side_share = common[: side_weight.size].reshape(side_weight.shape)
    common = common[side_weight.size :]
    quarter = half // 2
    mixed_own = [
        (
            lax.dynamic_slice_in_dim(tokens, core * half + i * quarter, quarter, 0).astype(F32)
            + (out_chip[i * quarter : (i + 1) * quarter].astype(F32) + out_others[i].astype(F32))
        ).astype(BF16)
        for i in range(2)
    ]
    mixed_other = [swap(part, "tensor", 1) for part in mixed_own]
    lower_half = core == 0
    mixed = jnp.concatenate(
        [jnp.where(lower_half, own, other) for own, other in zip(mixed_own, mixed_other)]
        + [jnp.where(lower_half, other, own) for own, other in zip(mixed_own, mixed_other)],
        axis=0,
    )

    pre_share = lax.dynamic_slice_in_dim(common[:D], tensor_rank * model_local, model_local, 0)
    bc_share = lax.dynamic_slice_in_dim(
        common[D:].reshape(CONV + 1, 2 * NS), tensor_rank * bc_local, bc_local, 1
    )
    vector_total = jnp.concatenate([all_vector[:split_at], pre_share, bc_share.reshape(-1)])[None]

    side_m, side_v, side_new = adam_update(
        side_weight, side_moment, side_second, side_share, LR_SIDE
    )
    vec_m, vec_v, vec_new = adam_update(
        vector_params, vector_moment, vector_second, vector_total, LR_VEC
    )
    return (
        mixed,
        input_grad,
        tile_share[None],
        left_new[None],
        right_new[None],
        tiles_new[None],
        tiles_copy[None],
        side_m,
        side_v,
        side_new,
        vec_m,
        vec_v,
        vec_new,
    )


def solution(mesh):
    by_dp = P("dp", None)
    by_tensor = P("tensor", None)
    by_tile = P("tensor", "dp", None, None)
    return jax.shard_map(
        on_device,
        mesh=mesh,
        in_specs=(by_dp,) * 3
        + (by_tensor,)
        + (by_tile,) * 5
        + (by_dp,) * 3
        + (by_tensor,) * 3,
        out_specs=(by_dp,) * 2 + (by_tile,) * 5 + (by_dp,) * 3 + (by_tensor,) * 3,
        check_vma=False,
    )
```

```python
import functools

import jax
import jax.numpy as jnp
from jax import lax
from jax.experimental import pallas as pl
from jax.experimental.pallas import tpu as pltpu
from jax.sharding import PartitionSpec as P

D = 2048
HEADS = 64
NS = 128
CONV = 4
TILE = 128
STEP = 10
DI = 4096
SIDE = 320
BLK = 128
LANES = 128
MID_ROWS = 512
PART_ROWS = 256
TILES_STEP = 6
COPY_ROWS = 16
SLACK = 2
ONE_PASS = True

EPS = 1e-05
HIGH = lax.Precision.HIGHEST
STAT_DECAY = 0.5
LR_MAT = 0.25
LR_SIDE = 0.02
LR_VEC = 0.25
BETA_ONE = 0.9
BETA_TWO = 0.95
ADAM_EPS = 1e-08
DECAY_WD = 0.1
LOG2E = 1.4426950408889634
FAR = -1e30
VMEM_LIMIT = 60 * 1024 * 1024

F32 = jnp.float32
BF16 = jnp.bfloat16

NN = (((1,), (0,)), ((), ()))
NT = (((1,), (1,)), ((), ()))


def segment_bounds(di_local, heads_local, model_local, bc_local, tap_count):
    widths = [
        tap_count * di_local,
        di_local,
        di_local,
        heads_local,
        heads_local,
        heads_local,
        model_local,
        tap_count * bc_local,
        bc_local,
    ]
    bounds = [0]
    for item in widths:
        bounds.append(bounds[-1] + item)
    return bounds


def adam_update(weight, moment, second, gradient, learn_rate):
    moment_new = BETA_ONE * moment + (1.0 - BETA_ONE) * gradient
    second_new = BETA_TWO * second + (1.0 - BETA_TWO) * gradient * gradient
    corrected = moment_new / (1.0 - BETA_ONE**STEP)
    scaled = jnp.sqrt(second_new / (1.0 - BETA_TWO**STEP)) + ADAM_EPS
    return (moment_new, second_new, weight - learn_rate * (corrected / scaled + DECAY_WD * weight))


def contract_rows(left, right):
    return lax.dot_general(left, right, (((0,), (0,)), ((), ())), preferred_element_type=F32)


def contract_cols(left, right):
    return lax.dot_general(left, right, NT, preferred_element_type=F32)


def swap(value, axis, bit):
    size = lax.axis_size(axis)
    return lax.ppermute(value, axis, [(i, i ^ bit) for i in range(size)])


def sum_over(value, axis):
    bit = 1
    while bit < lax.axis_size(axis):
        value = value + swap(value, axis, bit)
        bit *= 2
    return value


class SharedSums:
    def __init__(self, owned, shared):
        self.owned, self.shared = owned, shared
        self.bit = lax.axis_size("dp") // 2

    def send(self):
        upper = (lax.axis_index("dp") // self.bit) % 2
        pairs = self.owned.reshape(2, -1, self.owned.shape[1])
        sent = lax.dynamic_index_in_dim(pairs, 1 - upper, 0, keepdims=False)
        self.kept = lax.dynamic_index_in_dim(pairs, upper, 0, keepdims=False)
        return swap(jnp.concatenate([sent.reshape(-1), self.shared])[None], "dp", self.bit)

    def add(self, arrived):
        size = self.kept.size
        self.owned = self.kept + arrived[0, :size].reshape(self.kept.shape)
        self.shared = self.shared + arrived[0, size:]
        self.bit //= 2

    def finish(self):
        while self.bit > 0:
            self.add(self.send())


class OwnerSum:
    def __init__(self, grads, groups):
        owners = lax.axis_size("dp")
        self.grads = grads.reshape(owners, -1, TILE)
        self.lined = owners == 8
        if not self.lined:
            return
        me = lax.axis_index("dp")
        x, z = me % 2, me // 2
        self.low = z < 2
        order = [jnp.where(self.low, z + 3 - k, z + 1 + k) % 4 for k in range(4)]
        self.own = [self.part(seg, x) for seg in order]
        self.found = [(i, group.index(k)) for k in range(4) for i, group in enumerate(groups) if k in group]
        self.groups = [
            swap(jnp.concatenate([self.part(order[k], 1 - x) for k in group]), "dp", 1)
            for group in groups
        ]

    def part(self, seg, x):
        return lax.dynamic_index_in_dim(self.grads, seg * 2 + x, 0, keepdims=False)

    def pair_sum(self, k):
        rows = self.own[k].shape[0]
        group, place = self.found[k]
        arrived = self.groups[group][place * rows : (place + 1) * rows]
        return self.own[k].astype(F32) + arrived.astype(F32)

    def hop(self, value, moves):
        pairs = [(2 * a + x, 2 * b + x) for a, b in moves for x in (0, 1)]
        return lax.ppermute(value.astype(BF16), "dp", pairs)


    def first(self, other):
        if self.lined:
            self.groups[0], other = tied(self.groups[0], other)
            self.ahead = self.hop(self.pair_sum(0), [(0, 1), (3, 2)])
        return other

    def second(self, other):
        if self.lined:
            needed = self.found[1][0]
            self.ahead, self.groups[needed], other = tied(self.ahead, self.groups[needed], other)
            value = self.pair_sum(1) + self.ahead.astype(F32)
            self.up = self.hop(value, [(0, 1), (1, 2)])
            self.down = self.hop(value, [(3, 2), (2, 1)])
        return other

    def third(self, other):
        if self.lined:
            needed = self.found[2][0]
            self.up, self.down, self.groups[needed], other = tied(
                self.up, self.down, self.groups[needed], other
            )
            near, far = self.pair_sum(2), self.pair_sum(0)
            up = jnp.where(self.low, near, far) + self.up.astype(F32)
            down = jnp.where(self.low, far, near) + self.down.astype(F32)
            self.up = self.hop(up, [(0, 1), (1, 2), (2, 3)])
            self.down = self.hop(down, [(3, 2), (2, 1), (1, 0)])
        return other

    def total(self, other):
        if not self.lined:
            flat = self.grads.reshape(-1, TILE)
            return lax.psum_scatter(flat, "dp", scatter_dimension=0, tiled=True).astype(F32), other
        self.up, self.down, self.groups[-1], other = tied(
            self.up, self.down, self.groups[-1], other
        )
        return self.pair_sum(3) + (self.up.astype(F32) + self.down.astype(F32)), other


def tied(*values):
    return lax.optimization_barrier(values)


def halves(value):
    high = value.astype(BF16)
    return high, (value - high.astype(F32)).astype(BF16)


def dot(left, right, dims=NN):
    return lax.dot_general(left, right, dims, preferred_element_type=F32)


def product(left, right, dims=NN):
    return dot(left.astype(BF16), right.astype(BF16), dims)


def by_halves(left, right):
    both = dot(left.astype(BF16), jnp.concatenate(halves(right), axis=1))
    return both[:, : right.shape[1]] + both[:, right.shape[1] :]


def careful(left, right, dims=NN):
    left_high, left_low = halves(left)
    right_high, right_low = halves(right)
    return dot(
        jnp.concatenate([left_high, left_low, left_high], axis=1),
        jnp.concatenate([right_high, right_high, right_low], axis=dims[0][1][0]),
        dims,
    )


def summed(mask, value):
    high, rest = halves(value)
    low = (value - high.astype(F32) - rest.astype(F32)).astype(BF16)
    mask = mask.astype(BF16)
    return dot(jnp.concatenate([mask] * 3, axis=1), jnp.concatenate([high, rest, low], axis=0))


def sigmoid(value):
    return 0.5 * jnp.tanh(0.5 * value) + 0.5


def softplus(value):
    return jnp.maximum(value, 0.0) + jnp.log1p(jnp.exp(-jnp.abs(value)))


def taps_of(padded, lanes, masks):
    rows = masks[0].shape[0]
    shifted = [padded[8 : 8 + rows, lanes]]
    for shift in range(1, CONV):
        shifted.append(padded[8 - shift : 8 - shift + rows, lanes] * masks[shift - 1])
    return shifted


def convolve(shifted, params, lanes):
    total = params[CONV : CONV + 1, lanes]
    for shift in range(CONV):
        total = total + params[CONV - 1 - shift : CONV - shift, lanes] * shifted[shift]
    return total


def wide(column, shape):
    return jnp.broadcast_to(column, shape)


def ssd_forward_kernel(
    rest_ref, prev_ref, start_ref, par_ref, bcpar_ref, hp_ref,
    ssd_ref, states_ref, xs, ss, state, tails, keeps,
):
    width = ssd_ref.shape[1]
    pairs = width // LANES
    shape = (BLK, LANES)
    base_i = pl.program_id(1) * BLK
    base = base_i.astype(F32)

    @pl.when(pl.program_id(1) == 0)
    def _():
        state[...] = jnp.zeros_like(state)

    xs[0:8, :] = prev_ref[:, 0:width]
    xs[8 : 8 + BLK, :] = rest_ref[:, 0:width]
    ss[0:8, :] = prev_ref[:, width : width + 2 * NS]
    ss[8 : 8 + BLK, :] = rest_ref[:, width : width + 2 * NS]
    start = start_ref[...]
    row = (lax.broadcasted_iota(jnp.int32, shape, 0) + base_i).astype(F32)
    col = (lax.broadcasted_iota(jnp.int32, shape, 1) + base_i).astype(F32)
    lane = lax.broadcasted_iota(jnp.int32, shape, 1)
    low = lane < LANES // 2
    pos = row - start
    masks = [jnp.where(pos >= float(k), 1.0, 0.0) for k in range(1, CONV)]
    bias = jnp.where((col >= start) & (col <= row), 0.0, FAR)
    carried = start < base
    last_start = start_ref[BLK - 1 : BLK, :]
    tail_ok = row >= last_start
    keep_ok = last_start < base

    acts = []
    for part in range(2):
        lanes = slice(part * NS, (part + 1) * NS)
        raw = convolve(taps_of(ss, lanes, masks), bcpar_ref, lanes)
        acts.append(raw * sigmoid(raw))
    b_act, c_act = acts
    first_step = width + 2 * NS
    steps = softplus(rest_ref[:, first_step : first_step + LANES] + hp_ref[0:1, :])
    lower = jnp.where(col <= row, 1.0, 0.0)
    cum = summed(lower, steps * hp_ref[1:2, :])
    cum_t = cum.T
    scores = careful(c_act, b_act, NT)
    states_ref[0] = state[...]
    from_state = product(c_act, state[...])
    for pair in range(pairs):
        lanes = slice(pair * LANES, (pair + 1) * LANES)
        raw = convolve(taps_of(xs, lanes, masks), par_ref, lanes)
        act = raw * sigmoid(raw)
        col_a = wide(cum[:, 2 * pair : 2 * pair + 1], shape)
        col_b = wide(cum[:, 2 * pair + 1 : 2 * pair + 2], shape)
        both = jnp.where(low, col_a, col_b)
        step_both = jnp.where(
            low,
            wide(steps[:, 2 * pair : 2 * pair + 1], shape),
            wide(steps[:, 2 * pair + 1 : 2 * pair + 2], shape),
        )
        scaled = act * step_both
        weight_a = scores * jnp.exp2(col_a - cum_t[2 * pair : 2 * pair + 1, :] + bias)
        weight_b = scores * jnp.exp2(col_b - cum_t[2 * pair + 1 : 2 * pair + 2, :] + bias)
        inner = by_halves(
            jnp.concatenate([weight_a, weight_b], axis=1),
            jnp.concatenate([jnp.where(low, scaled, 0.0), jnp.where(low, 0.0, scaled)], axis=0),
        )
        carry = jnp.where(carried, jnp.exp2(both), 0.0)
        ssd_ref[:, lanes] = inner + carry * from_state[:, lanes] + par_ref[5:6, lanes] * act
        last = both[BLK - 1 : BLK, :]
        tails[:, lanes] = scaled * jnp.where(tail_ok, jnp.exp2(last - both), 0.0)
        keeps[0:1, lanes] = jnp.where(keep_ok, jnp.exp2(last), 0.0)
    state[...] = keeps[0:1, :] * state[...] + product(b_act.T, tails[...])


def both_halves(left_high, left_low, right_high, right_low, low, which):
    mine = low if which == 0 else jnp.logical_not(low)

    def turned(value):
        return pltpu.roll(value.astype(F32), LANES // 2, 1)

    left_high, right_high = left_high.astype(F32), right_high.astype(F32)
    left = jnp.concatenate(
        [jnp.where(mine, left_high, turned(left_low)), jnp.where(mine, left_high, 0.0)], axis=1
    )
    right = jnp.concatenate(
        [
            jnp.where(mine, right_high, turned(right_high)),
            jnp.where(mine, right_low.astype(F32), 0.0),
        ],
        axis=1,
    )
    return dot(left.astype(BF16), right.astype(BF16), NT)


def ssd_backward_kernel(
    *refs,
):
    held = max(len(refs) - 27, 0)
    ssd_backward_body(*refs[held:])


def ssd_backward_body(
    place_ref, rest_ref, prev_ref, dy_ref, states_ref, start_ref, end_ref, srow_ref,
    par_ref, bcpar_ref, hp_ref, pick_ref,
    drest_ref, dside_ref, gx_ref, gbc_ref, gh_ref,
    xs, ss, dxs, dbs, dstate, tails, carries, terms, rows_in, keeps,
):
    width = dy_ref.shape[1]
    pairs = width // LANES
    shape = (BLK, LANES)
    blocks = pl.num_programs(0)
    base_i = (blocks - 1 - pl.program_id(0)) * BLK
    base = base_i.astype(F32)

    @pl.when(pl.program_id(0) == 0)
    def _():
        gx_ref[...] = jnp.zeros_like(gx_ref)
        gbc_ref[...] = jnp.zeros_like(gbc_ref)
        gh_ref[...] = jnp.zeros_like(gh_ref)
        rows_in[...] = jnp.zeros_like(rows_in)
        dxs[0:8, :] = jnp.zeros((8, width), F32)
        dbs[0:8, :] = jnp.zeros((8, 2 * NS), F32)
        dstate[...] = jnp.zeros_like(dstate)

    dxs[BLK : BLK + 8, :] = dxs[0:8, :]
    dbs[BLK : BLK + 8, :] = dbs[0:8, :]
    xs[0:8, :] = prev_ref[:, 0:width]
    xs[8 : 8 + BLK, :] = rest_ref[:, 0:width]
    ss[0:8, :] = prev_ref[:, width : width + 2 * NS]
    ss[8 : 8 + BLK, :] = rest_ref[:, width : width + 2 * NS]
    start = start_ref[...]
    row_i = lax.broadcasted_iota(jnp.int32, shape, 0)
    lane = lax.broadcasted_iota(jnp.int32, shape, 1)
    row = (row_i + base_i).astype(F32)
    col = (lane + base_i).astype(F32)
    low = lane < LANES // 2
    pos = row - start
    left = end_ref[...] - row
    masks = [jnp.where(pos >= float(k), 1.0, 0.0) for k in range(1, CONV)]
    after = [jnp.where(left > float(k), 1.0, 0.0) for k in range(1, CONV)]
    bias_t = jnp.where((row >= srow_ref[...]) & (row <= col), 0.0, FAR)
    carried = start < base
    last_start = start_ref[BLK - 1 : BLK, :]
    tail_ok = row >= last_start
    keep_ok = last_start < base

    acts, slopes, bc_taps = [], [], []
    for part in range(2):
        lanes = slice(part * NS, (part + 1) * NS)
        shifted = taps_of(ss, lanes, masks)
        raw = convolve(shifted, bcpar_ref, lanes)
        sig = sigmoid(raw)
        acts.append(raw * sig)
        slopes.append(sig * (1.0 + raw * (1.0 - sig)))
        bc_taps.append(shifted)
    b_act, c_act = acts
    first_step = width + 2 * NS
    raw_steps = rest_ref[:, first_step : first_step + LANES] + hp_ref[0:1, :]
    steps = softplus(raw_steps)
    lower = jnp.where(col <= row, 1.0, 0.0)
    upper = jnp.where(col >= row, 1.0, 0.0)
    cum = summed(lower, steps * hp_ref[1:2, :])
    cum_t = cum.T
    scores_t = careful(b_act, c_act, NT)
    old = states_ref[0]
    from_state = product(c_act, old)
    from_next = product(b_act, dstate[...])
    d_scores = jnp.zeros(shape, F32)
    direct = jnp.zeros(shape, F32)

    def add_rows(ref, first, lanes, value):
        ref[first : first + 8, lanes] += jnp.sum(value.reshape(BLK // 8, 8, value.shape[1]), axis=0)

    for pair in range(pairs):
        lanes = slice(pair * LANES, (pair + 1) * LANES)
        shifted = taps_of(xs, lanes, masks)
        raw = convolve(shifted, par_ref, lanes)
        sig = sigmoid(raw)
        act = raw * sig
        dy = dy_ref[:, lanes]
        cols = [wide(cum[:, h : h + 1], shape) for h in (2 * pair, 2 * pair + 1)]
        step_cols = [wide(steps[:, h : h + 1], shape) for h in (2 * pair, 2 * pair + 1)]
        both = jnp.where(low, cols[0], cols[1])
        step_both = jnp.where(low, step_cols[0], step_cols[1])
        act_high, act_low = halves(act)
        dy_high, dy_low = halves(dy)
        inners = [
            both_halves(act_high, act_low, dy_high, dy_low, low, which) for which in range(2)
        ]
        weights = []
        for which in range(2):
            head = 2 * pair + which
            decay = jnp.exp2(cum_t[head : head + 1, :] - cols[which] + bias_t)
            inner = inners[which]
            weight = decay * scores_t
            weights.append(weight)
            d_scores = d_scores + decay * inner * step_cols[which]
            pulled = weight * inner
            direct = jnp.where(lane == head, jnp.sum(pulled, axis=1, keepdims=True), direct)
            rows_in[head : head + 1, :] = jnp.sum(pulled * step_cols[which], axis=0, keepdims=True)
        d_intra = by_halves(
            jnp.concatenate(weights, axis=1),
            jnp.concatenate([jnp.where(low, dy, 0.0), jnp.where(low, 0.0, dy)], axis=0),
        )
        last = both[BLK - 1 : BLK, :]
        tail = jnp.where(tail_ok, jnp.exp2(last - both), 0.0)
        d_tail = tail * from_next[:, lanes]
        terms[0:BLK, lanes] = act * d_tail
        tails[:, lanes] = act * step_both * tail
        carry = dy * jnp.where(carried, jnp.exp2(both), 0.0)
        carries[:, lanes] = carry
        terms[BLK : 2 * BLK, lanes] = carry * from_state[:, lanes]
        keeps[0:1, lanes] = jnp.where(keep_ok, jnp.exp2(last), 0.0)
        d_act = step_both * (d_intra + d_tail) + par_ref[5:6, lanes] * dy
        d_conv = d_act * (sig * (1.0 + raw * (1.0 - sig)))
        dxs[0:BLK, lanes] = d_conv
        for shift in range(CONV):
            add_rows(gx_ref, 8 * (CONV - 1 - shift), lanes, d_conv * shifted[shift])
        add_rows(gx_ref, 8 * CONV, lanes, d_conv)
        add_rows(gx_ref, 8 * (CONV + 1), lanes, dy * act)
        d_in = par_ref[CONV - 1 : CONV, lanes] * d_conv
        for shift in range(1, CONV):
            d_in = d_in + par_ref[CONV - 1 - shift : CONV - shift, lanes] * (
                after[shift - 1] * dxs[shift : shift + BLK, lanes]
            )
        drest_ref[:, lanes] = d_in.astype(BF16)

    stay = keeps[0:1, :] * jnp.sum((old * dstate[...]).reshape(NS // 8, 8, width), axis=0)
    terms[2 * BLK : 2 * BLK + 8, :] = stay
    by_head = dot(terms[...].astype(BF16), pick_ref[...])
    at_heads = by_head[0:BLK, :]
    stay_heads = jnp.sum(by_head[2 * BLK : 2 * BLK + 8, :], axis=0, keepdims=True)
    direct = direct + at_heads
    d_cum = rows_in[...].T + by_head[BLK : 2 * BLK, :] - steps * direct
    at_last = jnp.sum(steps * at_heads, axis=0, keepdims=True) + stay_heads
    through = summed(upper, d_cum) + at_last
    decay_rate = hp_ref[2:3, :]
    d_steps = direct + decay_rate * through
    d_raw = d_steps * sigmoid(raw_steps)
    every = slice(0, LANES)
    add_rows(gh_ref, 0, every, decay_rate * steps * through)
    add_rows(gh_ref, 8, every, d_raw)
    dside_ref[:, 2 * NS :] = pltpu.roll(d_raw, place_ref[0], 1)
    drest_ref[:, first_step : first_step + LANES] = d_raw.astype(BF16)
    drest_ref[:, first_step + LANES :] = jnp.zeros(
        (BLK, drest_ref.shape[1] - first_step - LANES), BF16
    )
    d_b = careful(d_scores, c_act) + product(tails[...], dstate[...], NT)
    d_c = careful(d_scores.T, b_act) + product(carries[...], old, NT)
    for part, value in ((0, d_b), (1, d_c)):
        lanes = slice(part * NS, (part + 1) * NS)
        d_conv = value * slopes[part]
        dbs[0:BLK, lanes] = d_conv
        for shift in range(CONV):
            add_rows(gbc_ref, 8 * (CONV - 1 - shift), lanes, d_conv * bc_taps[part][shift])
        add_rows(gbc_ref, 8 * CONV, lanes, d_conv)
        d_in = bcpar_ref[CONV - 1 : CONV, lanes] * d_conv
        for shift in range(1, CONV):
            d_in = d_in + bcpar_ref[CONV - 1 - shift : CONV - shift, lanes] * (
                after[shift - 1] * dbs[shift : shift + BLK, lanes]
            )
        dside_ref[:, lanes] = d_in
        drest_ref[:, width + part * NS : width + (part + 1) * NS] = d_in.astype(BF16)
    dstate[...] = keeps[0:1, :] * dstate[...] + product(c_act.T, carries[...])


def ssd_forward(rest, starts, par, bcpar, hp, sequences):
    rows, width = rest.shape[0], par.shape[1]
    blocks = rows // sequences // BLK
    here = lambda s, b: (s * blocks + b, 0)
    before = lambda s, b: (jnp.maximum((s * blocks + b) * (BLK // 8) - 1, 0), 0)
    fixed = lambda s, b: (0, 0)
    return pl.pallas_call(
        ssd_forward_kernel,
        grid=(sequences, blocks),
        in_specs=[
            pl.BlockSpec((BLK, rest.shape[1]), here),
            pl.BlockSpec((8, rest.shape[1]), before),
            pl.BlockSpec((BLK, LANES), here),
            pl.BlockSpec(par.shape, fixed),
            pl.BlockSpec(bcpar.shape, fixed),
            pl.BlockSpec(hp.shape, fixed),
        ],
        out_specs=[
            pl.BlockSpec((BLK, width), here),
            pl.BlockSpec((1, NS, width), lambda s, b: (s * blocks + b, 0, 0)),
        ],
        out_shape=[
            jax.ShapeDtypeStruct((rows, width), F32),
            jax.ShapeDtypeStruct((sequences * blocks, NS, width), F32),
        ],
        scratch_shapes=[
            pltpu.VMEM((BLK + 8, width), F32),
            pltpu.VMEM((BLK + 8, 2 * NS), F32),
            pltpu.VMEM((NS, width), F32),
            pltpu.VMEM((BLK, width), F32),
            pltpu.VMEM((8, width), F32),
        ],
        compiler_params=pltpu.CompilerParams(vmem_limit_bytes=VMEM_LIMIT),
        cost_estimate=pl.CostEstimate(
            flops=40 * rows * BLK * width, bytes_accessed=20 * rows * width, transcendentals=0
        ),
        name="ssd_forward",
    )(rest, rest, starts, par, bcpar, hp)


def ssd_backward(
    sequence, before_it, place, rest, d_ssd, states, starts, ends, start_row, par, bcpar, hp, pick, sequences
):
    rows, width = d_ssd.shape
    rest_width = rest.shape[1]
    blocks = rows // sequences // BLK
    at = lambda b: sequence * blocks + blocks - 1 - b
    here = lambda b: (at(b), 0)
    before = lambda b: (jnp.maximum(at(b) * (BLK // 8) - 1, 0), 0)
    fixed = lambda b: (0, 0)
    return pl.pallas_call(
        ssd_backward_kernel,
        grid=(blocks,),
        in_specs=[pl.BlockSpec(memory_space=pl.ANY)] * len(before_it)
        + [
            pl.BlockSpec(memory_space=pltpu.SMEM),
            pl.BlockSpec((BLK, rest_width), here),
            pl.BlockSpec((8, rest_width), before),
            pl.BlockSpec((BLK, width), here),
            pl.BlockSpec((1, NS, width), lambda b: (at(b), 0, 0)),
            pl.BlockSpec((BLK, LANES), here),
            pl.BlockSpec((BLK, LANES), here),
            pl.BlockSpec((1, BLK), lambda b: (0, at(b))),
            pl.BlockSpec(par.shape, fixed),
            pl.BlockSpec(bcpar.shape, fixed),
            pl.BlockSpec(hp.shape, fixed),
            pl.BlockSpec(pick.shape, fixed),
        ],
        out_specs=[
            pl.BlockSpec((BLK, rest_width), here),
            pl.BlockSpec((BLK, 2 * NS + LANES), lambda b: (blocks - 1 - b, 0)),
            pl.BlockSpec((8 * (CONV + 2), width), fixed),
            pl.BlockSpec((8 * (CONV + 1), 2 * NS), fixed),
            pl.BlockSpec((16, LANES), fixed),
        ],
        out_shape=[
            jax.ShapeDtypeStruct((rows, rest_width), BF16),
            jax.ShapeDtypeStruct((rows // sequences, 2 * NS + LANES), F32),
            jax.ShapeDtypeStruct((8 * (CONV + 2), width), F32),
            jax.ShapeDtypeStruct((8 * (CONV + 1), 2 * NS), F32),
            jax.ShapeDtypeStruct((16, LANES), F32),
        ],
        scratch_shapes=[
            pltpu.VMEM((BLK + 8, width), F32),
            pltpu.VMEM((BLK + 8, 2 * NS), F32),
            pltpu.VMEM((BLK + 8, width), F32),
            pltpu.VMEM((BLK + 8, 2 * NS), F32),
            pltpu.VMEM((NS, width), F32),
            pltpu.VMEM((BLK, width), F32),
            pltpu.VMEM((BLK, width), F32),
            pltpu.VMEM((2 * BLK + 8, width), F32),
            pltpu.VMEM((LANES, BLK), F32),
            pltpu.VMEM((8, width), F32),
        ],
        input_output_aliases={i: i for i in range(len(before_it))},
        compiler_params=pltpu.CompilerParams(vmem_limit_bytes=VMEM_LIMIT),
        cost_estimate=pl.CostEstimate(
            flops=100 * rows * BLK * width // sequences,
            bytes_accessed=4 * rows * 5 * width // sequences,
            transcendentals=0,
        ),
        name="ssd_backward",
    )(*before_it, place, rest, rest, d_ssd, states, starts, ends, start_row, par, bcpar, hp, pick)


def resident(array):
    return pl.BlockSpec(
        array.shape, lambda *i: (0,) * array.ndim, pipeline_mode=pl.Buffered(buffer_count=1)
    )


def matmul_kernel(left_ref, right_ref, out_ref):
    out_ref[...] = dot(left_ref[...], right_ref[...])


def project(normed, weights):
    rows = normed.shape[0]
    step = min(MID_ROWS, rows)
    width = weights.shape[1]
    here = lambda i: (i, 0)
    return pl.pallas_call(
        matmul_kernel,
        grid=(rows // step,),
        in_specs=[pl.BlockSpec((step, D), here), resident(weights)],
        out_specs=pl.BlockSpec((step, width), here),
        out_shape=jax.ShapeDtypeStruct((rows, width), F32),
        compiler_params=pltpu.CompilerParams(vmem_limit_bytes=VMEM_LIMIT),
        cost_estimate=pl.CostEstimate(
            flops=2 * rows * D * width,
            bytes_accessed=4 * rows * width + 2 * D * (rows + width),
            transcendentals=0,
        ),
        name="project",
    )(normed, weights)


def gate_kernel(normed_ref, cot_ref, wgate_ref, wout_ref, ssd_ref, gain_ref, gate_ref, dh_ref, sums_ref):
    rows, width = ssd_ref.shape
    part = min(PART_ROWS, rows)
    for first in range(0, rows, LANES):
        if first % part == 0:
            now = slice(first, first + part)
            gate_ref[now, :] = dot(normed_ref[now, :], wgate_ref[...])
            dh_ref[now, :] = dot(cot_ref[now, :], wout_ref[...], NT)
        at = slice(first, first + LANES)
        squares = jnp.zeros((LANES, LANES), F32)
        inners = jnp.zeros((LANES, LANES), F32)
        for piece in range(width // LANES):
            lanes = slice(piece * LANES, (piece + 1) * LANES)
            gate = gate_ref[at, lanes]
            gated = ssd_ref[at, lanes] * (gate * sigmoid(gate))
            squares = squares + gated * gated
            inners = inners + dh_ref[at, lanes] * gain_ref[0:1, lanes] * gated
        sums_ref[0:1, at] = jnp.sum(squares.T, axis=0, keepdims=True)
        sums_ref[1:2, at] = jnp.sum(inners.T, axis=0, keepdims=True)
    sums_ref[2:8, :] = jnp.zeros((6, rows), F32)


def gate_project(normed, cotangent, w_gate, w_output, ssd, gain):
    rows, width = ssd.shape
    step = min(MID_ROWS, rows)
    here = lambda i: (i, 0)
    return pl.pallas_call(
        gate_kernel,
        grid=(rows // step,),
        in_specs=[
            pl.BlockSpec((step, D), here),
            pl.BlockSpec((step, D), here),
            resident(w_gate),
            resident(w_output),
            pl.BlockSpec((step, width), here),
            pl.BlockSpec((1, width), lambda i: (0, 0)),
        ],
        out_specs=[
            pl.BlockSpec((step, width), here),
            pl.BlockSpec((step, width), here),
            pl.BlockSpec((8, step), lambda i: (0, i)),
        ],
        out_shape=[
            jax.ShapeDtypeStruct((rows, width), F32),
            jax.ShapeDtypeStruct((rows, width), F32),
            jax.ShapeDtypeStruct((8, rows), F32),
        ],
        compiler_params=pltpu.CompilerParams(vmem_limit_bytes=VMEM_LIMIT),
        cost_estimate=pl.CostEstimate(
            flops=4 * rows * D * width, bytes_accessed=16 * rows * width, transcendentals=0
        ),
        name="gate_project",
    )(normed, cotangent, w_gate, w_output, ssd, gain)


def gated_kernel(
    core_ref, ssd_ref, gate_ref, dh_ref, sums_ref, gain_ref, wout_ref,
    hidden_ref, dgate_ref, dssd_ref, gain_out, sent_ref, kept_ref,
):
    @pl.when(pl.program_id(0) == 0)
    def _():
        gain_out[...] = jnp.zeros_like(gain_out)

    width = ssd_ref.shape[1]
    rows = ssd_ref.shape[0]
    scale = lax.rsqrt(sums_ref[0:1, :] / DI + EPS)
    shift = scale * scale * scale * (sums_ref[1:2, :] / DI)
    turned = jnp.concatenate([scale] * 8 + [shift] * 8 + [jnp.zeros((LANES - 16, rows), F32)], axis=0).T
    chunk = min(64, rows)
    part = min(PART_ROWS, rows)
    sending = pl.program_id(0) < pl.num_programs(0) // 2
    for first in range(0, rows, chunk):
        at = slice(first, first + chunk)
        scales = wide(turned[at, 0:1], (chunk, LANES))
        shifts = wide(turned[at, 8:9], (chunk, LANES))
        for piece in range(width // LANES):
            lanes = slice(piece * LANES, (piece + 1) * LANES)
            gate = gate_ref[at, lanes]
            ssd = ssd_ref[at, lanes]
            d_hidden = dh_ref[at, lanes]
            gain = gain_ref[0:1, lanes]
            sig = sigmoid(gate)
            act = gate * sig
            gated = ssd * act
            unit = gated * scales
            hidden_ref[at, lanes] = (unit * gain).astype(BF16)
            gain_out[:, lanes] += jnp.sum((d_hidden * unit).reshape(chunk // 8, 8, LANES), axis=0)
            d_gated = scales * (d_hidden * gain) - gated * shifts
            dssd_ref[at, lanes] = d_gated * act
            dgate_ref[at, lanes] = (
                d_gated * ssd * (sig * (1.0 + gate * (1.0 - sig)))
            ).astype(BF16)
        done = first + chunk
        if done % part == 0:
            now = slice(done - part, done)
            mixed = dot(hidden_ref[now, :], wout_ref[...]).astype(BF16)
            sent_ref[now, :] = jnp.where(sending, mixed, sent_ref[now, :])
            kept_ref[now, :] = jnp.where(sending, kept_ref[now, :], mixed)


def gated_pass(core, ssd, gate, d_hidden, sums, gain, w_output):
    rows, width = ssd.shape
    step = min(MID_ROWS, rows // 2)
    steps = rows // step // 2

    def at(i, core):
        half = jnp.where(i < steps, 1 - core[0], core[0])
        return half * steps + i % steps

    here = lambda i, core: (at(i, core), 0)
    fixed = lambda i, core: (0, 0)
    return pl.pallas_call(
        gated_kernel,
        grid_spec=pltpu.PrefetchScalarGridSpec(
            num_scalar_prefetch=1,
            grid=(2 * steps,),
            in_specs=[
                pl.BlockSpec((step, width), here),
                pl.BlockSpec((step, width), here),
                pl.BlockSpec((step, width), here),
                pl.BlockSpec((8, step), lambda i, core: (0, at(i, core))),
                pl.BlockSpec((1, width), fixed),
                resident(w_output),
            ],
            out_specs=[
                pl.BlockSpec((step, width), here),
                pl.BlockSpec((step, width), here),
                pl.BlockSpec((step, width), here),
                pl.BlockSpec((8, width), fixed),
                pl.BlockSpec((step, D), lambda i, core: (jnp.minimum(i, steps - 1), 0)),
                pl.BlockSpec((step, D), lambda i, core: (jnp.maximum(i - steps, 0), 0)),
            ],
        ),
        out_shape=[
            jax.ShapeDtypeStruct((rows, width), BF16),
            jax.ShapeDtypeStruct((rows, width), BF16),
            jax.ShapeDtypeStruct((rows, width), F32),
            jax.ShapeDtypeStruct((8, width), F32),
            jax.ShapeDtypeStruct((rows // 2, D), BF16),
            jax.ShapeDtypeStruct((rows // 2, D), BF16),
        ],
        compiler_params=pltpu.CompilerParams(vmem_limit_bytes=VMEM_LIMIT),
        cost_estimate=pl.CostEstimate(
            flops=2 * rows * width * D, bytes_accessed=20 * rows * width, transcendentals=0
        ),
        name="gated_pass",
    )(core, ssd, gate, d_hidden, sums, gain, w_output)


def unit_rows(tokens):
    rows = tokens.astype(F32)
    inverse = lax.rsqrt(jnp.mean(rows * rows, axis=1, keepdims=True) + EPS)
    return rows, inverse


def normed_grad_kernel(half_ref, dgate_ref, drest_ref, tokens_ref, wgate_ref, wrest_ref, out_ref, gain_out):
    @pl.when(pl.program_id(0) == 0)
    def _():
        gain_out[...] = jnp.zeros_like(gain_out)

    rows = tokens_ref.shape[0]
    part = min(PART_ROWS, rows)
    for first in range(0, rows, part):
        now = slice(first, first + part)
        total = dot(dgate_ref[now, :], wgate_ref[...], NT) + dot(drest_ref[now, :], wrest_ref[...], NT)
        out_ref[now, :] = total.astype(BF16)
        values, inverse = unit_rows(tokens_ref[now, :])
        weighted = total * (values * inverse)
        gain_out[...] += jnp.sum(weighted.reshape(-1, 8, D), axis=0)


def normed_grad(half, weight, d_gate, d_rest, tokens, w_gate, w_rest):
    rows = tokens.shape[0]
    step = min(MID_ROWS, rows // 2)
    steps = rows // step // 2
    here = lambda i, half: (half[0] * steps + i, 0)
    return pl.pallas_call(
        normed_grad_kernel,
        grid_spec=pltpu.PrefetchScalarGridSpec(
            num_scalar_prefetch=1,
            grid=(steps,),
            in_specs=[
                pl.BlockSpec((step, d_gate.shape[1]), here),
                pl.BlockSpec((step, d_rest.shape[1]), here),
                pl.BlockSpec((step, D), here),
                resident(w_gate),
                resident(w_rest),
            ],
            out_specs=[
                pl.BlockSpec((step, D), lambda i, half: (i, 0)),
                pl.BlockSpec((8, D), lambda i, half: (0, 0)),
            ],
        ),
        out_shape=[
            jax.ShapeDtypeStruct((rows // 2, D), BF16),
            jax.ShapeDtypeStruct((8, D), F32),
        ],
        compiler_params=pltpu.CompilerParams(vmem_limit_bytes=VMEM_LIMIT),
        cost_estimate=pl.CostEstimate(
            flops=weight * rows * D * (d_gate.shape[1] + d_rest.shape[1]),
            bytes_accessed=weight * 6 * rows * D,
            transcendentals=0,
        ),
        name="normed_grad",
    )(half, d_gate, d_rest, tokens, w_gate, w_rest)


def input_grad_kernel(core_ref, own_ref, other_ref, tokens_ref, cot_ref, gain_ref, out_ref, terms):
    steps = pl.num_programs(0) // 2
    mine = pl.program_id(0) // steps == core_ref[0]

    @pl.when(mine)
    def _():
        terms[...] = own_ref[...].astype(F32)

    @pl.when(jnp.logical_not(mine))
    def _():
        terms[...] = other_ref[...].astype(F32)

    rows, inverse = unit_rows(tokens_ref[...])
    weighted = terms[...] * gain_ref[0:1, :]
    inner = jnp.mean(weighted * rows, axis=1, keepdims=True)
    out_ref[...] = (
        cot_ref[...].astype(F32) + inverse * weighted - rows * (inverse * inverse * inverse * inner)
    )


def input_grads(core, own, other, tokens, cotangent, gain):
    rows = tokens.shape[0]
    step = min(MID_ROWS, rows // 2)
    steps = rows // step // 2
    here = lambda i, core: (i, 0)

    def part_at(is_own):
        def index(i, core):
            wanted = (i // steps == core[0]) == is_own
            parked = jnp.where((core[0] == 0) == is_own, steps - 1, 0)
            return (jnp.where(wanted, i % steps, parked), 0)

        return index

    return pl.pallas_call(
        input_grad_kernel,
        grid_spec=pltpu.PrefetchScalarGridSpec(
            num_scalar_prefetch=1,
            grid=(2 * steps,),
            in_specs=[
                pl.BlockSpec((step, D), part_at(True)),
                pl.BlockSpec((step, D), part_at(False)),
                pl.BlockSpec((step, D), here),
                pl.BlockSpec((step, D), here),
                pl.BlockSpec((1, D), lambda i, core: (0, 0)),
            ],
            out_specs=pl.BlockSpec((step, D), here),
            scratch_shapes=[pltpu.VMEM((step, D), F32)],
        ),
        out_shape=jax.ShapeDtypeStruct((rows, D), F32),
        compiler_params=pltpu.CompilerParams(vmem_limit_bytes=VMEM_LIMIT),
        cost_estimate=pl.CostEstimate(
            flops=0, bytes_accessed=10 * rows * D, transcendentals=0
        ),
        name="input_grads",
    )(core, own, other, tokens, cotangent, gain)


def held_rows(first):
    return (pl.ds(pl.multiple_of(first, COPY_ROWS), TILE), slice(None))


def band_tiles(ref):
    columns = ref.shape[1] // TILE
    for tile in range(columns * (ref.shape[0] // TILE)):
        down, across = tile // columns, tile % columns
        yield tile, (
            slice(down * TILE, (down + 1) * TILE),
            slice(across * TILE, (across + 1) * TILE),
        )


def copied(first, helds, ref, at):
    past = 0
    for held_ref in helds:
        size = held_ref.shape[0]
        if len(helds) == 1:
            ref[at] = held_ref[held_rows(first)]
        else:

            @pl.when((first >= past) & (first < past + size))
            def _(held_ref=held_ref, past=past):
                ref[at] = held_ref[held_rows(first - past)]

        past += size


def assemble_kernel(parts, width, rows_ref, *refs):
    helds = refs[:parts]
    band = pl.program_id(0)
    outs = refs[parts:]
    if width:
        outs[1][:, width:] = outs[0][...]
        outs = (outs[1].at[:, 0:width],)
    base = 0
    for ref in outs:
        count = (ref.shape[0] // TILE) * (ref.shape[1] // TILE)
        for tile, at in band_tiles(ref):
            copied(rows_ref[base + band * count + tile], helds, ref, at)
        base += count * pl.num_programs(0)


def assemble(rows, helds, side_cols, shapes):
    bands = min(shape[0] for shape in shapes) // TILE
    bands = min(bands, 8)
    here = lambda i: (i, 0)
    width = shapes[0][1] - side_cols[0].shape[1] if side_cols else 0
    return pl.pallas_call(
        functools.partial(assemble_kernel, len(helds), width),
        grid=(bands,),
        in_specs=[pl.BlockSpec(memory_space=pltpu.SMEM)]
        + [resident(held) for held in helds]
        + [pl.BlockSpec((side.shape[0] // bands, side.shape[1]), here) for side in side_cols],
        out_specs=[pl.BlockSpec((shape[0] // bands, shape[1]), here) for shape in shapes],
        out_shape=[jax.ShapeDtypeStruct(shape, BF16) for shape in shapes],
        compiler_params=pltpu.CompilerParams(vmem_limit_bytes=VMEM_LIMIT),
        cost_estimate=pl.CostEstimate(
            flops=0, bytes_accessed=4 * sum(held.size for held in helds), transcendentals=0
        ),
        name="assemble",
    )(rows, *helds, *side_cols)


def spread_kernel(rows_ref, *refs):
    out_ref = refs[-1]
    band = pl.program_id(0)
    base = 0
    for ref in refs[:-1]:
        count = (ref.shape[0] // TILE) * (ref.shape[1] // TILE)
        for tile, place in band_tiles(ref):
            first = rows_ref[base + band * count + tile]

            @pl.when(first >= 0)
            def _(first=first, place=place, ref=ref):
                out_ref[held_rows(first)] = ref[place]

        base += count * pl.num_programs(0)


def spread(grad_rows, grads, total_rows):
    bands = min(grad.shape[0] for grad in grads) // TILE
    return pl.pallas_call(
        spread_kernel,
        grid=(bands,),
        in_specs=[pl.BlockSpec(memory_space=pltpu.SMEM)]
        + [pl.BlockSpec((grad.shape[0] // bands, grad.shape[1]), lambda i: (i, 0)) for grad in grads],
        out_specs=pl.BlockSpec((total_rows, TILE), lambda i: (0, 0)),
        out_shape=jax.ShapeDtypeStruct((total_rows, TILE), BF16),
        compiler_params=pltpu.CompilerParams(vmem_limit_bytes=VMEM_LIMIT),
        cost_estimate=pl.CostEstimate(
            flops=0,
            bytes_accessed=2 * total_rows * TILE + sum(2 * grad.size for grad in grads),
            transcendentals=0,
        ),
        name="spread",
    )(grad_rows, *grads)


def update_kernel(
    rows_ref, early_ref, late_ref, repair_ref, tiles_ref, lstat_ref, rstat_ref, lroot_ref, rroot_ref,
    grads_out, left_out, right_out, tiles_out, copy_out, grad_tile,
):
    dot = functools.partial(lax.dot_general, dimension_numbers=NN, preferred_element_type=F32)
    step = tiles_ref.shape[0]
    for tile in range(step):
        first = rows_ref[pl.program_id(0) * step + tile]
        past = 0
        for source in (early_ref, late_ref, repair_ref):
            size = source.shape[0]

            @pl.when((first >= past) & (first < past + size))
            def _(source=source, past=past, tile=tile):
                grad_tile[tile] = source[held_rows(first - past)]

            past += size
    for tile in range(step):
        exact_grad = grad_tile[tile]
        grad = exact_grad.astype(BF16)
        turned = exact_grad.T.astype(BF16)
        grads_out[tile] = exact_grad
        left_out[tile] = STAT_DECAY * lstat_ref[tile] + (1.0 - STAT_DECAY) * dot(grad, turned)
        right_out[tile] = STAT_DECAY * rstat_ref[tile] + (1.0 - STAT_DECAY) * dot(turned, grad)
        shaped = careful(careful(lroot_ref[tile], exact_grad), rroot_ref[tile])
        updated = tiles_ref[tile] - LR_MAT * shaped
        tiles_out[tile] = updated
        copy_out[tile] = updated.astype(BF16)


def update_tiles(rows, early, late, repair, tiles, left_stats, right_stats, left_roots, right_roots):
    count = tiles.shape[0]
    step = TILES_STEP if count % TILES_STEP == 0 else 1
    spec = pl.BlockSpec((step, TILE, TILE), lambda i, rows: (i, 0, 0))
    sources = [pl.BlockSpec(part.shape, lambda i, rows: (0, 0)) for part in (early, late, repair)]
    whole = jax.ShapeDtypeStruct(tiles.shape, F32)
    return pl.pallas_call(
        update_kernel,
        grid_spec=pltpu.PrefetchScalarGridSpec(
            num_scalar_prefetch=1,
            grid=(count // step,),
            in_specs=sources + [spec] * 5,
            out_specs=[spec] * 5,
            scratch_shapes=[pltpu.VMEM((step, TILE, TILE), F32)],
        ),
        out_shape=[whole] * 4 + [jax.ShapeDtypeStruct(tiles.shape, BF16)],
        compiler_params=pltpu.CompilerParams(vmem_limit_bytes=VMEM_LIMIT),
        cost_estimate=pl.CostEstimate(
            flops=18 * count * TILE**3, bytes_accessed=42 * count * TILE**2, transcendentals=0
        ),
        name="update_tiles",
    )(rows, early, late, repair, tiles, left_stats, right_stats, left_roots, right_roots)


def fetch_plan(slot_map, own_tiles, side_rows):
    count = slot_map.shape[0]
    tiles = jnp.arange(count, dtype=jnp.int32)
    waits = tiles // (count // 3) != 1
    key = tiles + waits * count
    owner = slot_map // own_tiles
    together = owner[:, None] == owner[None, :]
    place = jnp.sum(together & (key[None, :] < key[:, None]), axis=1, dtype=jnp.int32)
    first = max(1, own_tiles * 13 // 24)
    first_rows, second_rows = first * TILE + side_rows, (own_tiles - first) * TILE
    early = place < first
    owners = count // own_tiles
    rows = jnp.where(
        early,
        owner * first_rows + place * TILE,
        owners * first_rows + owner * second_rows + (place - first) * TILE,
    )
    rank = lax.axis_index("dp")
    places = jnp.arange(own_tiles, dtype=jnp.int32)
    order = jnp.sum(
        jnp.where(
            (owner == rank)[None, :] & (place[None, :] == places[:, None]),
            slot_map[None, :] - rank * own_tiles,
            0,
        ),
        axis=1,
        dtype=jnp.int32,
    )
    return rows, order, first, jnp.any(~waits & ~early)


def tile_plan(slot_map, own_tiles):
    count = slot_map.shape[0]
    tiles = jnp.arange(count, dtype=jnp.int32)
    kind = tiles // (count // 3)
    waits = kind == 1
    key = tiles + waits * count
    owner = slot_map // own_tiles
    together = owner[:, None] == owner[None, :]
    first = own_tiles // 2
    last = min(own_tiles, own_tiles - first + SLACK)
    place = jnp.sum(together & (key[None, :] < key[:, None]), axis=1, dtype=jnp.int32)
    early = (place < first) & ~waits
    behind = jnp.sum(
        together & ~early[None, :] & (key[None, :] < key[:, None]), axis=1, dtype=jnp.int32
    )
    late = ~early & (behind < last)
    repair = ~early & ~late

    def rows_where(chosen, position, rows):
        return jnp.where(chosen, owner * rows + position * TILE, -1)

    early_rows, late_rows = first * TILE, last * TILE
    plans = (
        (rows_where(early, place, early_rows), early_rows),
        (rows_where(late, behind, late_rows), late_rows),
        (rows_where(repair, behind - last, early_rows), early_rows),
    )
    in_owner = jnp.where(early, place, first + behind) * TILE
    rank = lax.axis_index("dp")
    slots = rank * own_tiles + jnp.arange(own_tiles, dtype=jnp.int32)
    own_rows = jnp.sum(
        jnp.where(slot_map[None, :] == slots[:, None], in_owner[None, :], 0), axis=1, dtype=jnp.int32
    )
    return plans, own_rows, jnp.any(repair).astype(F32)


def on_device(
    tokens,
    cotangent,
    doc_ids,
    tile_slots,
    matrix_tiles,
    left_stats,
    right_stats,
    left_roots,
    right_roots,
    side_weight,
    side_moment,
    side_second,
    vector_params,
    vector_moment,
    vector_second,
):
    n_tensor = lax.axis_size("tensor")
    n_dp = lax.axis_size("dp")
    tensor_rank = lax.axis_index("tensor")
    core = tensor_rank % 2
    di_local = DI // n_tensor
    heads_local = HEADS // n_tensor
    model_local = D // n_tensor
    bc_local = 2 * NS // n_tensor
    rows = tokens.shape[0]
    half = rows // 2
    sequences, seq_len = doc_ids.shape
    slot_map = tile_slots[0]
    own_tiles = matrix_tiles.shape[1]
    side_rows = side_weight.shape[0] * SIDE // TILE
    fetch_rows, order, first_tiles, misfetch = fetch_plan(
        slot_map, own_tiles, side_rows
    )
    plans, own_rows, misfit = tile_plan(slot_map, own_tiles)
    misfits = sum_over(jnp.full((8, LANES), misfit), "tensor")
    vector = vector_params[0]
    bounds = segment_bounds(di_local, heads_local, model_local, bc_local, CONV)

    def segment_of(index):
        return vector[bounds[index] : bounds[index + 1]]

    conv_kernel = segment_of(0).reshape(CONV, di_local)
    conv_offset = segment_of(1)
    gate_gain = segment_of(2)
    log_rate = segment_of(3)
    skip_gain = segment_of(4)
    dt_offset = segment_of(5)

    mine = matrix_tiles[0].astype(BF16)[order].reshape(own_tiles * TILE, TILE)
    cut = first_tiles * TILE
    first_share = jnp.concatenate(
        [mine[:cut], side_weight.astype(BF16).reshape(side_rows, TILE)], axis=0
    )
    first_held = lax.all_gather(first_share, "dp", axis=0, tiled=True)
    second_held = lax.all_gather(mine[cut:], "dp", axis=0, tiled=True)
    shared = lax.all_gather(vector[bounds[6] :][None, :], "tensor", axis=0, tiled=True)
    pre_gain = shared[:, :model_local].reshape(D)
    bc_kernel = (
        shared[:, model_local : model_local + CONV * bc_local]
        .reshape(n_tensor, CONV, bc_local)
        .transpose(1, 0, 2)
        .reshape(CONV, 2 * NS)
    )
    bc_offset = shared[:, model_local + CONV * bc_local :].reshape(2 * NS)
    par = jnp.concatenate(
        [
            conv_kernel,
            conv_offset[None],
            jnp.repeat(skip_gain, di_local // heads_local)[None],
            gate_gain[None],
            jnp.zeros((1, di_local), F32),
        ],
        axis=0,
    )
    bcpar = jnp.concatenate([bc_kernel, bc_offset[None], jnp.zeros((3, 2 * NS), F32)], axis=0)
    decay_rate = -jnp.exp(log_rate)
    hp = jnp.pad(
        jnp.stack([dt_offset, decay_rate * LOG2E, decay_rate]), ((0, 5), (0, LANES - heads_local))
    )
    pick = (
        jnp.arange(di_local)[:, None] // (di_local // heads_local) == jnp.arange(LANES)[None, :]
    ).astype(BF16)
    starts = jnp.sum(doc_ids[:, None, :] < doc_ids[:, :, None], axis=2).astype(F32).reshape(rows)
    ends = jnp.sum(doc_ids[:, None, :] <= doc_ids[:, :, None], axis=2).astype(F32).reshape(rows)
    start_row = starts[None, :]
    start_wide = jnp.broadcast_to(starts[:, None], (rows, LANES))
    end_wide = jnp.broadcast_to(ends[:, None], (rows, LANES))

    residual = tokens.astype(F32)
    inverse = lax.rsqrt(jnp.mean(residual * residual, axis=1, keepdims=True) + EPS)
    normed = (residual * inverse * pre_gain).astype(BF16)
    normed, misfits = tied(normed, misfits)
    misfit = misfits[0, 0] > 0.0

    side_copy = first_held.reshape(n_dp, -1, TILE)[:, cut:].reshape(D, SIDE)
    side_cols = jnp.concatenate(
        [
            side_copy[:, : 2 * NS],
            lax.dynamic_slice_in_dim(side_copy, 2 * NS + tensor_rank * heads_local, heads_local, 1),
            jnp.zeros((D, 2 * NS - heads_local), BF16),
        ],
        axis=1,
    )
    per_block = (D // TILE) * (di_local // TILE)
    rest_shape = ((D, di_local + side_cols.shape[1]),)

    rest_rows = fetch_rows[per_block : 2 * per_block]

    def forward_with(rows, helds):
        weights = assemble(rows, helds, (side_cols,), rest_shape)[0]
        projected = project(normed, weights)
        scanned = ssd_forward(projected, start_wide, par, bcpar, hp, sequences)
        return (weights, projected, *scanned)

    tried = forward_with(
        jnp.minimum(rest_rows, first_held.shape[0] - TILE), (first_held,)
    )
    tried, second_held = tied(tried, second_held)
    w_rest, rest, ssd, states = lax.while_loop(
        lambda carry: carry[0],
        lambda carry: (False, forward_with(rest_rows, (first_held, second_held))),
        (misfetch, tried),
    )[1]
    w_gate, w_output = assemble(
        jnp.concatenate([fetch_rows[:per_block], fetch_rows[2 * per_block :]]),
        (first_held, second_held),
        (),
        ((D, di_local), (di_local, D)),
    )
    gate, d_hidden, sums = gate_project(
        normed, cotangent, w_gate, w_output, ssd, gate_gain[None, :]
    )
    sums = sum_over(sums, "tensor")
    core_at = core[None].astype(jnp.int32)
    hidden, d_gate, d_ssd, gain_sums, out_sent, out_kept = gated_pass(
        core_at, ssd, gate, d_hidden, sums, gate_gain[None, :], w_output
    )

    def chip_sum(kept, sent):
        return (kept.astype(F32) + swap(sent, "tensor", 1).astype(F32)).astype(BF16)

    out_chip = chip_sum(out_kept, out_sent)
    grad_output = contract_rows(hidden, cotangent).astype(BF16)
    out_chip, normed_now = tied(out_chip, normed)
    out_others = [swap(part, "tensor", 2) for part in jnp.split(out_chip, 2)]
    grad_gate = contract_rows(normed_now, d_gate).astype(BF16)
    early_grads = spread(
        jnp.concatenate([plans[0][0][:per_block], plans[0][0][2 * per_block :]]),
        (grad_gate, grad_output),
        n_dp * plans[0][1],
    )
    d_ssd, early_grads = tied(d_ssd, early_grads)
    early = OwnerSum(early_grads, ((0, 1), (2, 3)))
    given = (states, start_wide, end_wide, start_row, par, bcpar, hp, pick, sequences)
    place = (tensor_rank * heads_local).astype(jnp.int32)[None]
    back, parts, side_parts = (), [], []
    for sequence in range(sequences):
        d_rest, d_side, *sums_here = ssd_backward(sequence, back, place, rest, d_ssd, *given)
        parts.append(sums_here)
        if sequence == 0:
            d_rest, out_others[0] = early.first((d_rest, out_others[0]))
        else:
            d_rest, side_parts[-1] = tied(d_rest, side_parts[-1])
        side_parts.append((d_side, swap(d_side, "tensor", 1)))
        back = (d_rest,)
    gx, gbc, gh = (sum(terms) for terms in zip(*parts))
    d_rest, out_others[1] = early.second((back[0], out_others[1]))

    split_side = sequences // 2
    side_chips = [
        jnp.concatenate([(own + other).astype(BF16) for own, other in part], axis=0)
        for part in (side_parts[:split_side], side_parts[split_side:])
    ]
    d_rest, side_chips[0] = tied(d_rest, side_chips[0])
    side_others = [swap(side_chips[0], "tensor", 2)]
    d_sent, pre_sent = normed_grad(1 - core_at, 16, d_gate, d_rest, tokens, w_gate, w_rest)
    d_sent, side_chips[1], side_others[0], d_rest = early.third(
        (d_sent, side_chips[1], side_others[0], d_rest)
    )
    side_others.append(swap(side_chips[1], "tensor", 2))
    grad_input = contract_rows(normed, d_rest[:, :di_local]).astype(BF16)
    late_grads = spread(plans[1][0], (grad_gate, grad_input, grad_output), n_dp * plans[1][1])
    early_share, (late_grads, side_others[1], d_rest) = early.total(
        (late_grads, side_others[1], d_rest)
    )
    late = OwnerSum(late_grads, ((0,), (1,), (2,), (3,)))
    d_kept, pre_kept = normed_grad(core_at, 16, d_gate, d_rest, tokens, w_gate, w_rest)
    d_kept, pre_kept = late.first((d_kept, pre_kept))
    grad_pre = jnp.sum(pre_sent + pre_kept, axis=0)
    d_chip = chip_sum(d_kept, d_sent)
    d_others = [swap(part, "tensor", 2) for part in jnp.split(d_chip, 4)]
    d_others[0], side_chips, side_others, out_chip, out_others = late.second(
        (d_others[0], side_chips, side_others, out_chip, out_others)
    )

    side_total = jnp.concatenate(
        [
            (own.astype(F32) + other.astype(F32)).astype(BF16)
            for own, other in zip(side_chips, side_others)
        ],
        axis=0,
    )
    grad_side = lax.dynamic_index_in_dim(
        contract_rows(normed, side_total).reshape(n_dp, n_tensor, -1, side_total.shape[1]),
        tensor_rank,
        1,
        keepdims=False,
    )[:, :, :SIDE]
    gx_sums = jnp.sum(gx.reshape(CONV + 2, 8, di_local), axis=1)
    gbc_sums = jnp.sum(gbc.reshape(CONV + 1, 8, 2 * NS), axis=1)
    gh_sums = jnp.sum(gh.reshape(2, 8, LANES), axis=1)[:, :heads_local]
    own_vector = jnp.concatenate(
        [
            gx_sums[: CONV + 1].reshape(-1),
            jnp.sum(gain_sums, axis=0),
            gh_sums[0],
            jnp.sum(gx_sums[CONV + 1].reshape(heads_local, -1), axis=1),
            gh_sums[1],
        ]
    )
    small_sums = SharedSums(
        grad_side.reshape(n_dp, -1), jnp.concatenate([own_vector, grad_pre, gbc_sums.reshape(-1)])
    )
    arrived, d_others[1] = late.third((small_sums.send(), d_others[1]))
    small_sums.add(arrived)
    late_share, (arrived, d_others[2], misfit) = late.total(
        (small_sums.send(), d_others[2], misfit)
    )
    small_sums.add(arrived)
    small_sums.finish()

    def repaired(grads):
        again = spread(plans[2][0], grads, n_dp * plans[2][1])
        return lax.psum_scatter(again, "dp", scatter_dimension=0, tiled=True).astype(F32)

    repair_share = lax.cond(
        misfit,
        repaired,
        lambda grads: jnp.zeros((plans[2][1], TILE), F32),
        (grad_gate, grad_input, grad_output),
    )

    tile_share, left_new, right_new, tiles_new, tiles_copy = update_tiles(
        own_rows,
        early_share,
        late_share,
        repair_share,
        matrix_tiles[0],
        left_stats[0],
        right_stats[0],
        left_roots[0],
        right_roots[0],
    )
    split_at = own_vector.shape[0]
    side_own, all_vector = small_sums.owned, small_sums.shared
    quarters = jnp.where(
        (jnp.arange(n_tensor) == tensor_rank)[:, None], side_own, jnp.zeros((), F32)
    )
    common = sum_over(
        jnp.concatenate([quarters.reshape(-1), all_vector[split_at:]])[None], "tensor"
    )[0]
    side_share = common[: side_weight.size].reshape(side_weight.shape)
    common = common[side_weight.size :]
    quarter = half // 2
    mixed_own = [
        (
            lax.dynamic_slice_in_dim(tokens, core * half + i * quarter, quarter, 0).astype(F32)
            + (out_chip[i * quarter : (i + 1) * quarter].astype(F32) + out_others[i].astype(F32))
        ).astype(BF16)
        for i in range(2)
    ]
    mixed_other = [swap(part, "tensor", 1) for part in mixed_own]
    lower_half = core == 0
    mixed = jnp.concatenate(
        [jnp.where(lower_half, own, other) for own, other in zip(mixed_own, mixed_other)]
        + [jnp.where(lower_half, other, own) for own, other in zip(mixed_own, mixed_other)],
        axis=0,
    )

    d_half = (d_chip.astype(F32) + jnp.concatenate(d_others).astype(F32)).astype(BF16)
    input_grad = input_grads(
        core_at, d_half, swap(d_half, "tensor", 1), tokens, cotangent, pre_gain[None, :]
    )

    pre_share = lax.dynamic_slice_in_dim(common[:D], tensor_rank * model_local, model_local, 0)
    bc_share = lax.dynamic_slice_in_dim(
        common[D:].reshape(CONV + 1, 2 * NS), tensor_rank * bc_local, bc_local, 1
    )
    vector_total = jnp.concatenate([all_vector[:split_at], pre_share, bc_share.reshape(-1)])[None]

    side_m, side_v, side_new = adam_update(
        side_weight, side_moment, side_second, side_share, LR_SIDE
    )
    vec_m, vec_v, vec_new = adam_update(
        vector_params, vector_moment, vector_second, vector_total, LR_VEC
    )
    return (
        mixed,
        input_grad,
        tile_share[None],
        left_new[None],
        right_new[None],
        tiles_new[None],
        tiles_copy[None],
        side_m,
        side_v,
        side_new,
        vec_m,
        vec_v,
        vec_new,
    )


def solution(mesh):
    by_dp = P("dp", None)
    by_tensor = P("tensor", None)
    by_tile = P("tensor", "dp", None, None)
    return jax.shard_map(
        on_device,
        mesh=mesh,
        in_specs=(by_dp,) * 3
        + (by_tensor,)
        + (by_tile,) * 5
        + (by_dp,) * 3
        + (by_tensor,) * 3,
        out_specs=(by_dp,) * 2 + (by_tile,) * 5 + (by_dp,) * 3 + (by_tensor,) * 3,
        check_vma=False,
    )
```

```python
import functools

import jax
import jax.numpy as jnp
from jax import lax
from jax.experimental import pallas as pl
from jax.experimental.pallas import tpu as pltpu
from jax.sharding import PartitionSpec as P

D = 2048
HEADS = 64
NS = 128
CONV = 4
TILE = 128
STEP = 10
DI = 4096
SIDE = 320
BLK = 128
LANES = 128
MID_ROWS = 512
PART_ROWS = 256
TILES_STEP = 6
COPY_ROWS = 16
SLACK = 2
ONE_PASS = True

EPS = 1e-05
HIGH = lax.Precision.HIGHEST
STAT_DECAY = 0.5
LR_MAT = 0.25
LR_SIDE = 0.02
LR_VEC = 0.25
BETA_ONE = 0.9
BETA_TWO = 0.95
ADAM_EPS = 1e-08
DECAY_WD = 0.1
LOG2E = 1.4426950408889634
FAR = -1e30
VMEM_LIMIT = 60 * 1024 * 1024

F32 = jnp.float32
BF16 = jnp.bfloat16

NN = (((1,), (0,)), ((), ()))
NT = (((1,), (1,)), ((), ()))


def segment_bounds(di_local, heads_local, model_local, bc_local, tap_count):
    widths = [
        tap_count * di_local,
        di_local,
        di_local,
        heads_local,
        heads_local,
        heads_local,
        model_local,
        tap_count * bc_local,
        bc_local,
    ]
    bounds = [0]
    for item in widths:
        bounds.append(bounds[-1] + item)
    return bounds


def adam_update(weight, moment, second, gradient, learn_rate):
    moment_new = BETA_ONE * moment + (1.0 - BETA_ONE) * gradient
    second_new = BETA_TWO * second + (1.0 - BETA_TWO) * gradient * gradient
    corrected = moment_new / (1.0 - BETA_ONE**STEP)
    scaled = jnp.sqrt(second_new / (1.0 - BETA_TWO**STEP)) + ADAM_EPS
    return (moment_new, second_new, weight - learn_rate * (corrected / scaled + DECAY_WD * weight))


def contract_rows(left, right):
    return lax.dot_general(left, right, (((0,), (0,)), ((), ())), preferred_element_type=F32)


def contract_cols(left, right):
    return lax.dot_general(left, right, NT, preferred_element_type=F32)


def swap(value, axis, bit):
    size = lax.axis_size(axis)
    return lax.ppermute(value, axis, [(i, i ^ bit) for i in range(size)])


def sum_over(value, axis):
    bit = 1
    while bit < lax.axis_size(axis):
        value = value + swap(value, axis, bit)
        bit *= 2
    return value


class SharedSums:
    def __init__(self, owned, shared):
        self.owned, self.shared = owned, shared
        self.bit = lax.axis_size("dp") // 2

    def send(self):
        upper = (lax.axis_index("dp") // self.bit) % 2
        pairs = self.owned.reshape(2, -1, self.owned.shape[1])
        sent = lax.dynamic_index_in_dim(pairs, 1 - upper, 0, keepdims=False)
        self.kept = lax.dynamic_index_in_dim(pairs, upper, 0, keepdims=False)
        return swap(jnp.concatenate([sent.reshape(-1), self.shared])[None], "dp", self.bit)

    def add(self, arrived):
        size = self.kept.size
        self.owned = self.kept + arrived[0, :size].reshape(self.kept.shape)
        self.shared = self.shared + arrived[0, size:]
        self.bit //= 2

    def finish(self):
        while self.bit > 0:
            self.add(self.send())


class OwnerSum:
    def __init__(self, grads, groups):
        owners = lax.axis_size("dp")
        self.grads = grads.reshape(owners, -1, TILE)
        self.lined = owners == 8
        if not self.lined:
            return
        me = lax.axis_index("dp")
        x, z = me % 2, me // 2
        self.low = z < 2
        order = [jnp.where(self.low, z + 3 - k, z + 1 + k) % 4 for k in range(4)]
        self.own = [self.part(seg, x) for seg in order]
        self.found = [(i, group.index(k)) for k in range(4) for i, group in enumerate(groups) if k in group]
        self.groups = [
            swap(jnp.concatenate([self.part(order[k], 1 - x) for k in group]), "dp", 1)
            for group in groups
        ]

    def part(self, seg, x):
        return lax.dynamic_index_in_dim(self.grads, seg * 2 + x, 0, keepdims=False)

    def pair_sum(self, k):
        rows = self.own[k].shape[0]
        group, place = self.found[k]
        arrived = self.groups[group][place * rows : (place + 1) * rows]
        return self.own[k].astype(F32) + arrived.astype(F32)

    def hop(self, value, moves):
        pairs = [(2 * a + x, 2 * b + x) for a, b in moves for x in (0, 1)]
        return lax.ppermute(value.astype(BF16), "dp", pairs)


    def first(self, other):
        if self.lined:
            self.groups[0], other = tied(self.groups[0], other)
            self.ahead = self.hop(self.pair_sum(0), [(0, 1), (3, 2)])
        return other

    def second(self, other):
        if self.lined:
            needed = self.found[1][0]
            self.ahead, self.groups[needed], other = tied(self.ahead, self.groups[needed], other)
            value = self.pair_sum(1) + self.ahead.astype(F32)
            self.up = self.hop(value, [(0, 1), (1, 2)])
            self.down = self.hop(value, [(3, 2), (2, 1)])
        return other

    def third(self, other):
        if self.lined:
            needed = self.found[2][0]
            self.up, self.down, self.groups[needed], other = tied(
                self.up, self.down, self.groups[needed], other
            )
            near, far = self.pair_sum(2), self.pair_sum(0)
            up = jnp.where(self.low, near, far) + self.up.astype(F32)
            down = jnp.where(self.low, far, near) + self.down.astype(F32)
            self.up = self.hop(up, [(0, 1), (1, 2), (2, 3)])
            self.down = self.hop(down, [(3, 2), (2, 1), (1, 0)])
        return other

    def total(self, other):
        if not self.lined:
            flat = self.grads.reshape(-1, TILE)
            return lax.psum_scatter(flat, "dp", scatter_dimension=0, tiled=True).astype(F32), other
        self.up, self.down, self.groups[-1], other = tied(
            self.up, self.down, self.groups[-1], other
        )
        return self.pair_sum(3) + (self.up.astype(F32) + self.down.astype(F32)), other


def tied(*values):
    return lax.optimization_barrier(values)


def halves(value):
    high = value.astype(BF16)
    return high, (value - high.astype(F32)).astype(BF16)


def dot(left, right, dims=NN):
    return lax.dot_general(left, right, dims, preferred_element_type=F32)


def product(left, right, dims=NN):
    return dot(left.astype(BF16), right.astype(BF16), dims)


def by_halves(left, right):
    both = dot(left.astype(BF16), jnp.concatenate(halves(right), axis=1))
    return both[:, : right.shape[1]] + both[:, right.shape[1] :]


def careful(left, right, dims=NN):
    left_high, left_low = halves(left)
    right_high, right_low = halves(right)
    return dot(
        jnp.concatenate([left_high, left_low, left_high], axis=1),
        jnp.concatenate([right_high, right_high, right_low], axis=dims[0][1][0]),
        dims,
    )


def summed(mask, value):
    high, rest = halves(value)
    low = (value - high.astype(F32) - rest.astype(F32)).astype(BF16)
    mask = mask.astype(BF16)
    return dot(jnp.concatenate([mask] * 3, axis=1), jnp.concatenate([high, rest, low], axis=0))


def sigmoid(value):
    return 0.5 * jnp.tanh(0.5 * value) + 0.5


def softplus(value):
    return jnp.maximum(value, 0.0) + jnp.log1p(jnp.exp(-jnp.abs(value)))


def taps_of(padded, lanes, masks):
    rows = masks[0].shape[0]
    shifted = [padded[8 : 8 + rows, lanes]]
    for shift in range(1, CONV):
        shifted.append(padded[8 - shift : 8 - shift + rows, lanes] * masks[shift - 1])
    return shifted


def convolve(shifted, params, lanes):
    total = params[CONV : CONV + 1, lanes]
    for shift in range(CONV):
        total = total + params[CONV - 1 - shift : CONV - shift, lanes] * shifted[shift]
    return total


def wide(column, shape):
    return jnp.broadcast_to(column, shape)


def ssd_forward_kernel(
    rest_ref, prev_ref, start_ref, par_ref, bcpar_ref, hp_ref,
    ssd_ref, states_ref, xs, ss, state, tails, keeps,
):
    width = ssd_ref.shape[1]
    pairs = width // LANES
    shape = (BLK, LANES)
    base_i = pl.program_id(1) * BLK
    base = base_i.astype(F32)

    @pl.when(pl.program_id(1) == 0)
    def _():
        state[...] = jnp.zeros_like(state)

    xs[0:8, :] = prev_ref[:, 0:width]
    xs[8 : 8 + BLK, :] = rest_ref[:, 0:width]
    ss[0:8, :] = prev_ref[:, width : width + 2 * NS]
    ss[8 : 8 + BLK, :] = rest_ref[:, width : width + 2 * NS]
    start = start_ref[...]
    row = (lax.broadcasted_iota(jnp.int32, shape, 0) + base_i).astype(F32)
    col = (lax.broadcasted_iota(jnp.int32, shape, 1) + base_i).astype(F32)
    lane = lax.broadcasted_iota(jnp.int32, shape, 1)
    low = lane < LANES // 2
    pos = row - start
    masks = [jnp.where(pos >= float(k), 1.0, 0.0) for k in range(1, CONV)]
    bias = jnp.where((col >= start) & (col <= row), 0.0, FAR)
    carried = start < base
    last_start = start_ref[BLK - 1 : BLK, :]
    tail_ok = row >= last_start
    keep_ok = last_start < base

    acts = []
    for part in range(2):
        lanes = slice(part * NS, (part + 1) * NS)
        raw = convolve(taps_of(ss, lanes, masks), bcpar_ref, lanes)
        acts.append(raw * sigmoid(raw))
    b_act, c_act = acts
    first_step = width + 2 * NS
    steps = softplus(rest_ref[:, first_step : first_step + LANES] + hp_ref[0:1, :])
    lower = jnp.where(col <= row, 1.0, 0.0)
    cum = summed(lower, steps * hp_ref[1:2, :])
    cum_t = cum.T
    scores = careful(c_act, b_act, NT)
    states_ref[0] = state[...]
    from_state = product(c_act, state[...])
    for pair in range(pairs):
        lanes = slice(pair * LANES, (pair + 1) * LANES)
        raw = convolve(taps_of(xs, lanes, masks), par_ref, lanes)
        act = raw * sigmoid(raw)
        col_a = wide(cum[:, 2 * pair : 2 * pair + 1], shape)
        col_b = wide(cum[:, 2 * pair + 1 : 2 * pair + 2], shape)
        both = jnp.where(low, col_a, col_b)
        step_both = jnp.where(
            low,
            wide(steps[:, 2 * pair : 2 * pair + 1], shape),
            wide(steps[:, 2 * pair + 1 : 2 * pair + 2], shape),
        )
        scaled = act * step_both
        weight_a = scores * jnp.exp2(col_a - cum_t[2 * pair : 2 * pair + 1, :] + bias)
        weight_b = scores * jnp.exp2(col_b - cum_t[2 * pair + 1 : 2 * pair + 2, :] + bias)
        inner = by_halves(
            jnp.concatenate([weight_a, weight_b], axis=1),
            jnp.concatenate([jnp.where(low, scaled, 0.0), jnp.where(low, 0.0, scaled)], axis=0),
        )
        carry = jnp.where(carried, jnp.exp2(both), 0.0)
        ssd_ref[:, lanes] = inner + carry * from_state[:, lanes] + par_ref[5:6, lanes] * act
        last = both[BLK - 1 : BLK, :]
        tails[:, lanes] = scaled * jnp.where(tail_ok, jnp.exp2(last - both), 0.0)
        keeps[0:1, lanes] = jnp.where(keep_ok, jnp.exp2(last), 0.0)
    state[...] = keeps[0:1, :] * state[...] + product(b_act.T, tails[...])


def both_halves(left_high, left_low, right_high, right_low, low, which):
    mine = low if which == 0 else jnp.logical_not(low)

    def turned(value):
        return pltpu.roll(value.astype(F32), LANES // 2, 1)

    left_high, right_high = left_high.astype(F32), right_high.astype(F32)
    left = jnp.concatenate(
        [jnp.where(mine, left_high, turned(left_low)), jnp.where(mine, left_high, 0.0)], axis=1
    )
    right = jnp.concatenate(
        [
            jnp.where(mine, right_high, turned(right_high)),
            jnp.where(mine, right_low.astype(F32), 0.0),
        ],
        axis=1,
    )
    return dot(left.astype(BF16), right.astype(BF16), NT)


def ssd_backward_kernel(
    *refs,
):
    held = max(len(refs) - 27, 0)
    ssd_backward_body(*refs[held:])


def ssd_backward_body(
    place_ref, rest_ref, prev_ref, dy_ref, states_ref, start_ref, end_ref, srow_ref,
    par_ref, bcpar_ref, hp_ref, pick_ref,
    drest_ref, dside_ref, gx_ref, gbc_ref, gh_ref,
    xs, ss, dxs, dbs, dstate, tails, carries, terms, rows_in, keeps,
):
    width = dy_ref.shape[1]
    pairs = width // LANES
    shape = (BLK, LANES)
    blocks = pl.num_programs(0)
    base_i = (blocks - 1 - pl.program_id(0)) * BLK
    base = base_i.astype(F32)

    @pl.when(pl.program_id(0) == 0)
    def _():
        gx_ref[...] = jnp.zeros_like(gx_ref)
        gbc_ref[...] = jnp.zeros_like(gbc_ref)
        gh_ref[...] = jnp.zeros_like(gh_ref)
        rows_in[...] = jnp.zeros_like(rows_in)
        dxs[0:8, :] = jnp.zeros((8, width), F32)
        dbs[0:8, :] = jnp.zeros((8, 2 * NS), F32)
        dstate[...] = jnp.zeros_like(dstate)

    dxs[BLK : BLK + 8, :] = dxs[0:8, :]
    dbs[BLK : BLK + 8, :] = dbs[0:8, :]
    xs[0:8, :] = prev_ref[:, 0:width]
    xs[8 : 8 + BLK, :] = rest_ref[:, 0:width]
    ss[0:8, :] = prev_ref[:, width : width + 2 * NS]
    ss[8 : 8 + BLK, :] = rest_ref[:, width : width + 2 * NS]
    start = start_ref[...]
    row_i = lax.broadcasted_iota(jnp.int32, shape, 0)
    lane = lax.broadcasted_iota(jnp.int32, shape, 1)
    row = (row_i + base_i).astype(F32)
    col = (lane + base_i).astype(F32)
    low = lane < LANES // 2
    pos = row - start
    left = end_ref[...] - row
    masks = [jnp.where(pos >= float(k), 1.0, 0.0) for k in range(1, CONV)]
    after = [jnp.where(left > float(k), 1.0, 0.0) for k in range(1, CONV)]
    bias_t = jnp.where((row >= srow_ref[...]) & (row <= col), 0.0, FAR)
    carried = start < base
    last_start = start_ref[BLK - 1 : BLK, :]
    tail_ok = row >= last_start
    keep_ok = last_start < base

    acts, slopes, bc_taps = [], [], []
    for part in range(2):
        lanes = slice(part * NS, (part + 1) * NS)
        shifted = taps_of(ss, lanes, masks)
        raw = convolve(shifted, bcpar_ref, lanes)
        sig = sigmoid(raw)
        acts.append(raw * sig)
        slopes.append(sig * (1.0 + raw * (1.0 - sig)))
        bc_taps.append(shifted)
    b_act, c_act = acts
    first_step = width + 2 * NS
    raw_steps = rest_ref[:, first_step : first_step + LANES] + hp_ref[0:1, :]
    steps = softplus(raw_steps)
    lower = jnp.where(col <= row, 1.0, 0.0)
    upper = jnp.where(col >= row, 1.0, 0.0)
    cum = summed(lower, steps * hp_ref[1:2, :])
    cum_t = cum.T
    scores_t = careful(b_act, c_act, NT)
    old = states_ref[0]
    from_state = product(c_act, old)
    from_next = product(b_act, dstate[...])
    d_scores = jnp.zeros(shape, F32)
    direct = jnp.zeros(shape, F32)

    def add_rows(ref, first, lanes, value):
        ref[first : first + 8, lanes] += jnp.sum(value.reshape(BLK // 8, 8, value.shape[1]), axis=0)

    for pair in range(pairs):
        lanes = slice(pair * LANES, (pair + 1) * LANES)
        shifted = taps_of(xs, lanes, masks)
        raw = convolve(shifted, par_ref, lanes)
        sig = sigmoid(raw)
        act = raw * sig
        dy = dy_ref[:, lanes]
        cols = [wide(cum[:, h : h + 1], shape) for h in (2 * pair, 2 * pair + 1)]
        step_cols = [wide(steps[:, h : h + 1], shape) for h in (2 * pair, 2 * pair + 1)]
        both = jnp.where(low, cols[0], cols[1])
        step_both = jnp.where(low, step_cols[0], step_cols[1])
        act_high, act_low = halves(act)
        dy_high, dy_low = halves(dy)
        inners = [
            both_halves(act_high, act_low, dy_high, dy_low, low, which) for which in range(2)
        ]
        weights = []
        for which in range(2):
            head = 2 * pair + which
            decay = jnp.exp2(cum_t[head : head + 1, :] - cols[which] + bias_t)
            inner = inners[which]
            weight = decay * scores_t
            weights.append(weight)
            d_scores = d_scores + decay * inner * step_cols[which]
            pulled = weight * inner
            direct = jnp.where(lane == head, jnp.sum(pulled, axis=1, keepdims=True), direct)
            rows_in[head : head + 1, :] = jnp.sum(pulled * step_cols[which], axis=0, keepdims=True)
        d_intra = by_halves(
            jnp.concatenate(weights, axis=1),
            jnp.concatenate([jnp.where(low, dy, 0.0), jnp.where(low, 0.0, dy)], axis=0),
        )
        last = both[BLK - 1 : BLK, :]
        tail = jnp.where(tail_ok, jnp.exp2(last - both), 0.0)
        d_tail = tail * from_next[:, lanes]
        terms[0:BLK, lanes] = act * d_tail
        tails[:, lanes] = act * step_both * tail
        carry = dy * jnp.where(carried, jnp.exp2(both), 0.0)
        carries[:, lanes] = carry
        terms[BLK : 2 * BLK, lanes] = carry * from_state[:, lanes]
        keeps[0:1, lanes] = jnp.where(keep_ok, jnp.exp2(last), 0.0)
        d_act = step_both * (d_intra + d_tail) + par_ref[5:6, lanes] * dy
        d_conv = d_act * (sig * (1.0 + raw * (1.0 - sig)))
        dxs[0:BLK, lanes] = d_conv
        for shift in range(CONV):
            add_rows(gx_ref, 8 * (CONV - 1 - shift), lanes, d_conv * shifted[shift])
        add_rows(gx_ref, 8 * CONV, lanes, d_conv)
        add_rows(gx_ref, 8 * (CONV + 1), lanes, dy * act)
        d_in = par_ref[CONV - 1 : CONV, lanes] * d_conv
        for shift in range(1, CONV):
            d_in = d_in + par_ref[CONV - 1 - shift : CONV - shift, lanes] * (
                after[shift - 1] * dxs[shift : shift + BLK, lanes]
            )
        drest_ref[:, lanes] = d_in.astype(BF16)

    stay = keeps[0:1, :] * jnp.sum((old * dstate[...]).reshape(NS // 8, 8, width), axis=0)
    terms[2 * BLK : 2 * BLK + 8, :] = stay
    by_head = dot(terms[...].astype(BF16), pick_ref[...])
    at_heads = by_head[0:BLK, :]
    stay_heads = jnp.sum(by_head[2 * BLK : 2 * BLK + 8, :], axis=0, keepdims=True)
    direct = direct + at_heads
    d_cum = rows_in[...].T + by_head[BLK : 2 * BLK, :] - steps * direct
    at_last = jnp.sum(steps * at_heads, axis=0, keepdims=True) + stay_heads
    through = summed(upper, d_cum) + at_last
    decay_rate = hp_ref[2:3, :]
    d_steps = direct + decay_rate * through
    d_raw = d_steps * sigmoid(raw_steps)
    every = slice(0, LANES)
    add_rows(gh_ref, 0, every, decay_rate * steps * through)
    add_rows(gh_ref, 8, every, d_raw)
    dside_ref[:, 2 * NS :] = pltpu.roll(d_raw, place_ref[0], 1)
    drest_ref[:, first_step : first_step + LANES] = d_raw.astype(BF16)
    drest_ref[:, first_step + LANES :] = jnp.zeros(
        (BLK, drest_ref.shape[1] - first_step - LANES), BF16
    )
    d_b = careful(d_scores, c_act) + product(tails[...], dstate[...], NT)
    d_c = careful(d_scores.T, b_act) + product(carries[...], old, NT)
    for part, value in ((0, d_b), (1, d_c)):
        lanes = slice(part * NS, (part + 1) * NS)
        d_conv = value * slopes[part]
        dbs[0:BLK, lanes] = d_conv
        for shift in range(CONV):
            add_rows(gbc_ref, 8 * (CONV - 1 - shift), lanes, d_conv * bc_taps[part][shift])
        add_rows(gbc_ref, 8 * CONV, lanes, d_conv)
        d_in = bcpar_ref[CONV - 1 : CONV, lanes] * d_conv
        for shift in range(1, CONV):
            d_in = d_in + bcpar_ref[CONV - 1 - shift : CONV - shift, lanes] * (
                after[shift - 1] * dbs[shift : shift + BLK, lanes]
            )
        dside_ref[:, lanes] = d_in
        drest_ref[:, width + part * NS : width + (part + 1) * NS] = d_in.astype(BF16)
    dstate[...] = keeps[0:1, :] * dstate[...] + product(c_act.T, carries[...])


def ssd_forward(rest, starts, par, bcpar, hp, sequences):
    rows, width = rest.shape[0], par.shape[1]
    blocks = rows // sequences // BLK
    here = lambda s, b: (s * blocks + b, 0)
    before = lambda s, b: (jnp.maximum((s * blocks + b) * (BLK // 8) - 1, 0), 0)
    fixed = lambda s, b: (0, 0)
    return pl.pallas_call(
        ssd_forward_kernel,
        grid=(sequences, blocks),
        in_specs=[
            pl.BlockSpec((BLK, rest.shape[1]), here),
            pl.BlockSpec((8, rest.shape[1]), before),
            pl.BlockSpec((BLK, LANES), here),
            pl.BlockSpec(par.shape, fixed),
            pl.BlockSpec(bcpar.shape, fixed),
            pl.BlockSpec(hp.shape, fixed),
        ],
        out_specs=[
            pl.BlockSpec((BLK, width), here),
            pl.BlockSpec((1, NS, width), lambda s, b: (s * blocks + b, 0, 0)),
        ],
        out_shape=[
            jax.ShapeDtypeStruct((rows, width), F32),
            jax.ShapeDtypeStruct((sequences * blocks, NS, width), F32),
        ],
        scratch_shapes=[
            pltpu.VMEM((BLK + 8, width), F32),
            pltpu.VMEM((BLK + 8, 2 * NS), F32),
            pltpu.VMEM((NS, width), F32),
            pltpu.VMEM((BLK, width), F32),
            pltpu.VMEM((8, width), F32),
        ],
        compiler_params=pltpu.CompilerParams(vmem_limit_bytes=VMEM_LIMIT),
        cost_estimate=pl.CostEstimate(
            flops=40 * rows * BLK * width, bytes_accessed=20 * rows * width, transcendentals=0
        ),
        name="ssd_forward",
    )(rest, rest, starts, par, bcpar, hp)


def ssd_backward(
    sequence, before_it, place, rest, d_ssd, states, starts, ends, start_row, par, bcpar, hp, pick, sequences
):
    rows, width = d_ssd.shape
    rest_width = rest.shape[1]
    blocks = rows // sequences // BLK
    at = lambda b: sequence * blocks + blocks - 1 - b
    here = lambda b: (at(b), 0)
    before = lambda b: (jnp.maximum(at(b) * (BLK // 8) - 1, 0), 0)
    fixed = lambda b: (0, 0)
    return pl.pallas_call(
        ssd_backward_kernel,
        grid=(blocks,),
        in_specs=[pl.BlockSpec(memory_space=pl.ANY)] * len(before_it)
        + [
            pl.BlockSpec(memory_space=pltpu.SMEM),
            pl.BlockSpec((BLK, rest_width), here),
            pl.BlockSpec((8, rest_width), before),
            pl.BlockSpec((BLK, width), here),
            pl.BlockSpec((1, NS, width), lambda b: (at(b), 0, 0)),
            pl.BlockSpec((BLK, LANES), here),
            pl.BlockSpec((BLK, LANES), here),
            pl.BlockSpec((1, BLK), lambda b: (0, at(b))),
            pl.BlockSpec(par.shape, fixed),
            pl.BlockSpec(bcpar.shape, fixed),
            pl.BlockSpec(hp.shape, fixed),
            pl.BlockSpec(pick.shape, fixed),
        ],
        out_specs=[
            pl.BlockSpec((BLK, rest_width), here),
            pl.BlockSpec((BLK, 2 * NS + LANES), lambda b: (blocks - 1 - b, 0)),
            pl.BlockSpec((8 * (CONV + 2), width), fixed),
            pl.BlockSpec((8 * (CONV + 1), 2 * NS), fixed),
            pl.BlockSpec((16, LANES), fixed),
        ],
        out_shape=[
            jax.ShapeDtypeStruct((rows, rest_width), BF16),
            jax.ShapeDtypeStruct((rows // sequences, 2 * NS + LANES), F32),
            jax.ShapeDtypeStruct((8 * (CONV + 2), width), F32),
            jax.ShapeDtypeStruct((8 * (CONV + 1), 2 * NS), F32),
            jax.ShapeDtypeStruct((16, LANES), F32),
        ],
        scratch_shapes=[
            pltpu.VMEM((BLK + 8, width), F32),
            pltpu.VMEM((BLK + 8, 2 * NS), F32),
            pltpu.VMEM((BLK + 8, width), F32),
            pltpu.VMEM((BLK + 8, 2 * NS), F32),
            pltpu.VMEM((NS, width), F32),
            pltpu.VMEM((BLK, width), F32),
            pltpu.VMEM((BLK, width), F32),
            pltpu.VMEM((2 * BLK + 8, width), F32),
            pltpu.VMEM((LANES, BLK), F32),
            pltpu.VMEM((8, width), F32),
        ],
        input_output_aliases={i: i for i in range(len(before_it))},
        compiler_params=pltpu.CompilerParams(vmem_limit_bytes=VMEM_LIMIT),
        cost_estimate=pl.CostEstimate(
            flops=100 * rows * BLK * width // sequences,
            bytes_accessed=4 * rows * 5 * width // sequences,
            transcendentals=0,
        ),
        name="ssd_backward",
    )(*before_it, place, rest, rest, d_ssd, states, starts, ends, start_row, par, bcpar, hp, pick)


def resident(array):
    return pl.BlockSpec(
        array.shape, lambda *i: (0,) * array.ndim, pipeline_mode=pl.Buffered(buffer_count=1)
    )


def matmul_kernel(left_ref, right_ref, out_ref):
    out_ref[...] = dot(left_ref[...], right_ref[...])


def project(normed, weights):
    rows = normed.shape[0]
    step = min(MID_ROWS, rows)
    width = weights.shape[1]
    here = lambda i: (i, 0)
    return pl.pallas_call(
        matmul_kernel,
        grid=(rows // step,),
        in_specs=[pl.BlockSpec((step, D), here), resident(weights)],
        out_specs=pl.BlockSpec((step, width), here),
        out_shape=jax.ShapeDtypeStruct((rows, width), F32),
        compiler_params=pltpu.CompilerParams(vmem_limit_bytes=VMEM_LIMIT),
        cost_estimate=pl.CostEstimate(
            flops=2 * rows * D * width,
            bytes_accessed=4 * rows * width + 2 * D * (rows + width),
            transcendentals=0,
        ),
        name="project",
    )(normed, weights)


def gate_kernel(normed_ref, cot_ref, wgate_ref, wout_ref, ssd_ref, gain_ref, gate_ref, dh_ref, sums_ref):
    rows, width = ssd_ref.shape
    part = min(PART_ROWS, rows)
    for first in range(0, rows, LANES):
        if first % part == 0:
            now = slice(first, first + part)
            gate_ref[now, :] = dot(normed_ref[now, :], wgate_ref[...])
            dh_ref[now, :] = dot(cot_ref[now, :], wout_ref[...], NT)
        at = slice(first, first + LANES)
        squares = jnp.zeros((LANES, LANES), F32)
        inners = jnp.zeros((LANES, LANES), F32)
        for piece in range(width // LANES):
            lanes = slice(piece * LANES, (piece + 1) * LANES)
            gate = gate_ref[at, lanes]
            gated = ssd_ref[at, lanes] * (gate * sigmoid(gate))
            squares = squares + gated * gated
            inners = inners + dh_ref[at, lanes] * gain_ref[0:1, lanes] * gated
        sums_ref[0:1, at] = jnp.sum(squares.T, axis=0, keepdims=True)
        sums_ref[1:2, at] = jnp.sum(inners.T, axis=0, keepdims=True)
    sums_ref[2:8, :] = jnp.zeros((6, rows), F32)


def gate_project(normed, cotangent, w_gate, w_output, ssd, gain):
    rows, width = ssd.shape
    step = min(MID_ROWS, rows)
    here = lambda i: (i, 0)
    return pl.pallas_call(
        gate_kernel,
        grid=(rows // step,),
        in_specs=[
            pl.BlockSpec((step, D), here),
            pl.BlockSpec((step, D), here),
            resident(w_gate),
            resident(w_output),
            pl.BlockSpec((step, width), here),
            pl.BlockSpec((1, width), lambda i: (0, 0)),
        ],
        out_specs=[
            pl.BlockSpec((step, width), here),
            pl.BlockSpec((step, width), here),
            pl.BlockSpec((8, step), lambda i: (0, i)),
        ],
        out_shape=[
            jax.ShapeDtypeStruct((rows, width), F32),
            jax.ShapeDtypeStruct((rows, width), F32),
            jax.ShapeDtypeStruct((8, rows), F32),
        ],
        compiler_params=pltpu.CompilerParams(vmem_limit_bytes=VMEM_LIMIT),
        cost_estimate=pl.CostEstimate(
            flops=4 * rows * D * width, bytes_accessed=16 * rows * width, transcendentals=0
        ),
        name="gate_project",
    )(normed, cotangent, w_gate, w_output, ssd, gain)


def gated_kernel(
    core_ref, ssd_ref, gate_ref, dh_ref, sums_ref, gain_ref, wout_ref,
    hidden_ref, dgate_ref, dssd_ref, gain_out, sent_ref, kept_ref,
):
    @pl.when(pl.program_id(0) == 0)
    def _():
        gain_out[...] = jnp.zeros_like(gain_out)

    width = ssd_ref.shape[1]
    rows = ssd_ref.shape[0]
    scale = lax.rsqrt(sums_ref[0:1, :] / DI + EPS)
    shift = scale * scale * scale * (sums_ref[1:2, :] / DI)
    turned = jnp.concatenate([scale] * 8 + [shift] * 8 + [jnp.zeros((LANES - 16, rows), F32)], axis=0).T
    chunk = min(64, rows)
    part = min(PART_ROWS, rows)
    sending = pl.program_id(0) < pl.num_programs(0) // 2
    for first in range(0, rows, chunk):
        at = slice(first, first + chunk)
        scales = wide(turned[at, 0:1], (chunk, LANES))
        shifts = wide(turned[at, 8:9], (chunk, LANES))
        for piece in range(width // LANES):
            lanes = slice(piece * LANES, (piece + 1) * LANES)
            gate = gate_ref[at, lanes]
            ssd = ssd_ref[at, lanes]
            d_hidden = dh_ref[at, lanes]
            gain = gain_ref[0:1, lanes]
            sig = sigmoid(gate)
            act = gate * sig
            gated = ssd * act
            unit = gated * scales
            hidden_ref[at, lanes] = (unit * gain).astype(BF16)
            gain_out[:, lanes] += jnp.sum((d_hidden * unit).reshape(chunk // 8, 8, LANES), axis=0)
            d_gated = scales * (d_hidden * gain) - gated * shifts
            dssd_ref[at, lanes] = d_gated * act
            dgate_ref[at, lanes] = (
                d_gated * ssd * (sig * (1.0 + gate * (1.0 - sig)))
            ).astype(BF16)
        done = first + chunk
        if done % part == 0:
            now = slice(done - part, done)
            mixed = dot(hidden_ref[now, :], wout_ref[...]).astype(BF16)
            sent_ref[now, :] = jnp.where(sending, mixed, sent_ref[now, :])
            kept_ref[now, :] = jnp.where(sending, kept_ref[now, :], mixed)


def gated_pass(core, ssd, gate, d_hidden, sums, gain, w_output):
    rows, width = ssd.shape
    step = min(MID_ROWS, rows // 2)
    steps = rows // step // 2

    def at(i, core):
        half = jnp.where(i < steps, 1 - core[0], core[0])
        return half * steps + i % steps

    here = lambda i, core: (at(i, core), 0)
    fixed = lambda i, core: (0, 0)
    return pl.pallas_call(
        gated_kernel,
        grid_spec=pltpu.PrefetchScalarGridSpec(
            num_scalar_prefetch=1,
            grid=(2 * steps,),
            in_specs=[
                pl.BlockSpec((step, width), here),
                pl.BlockSpec((step, width), here),
                pl.BlockSpec((step, width), here),
                pl.BlockSpec((8, step), lambda i, core: (0, at(i, core))),
                pl.BlockSpec((1, width), fixed),
                resident(w_output),
            ],
            out_specs=[
                pl.BlockSpec((step, width), here),
                pl.BlockSpec((step, width), here),
                pl.BlockSpec((step, width), here),
                pl.BlockSpec((8, width), fixed),
                pl.BlockSpec((step, D), lambda i, core: (jnp.minimum(i, steps - 1), 0)),
                pl.BlockSpec((step, D), lambda i, core: (jnp.maximum(i - steps, 0), 0)),
            ],
        ),
        out_shape=[
            jax.ShapeDtypeStruct((rows, width), BF16),
            jax.ShapeDtypeStruct((rows, width), BF16),
            jax.ShapeDtypeStruct((rows, width), F32),
            jax.ShapeDtypeStruct((8, width), F32),
            jax.ShapeDtypeStruct((rows // 2, D), BF16),
            jax.ShapeDtypeStruct((rows // 2, D), BF16),
        ],
        compiler_params=pltpu.CompilerParams(vmem_limit_bytes=VMEM_LIMIT),
        cost_estimate=pl.CostEstimate(
            flops=2 * rows * width * D, bytes_accessed=20 * rows * width, transcendentals=0
        ),
        name="gated_pass",
    )(core, ssd, gate, d_hidden, sums, gain, w_output)


def unit_rows(tokens):
    rows = tokens.astype(F32)
    inverse = lax.rsqrt(jnp.mean(rows * rows, axis=1, keepdims=True) + EPS)
    return rows, inverse


def normed_grad_kernel(half_ref, dgate_ref, drest_ref, tokens_ref, wgate_ref, wrest_ref, out_ref, gain_out):
    @pl.when(pl.program_id(0) == 0)
    def _():
        gain_out[...] = jnp.zeros_like(gain_out)

    rows = tokens_ref.shape[0]
    part = min(PART_ROWS, rows)
    for first in range(0, rows, part):
        now = slice(first, first + part)
        total = dot(dgate_ref[now, :], wgate_ref[...], NT) + dot(drest_ref[now, :], wrest_ref[...], NT)
        out_ref[now, :] = total.astype(BF16)
        values, inverse = unit_rows(tokens_ref[now, :])
        weighted = total * (values * inverse)
        gain_out[...] += jnp.sum(weighted.reshape(-1, 8, D), axis=0)


def normed_grad(half, weight, d_gate, d_rest, tokens, w_gate, w_rest):
    rows = tokens.shape[0]
    step = min(MID_ROWS, rows // 2)
    steps = rows // step // 2
    here = lambda i, half: (half[0] * steps + i, 0)
    return pl.pallas_call(
        normed_grad_kernel,
        grid_spec=pltpu.PrefetchScalarGridSpec(
            num_scalar_prefetch=1,
            grid=(steps,),
            in_specs=[
                pl.BlockSpec((step, d_gate.shape[1]), here),
                pl.BlockSpec((step, d_rest.shape[1]), here),
                pl.BlockSpec((step, D), here),
                resident(w_gate),
                resident(w_rest),
            ],
            out_specs=[
                pl.BlockSpec((step, D), lambda i, half: (i, 0)),
                pl.BlockSpec((8, D), lambda i, half: (0, 0)),
            ],
        ),
        out_shape=[
            jax.ShapeDtypeStruct((rows // 2, D), BF16),
            jax.ShapeDtypeStruct((8, D), F32),
        ],
        compiler_params=pltpu.CompilerParams(vmem_limit_bytes=VMEM_LIMIT),
        cost_estimate=pl.CostEstimate(
            flops=weight * rows * D * (d_gate.shape[1] + d_rest.shape[1]),
            bytes_accessed=weight * 6 * rows * D,
            transcendentals=0,
        ),
        name="normed_grad",
    )(half, d_gate, d_rest, tokens, w_gate, w_rest)


def input_grad_kernel(core_ref, own_ref, other_ref, tokens_ref, cot_ref, gain_ref, out_ref, terms):
    steps = pl.num_programs(0) // 2
    mine = pl.program_id(0) // steps == core_ref[0]

    @pl.when(mine)
    def _():
        terms[...] = own_ref[...].astype(F32)

    @pl.when(jnp.logical_not(mine))
    def _():
        terms[...] = other_ref[...].astype(F32)

    rows, inverse = unit_rows(tokens_ref[...])
    weighted = terms[...] * gain_ref[0:1, :]
    inner = jnp.mean(weighted * rows, axis=1, keepdims=True)
    out_ref[...] = (
        cot_ref[...].astype(F32) + inverse * weighted - rows * (inverse * inverse * inverse * inner)
    )


def input_grads(core, own, other, tokens, cotangent, gain):
    rows = tokens.shape[0]
    step = min(MID_ROWS, rows // 2)
    steps = rows // step // 2
    here = lambda i, core: (i, 0)

    def part_at(is_own):
        def index(i, core):
            wanted = (i // steps == core[0]) == is_own
            parked = jnp.where((core[0] == 0) == is_own, steps - 1, 0)
            return (jnp.where(wanted, i % steps, parked), 0)

        return index

    return pl.pallas_call(
        input_grad_kernel,
        grid_spec=pltpu.PrefetchScalarGridSpec(
            num_scalar_prefetch=1,
            grid=(2 * steps,),
            in_specs=[
                pl.BlockSpec((step, D), part_at(True)),
                pl.BlockSpec((step, D), part_at(False)),
                pl.BlockSpec((step, D), here),
                pl.BlockSpec((step, D), here),
                pl.BlockSpec((1, D), lambda i, core: (0, 0)),
            ],
            out_specs=pl.BlockSpec((step, D), here),
            scratch_shapes=[pltpu.VMEM((step, D), F32)],
        ),
        out_shape=jax.ShapeDtypeStruct((rows, D), F32),
        compiler_params=pltpu.CompilerParams(vmem_limit_bytes=VMEM_LIMIT),
        cost_estimate=pl.CostEstimate(
            flops=0, bytes_accessed=10 * rows * D, transcendentals=0
        ),
        name="input_grads",
    )(core, own, other, tokens, cotangent, gain)


def held_rows(first):
    return (pl.ds(pl.multiple_of(first, COPY_ROWS), TILE), slice(None))


def band_tiles(ref):
    columns = ref.shape[1] // TILE
    for tile in range(columns * (ref.shape[0] // TILE)):
        down, across = tile // columns, tile % columns
        yield tile, (
            slice(down * TILE, (down + 1) * TILE),
            slice(across * TILE, (across + 1) * TILE),
        )


def copied(first, helds, ref, at):
    past = 0
    for held_ref in helds:
        size = held_ref.shape[0]
        if len(helds) == 1:
            ref[at] = held_ref[held_rows(first)]
        else:

            @pl.when((first >= past) & (first < past + size))
            def _(held_ref=held_ref, past=past):
                ref[at] = held_ref[held_rows(first - past)]

        past += size


def assemble_kernel(parts, width, rows_ref, *refs):
    helds = refs[:parts]
    band = pl.program_id(0)
    outs = refs[parts:]
    if width:
        outs[1][:, width:] = outs[0][...]
        outs = (outs[1].at[:, 0:width],)
    base = 0
    for ref in outs:
        count = (ref.shape[0] // TILE) * (ref.shape[1] // TILE)
        for tile, at in band_tiles(ref):
            copied(rows_ref[base + band * count + tile], helds, ref, at)
        base += count * pl.num_programs(0)


def assemble(rows, helds, side_cols, shapes):
    bands = min(shape[0] for shape in shapes) // TILE
    bands = min(bands, 8)
    here = lambda i: (i, 0)
    width = shapes[0][1] - side_cols[0].shape[1] if side_cols else 0
    return pl.pallas_call(
        functools.partial(assemble_kernel, len(helds), width),
        grid=(bands,),
        in_specs=[pl.BlockSpec(memory_space=pltpu.SMEM)]
        + [resident(held) for held in helds]
        + [pl.BlockSpec((side.shape[0] // bands, side.shape[1]), here) for side in side_cols],
        out_specs=[pl.BlockSpec((shape[0] // bands, shape[1]), here) for shape in shapes],
        out_shape=[jax.ShapeDtypeStruct(shape, BF16) for shape in shapes],
        compiler_params=pltpu.CompilerParams(vmem_limit_bytes=VMEM_LIMIT),
        cost_estimate=pl.CostEstimate(
            flops=0, bytes_accessed=4 * sum(held.size for held in helds), transcendentals=0
        ),
        name="assemble",
    )(rows, *helds, *side_cols)


def spread_kernel(rows_ref, *refs):
    out_ref = refs[-1]
    band = pl.program_id(0)
    base = 0
    for ref in refs[:-1]:
        count = (ref.shape[0] // TILE) * (ref.shape[1] // TILE)
        for tile, place in band_tiles(ref):
            first = rows_ref[base + band * count + tile]

            @pl.when(first >= 0)
            def _(first=first, place=place, ref=ref):
                out_ref[held_rows(first)] = ref[place]

        base += count * pl.num_programs(0)


def spread(grad_rows, grads, total_rows):
    bands = min(grad.shape[0] for grad in grads) // TILE
    return pl.pallas_call(
        spread_kernel,
        grid=(bands,),
        in_specs=[pl.BlockSpec(memory_space=pltpu.SMEM)]
        + [pl.BlockSpec((grad.shape[0] // bands, grad.shape[1]), lambda i: (i, 0)) for grad in grads],
        out_specs=pl.BlockSpec((total_rows, TILE), lambda i: (0, 0)),
        out_shape=jax.ShapeDtypeStruct((total_rows, TILE), BF16),
        compiler_params=pltpu.CompilerParams(vmem_limit_bytes=VMEM_LIMIT),
        cost_estimate=pl.CostEstimate(
            flops=0,
            bytes_accessed=2 * total_rows * TILE + sum(2 * grad.size for grad in grads),
            transcendentals=0,
        ),
        name="spread",
    )(grad_rows, *grads)


def update_kernel(
    rows_ref, early_ref, late_ref, repair_ref, tiles_ref, lstat_ref, rstat_ref, lroot_ref, rroot_ref,
    grads_out, left_out, right_out, tiles_out, copy_out, grad_tile,
):
    dot = functools.partial(lax.dot_general, dimension_numbers=NN, preferred_element_type=F32)
    step = tiles_ref.shape[0]
    for tile in range(step):
        first = rows_ref[pl.program_id(0) * step + tile]
        past = 0
        for source in (early_ref, late_ref, repair_ref):
            size = source.shape[0]

            @pl.when((first >= past) & (first < past + size))
            def _(source=source, past=past, tile=tile):
                grad_tile[tile] = source[held_rows(first - past)]

            past += size
    for tile in range(step):
        exact_grad = grad_tile[tile]
        grad = exact_grad.astype(BF16)
        turned = exact_grad.T.astype(BF16)
        grads_out[tile] = exact_grad
        left_out[tile] = STAT_DECAY * lstat_ref[tile] + (1.0 - STAT_DECAY) * dot(grad, turned)
        right_out[tile] = STAT_DECAY * rstat_ref[tile] + (1.0 - STAT_DECAY) * dot(turned, grad)
        shaped = careful(careful(lroot_ref[tile], exact_grad), rroot_ref[tile])
        updated = tiles_ref[tile] - LR_MAT * shaped
        tiles_out[tile] = updated
        copy_out[tile] = updated.astype(BF16)


def update_tiles(rows, early, late, repair, tiles, left_stats, right_stats, left_roots, right_roots):
    count = tiles.shape[0]
    step = TILES_STEP if count % TILES_STEP == 0 else 1
    spec = pl.BlockSpec((step, TILE, TILE), lambda i, rows: (i, 0, 0))
    sources = [pl.BlockSpec(part.shape, lambda i, rows: (0, 0)) for part in (early, late, repair)]
    whole = jax.ShapeDtypeStruct(tiles.shape, F32)
    return pl.pallas_call(
        update_kernel,
        grid_spec=pltpu.PrefetchScalarGridSpec(
            num_scalar_prefetch=1,
            grid=(count // step,),
            in_specs=sources + [spec] * 5,
            out_specs=[spec] * 5,
            scratch_shapes=[pltpu.VMEM((step, TILE, TILE), F32)],
        ),
        out_shape=[whole] * 4 + [jax.ShapeDtypeStruct(tiles.shape, BF16)],
        compiler_params=pltpu.CompilerParams(vmem_limit_bytes=VMEM_LIMIT),
        cost_estimate=pl.CostEstimate(
            flops=18 * count * TILE**3, bytes_accessed=42 * count * TILE**2, transcendentals=0
        ),
        name="update_tiles",
    )(rows, early, late, repair, tiles, left_stats, right_stats, left_roots, right_roots)


def fetch_plan(slot_map, own_tiles, side_rows):
    count = slot_map.shape[0]
    tiles = jnp.arange(count, dtype=jnp.int32)
    waits = tiles // (count // 3) != 1
    key = tiles + waits * count
    owner = slot_map // own_tiles
    together = owner[:, None] == owner[None, :]
    place = jnp.sum(together & (key[None, :] < key[:, None]), axis=1, dtype=jnp.int32)
    first = max(1, own_tiles * 13 // 24)
    first_rows, second_rows = first * TILE + side_rows, (own_tiles - first) * TILE
    early = place < first
    owners = count // own_tiles
    rows = jnp.where(
        early,
        owner * first_rows + place * TILE,
        owners * first_rows + owner * second_rows + (place - first) * TILE,
    )
    rank = lax.axis_index("dp")
    places = jnp.arange(own_tiles, dtype=jnp.int32)
    order = jnp.sum(
        jnp.where(
            (owner == rank)[None, :] & (place[None, :] == places[:, None]),
            slot_map[None, :] - rank * own_tiles,
            0,
        ),
        axis=1,
        dtype=jnp.int32,
    )
    return rows, order, first, jnp.any(~waits & ~early)


def tile_plan(slot_map, own_tiles):
    count = slot_map.shape[0]
    tiles = jnp.arange(count, dtype=jnp.int32)
    kind = tiles // (count // 3)
    waits = kind == 1
    key = tiles + waits * count
    owner = slot_map // own_tiles
    together = owner[:, None] == owner[None, :]
    first = own_tiles // 2
    last = min(own_tiles, own_tiles - first + SLACK)
    place = jnp.sum(together & (key[None, :] < key[:, None]), axis=1, dtype=jnp.int32)
    early = (place < first) & ~waits
    behind = jnp.sum(
        together & ~early[None, :] & (key[None, :] < key[:, None]), axis=1, dtype=jnp.int32
    )
    late = ~early & (behind < last)
    repair = ~early & ~late

    def rows_where(chosen, position, rows):
        return jnp.where(chosen, owner * rows + position * TILE, -1)

    early_rows, late_rows = first * TILE, last * TILE
    plans = (
        (rows_where(early, place, early_rows), early_rows),
        (rows_where(late, behind, late_rows), late_rows),
        (rows_where(repair, behind - last, early_rows), early_rows),
    )
    in_owner = jnp.where(early, place, first + behind) * TILE
    rank = lax.axis_index("dp")
    slots = rank * own_tiles + jnp.arange(own_tiles, dtype=jnp.int32)
    own_rows = jnp.sum(
        jnp.where(slot_map[None, :] == slots[:, None], in_owner[None, :], 0), axis=1, dtype=jnp.int32
    )
    return plans, own_rows, jnp.any(repair).astype(F32)


def on_device(
    tokens,
    cotangent,
    doc_ids,
    tile_slots,
    matrix_tiles,
    left_stats,
    right_stats,
    left_roots,
    right_roots,
    side_weight,
    side_moment,
    side_second,
    vector_params,
    vector_moment,
    vector_second,
):
    n_tensor = lax.axis_size("tensor")
    n_dp = lax.axis_size("dp")
    tensor_rank = lax.axis_index("tensor")
    core = tensor_rank % 2
    di_local = DI // n_tensor
    heads_local = HEADS // n_tensor
    model_local = D // n_tensor
    bc_local = 2 * NS // n_tensor
    rows = tokens.shape[0]
    half = rows // 2
    sequences, seq_len = doc_ids.shape
    slot_map = tile_slots[0]
    own_tiles = matrix_tiles.shape[1]
    side_rows = side_weight.shape[0] * SIDE // TILE
    fetch_rows, order, first_tiles, misfetch = fetch_plan(
        slot_map, own_tiles, side_rows
    )
    plans, own_rows, misfit = tile_plan(slot_map, own_tiles)
    misfits = sum_over(jnp.full((8, LANES), misfit), "tensor")
    vector = vector_params[0]
    bounds = segment_bounds(di_local, heads_local, model_local, bc_local, CONV)

    def segment_of(index):
        return vector[bounds[index] : bounds[index + 1]]

    conv_kernel = segment_of(0).reshape(CONV, di_local)
    conv_offset = segment_of(1)
    gate_gain = segment_of(2)
    log_rate = segment_of(3)
    skip_gain = segment_of(4)
    dt_offset = segment_of(5)

    mine = matrix_tiles[0].astype(BF16)[order].reshape(own_tiles * TILE, TILE)
    cut = first_tiles * TILE
    first_share = jnp.concatenate(
        [mine[:cut], side_weight.astype(BF16).reshape(side_rows, TILE)], axis=0
    )
    first_held = lax.all_gather(first_share, "dp", axis=0, tiled=True)
    second_held = lax.all_gather(mine[cut:], "dp", axis=0, tiled=True)
    shared = lax.all_gather(vector[bounds[6] :][None, :], "tensor", axis=0, tiled=True)
    pre_gain = shared[:, :model_local].reshape(D)
    bc_kernel = (
        shared[:, model_local : model_local + CONV * bc_local]
        .reshape(n_tensor, CONV, bc_local)
        .transpose(1, 0, 2)
        .reshape(CONV, 2 * NS)
    )
    bc_offset = shared[:, model_local + CONV * bc_local :].reshape(2 * NS)
    par = jnp.concatenate(
        [
            conv_kernel,
            conv_offset[None],
            jnp.repeat(skip_gain, di_local // heads_local)[None],
            gate_gain[None],
            jnp.zeros((1, di_local), F32),
        ],
        axis=0,
    )
    bcpar = jnp.concatenate([bc_kernel, bc_offset[None], jnp.zeros((3, 2 * NS), F32)], axis=0)
    decay_rate = -jnp.exp(log_rate)
    hp = jnp.pad(
        jnp.stack([dt_offset, decay_rate * LOG2E, decay_rate]), ((0, 5), (0, LANES - heads_local))
    )
    pick = (
        jnp.arange(di_local)[:, None] // (di_local // heads_local) == jnp.arange(LANES)[None, :]
    ).astype(BF16)
    starts = jnp.sum(doc_ids[:, None, :] < doc_ids[:, :, None], axis=2).astype(F32).reshape(rows)
    ends = jnp.sum(doc_ids[:, None, :] <= doc_ids[:, :, None], axis=2).astype(F32).reshape(rows)
    start_row = starts[None, :]
    start_wide = jnp.broadcast_to(starts[:, None], (rows, LANES))
    end_wide = jnp.broadcast_to(ends[:, None], (rows, LANES))

    residual = tokens.astype(F32)
    inverse = lax.rsqrt(jnp.mean(residual * residual, axis=1, keepdims=True) + EPS)
    normed = (residual * inverse * pre_gain).astype(BF16)
    normed, misfits = tied(normed, misfits)
    misfit = misfits[0, 0] > 0.0

    side_copy = first_held.reshape(n_dp, -1, TILE)[:, cut:].reshape(D, SIDE)
    side_cols = jnp.concatenate(
        [
            side_copy[:, : 2 * NS],
            lax.dynamic_slice_in_dim(side_copy, 2 * NS + tensor_rank * heads_local, heads_local, 1),
            jnp.zeros((D, 2 * NS - heads_local), BF16),
        ],
        axis=1,
    )
    per_block = (D // TILE) * (di_local // TILE)
    rest_shape = ((D, di_local + side_cols.shape[1]),)

    rest_rows = fetch_rows[per_block : 2 * per_block]

    def forward_with(rows, helds):
        weights = assemble(rows, helds, (side_cols,), rest_shape)[0]
        projected = project(normed, weights)
        scanned = ssd_forward(projected, start_wide, par, bcpar, hp, sequences)
        return (weights, projected, *scanned)

    tried = forward_with(
        jnp.minimum(rest_rows, first_held.shape[0] - TILE), (first_held,)
    )
    tried, second_held = tied(tried, second_held)
    w_rest, rest, ssd, states = lax.while_loop(
        lambda carry: carry[0],
        lambda carry: (False, forward_with(rest_rows, (first_held, second_held))),
        (misfetch, tried),
    )[1]
    w_gate, w_output = assemble(
        jnp.concatenate([fetch_rows[:per_block], fetch_rows[2 * per_block :]]),
        (first_held, second_held),
        (),
        ((D, di_local), (di_local, D)),
    )
    gate, d_hidden, sums = gate_project(
        normed, cotangent, w_gate, w_output, ssd, gate_gain[None, :]
    )
    sums = sum_over(sums, "tensor")
    core_at = core[None].astype(jnp.int32)
    hidden, d_gate, d_ssd, gain_sums, out_sent, out_kept = gated_pass(
        core_at, ssd, gate, d_hidden, sums, gate_gain[None, :], w_output
    )

    def chip_sum(kept, sent):
        return (kept.astype(F32) + swap(sent, "tensor", 1).astype(F32)).astype(BF16)

    out_chip = chip_sum(out_kept, out_sent)
    grad_output = contract_rows(hidden, cotangent).astype(BF16)
    out_chip, normed_now = tied(out_chip, normed)
    out_others = [swap(part, "tensor", 2) for part in jnp.split(out_chip, 2)]
    grad_gate = contract_rows(normed_now, d_gate).astype(BF16)
    early_grads = spread(
        jnp.concatenate([plans[0][0][:per_block], plans[0][0][2 * per_block :]]),
        (grad_gate, grad_output),
        n_dp * plans[0][1],
    )
    d_ssd, early_grads = tied(d_ssd, early_grads)
    early = OwnerSum(early_grads, ((0, 1), (2, 3)))
    given = (states, start_wide, end_wide, start_row, par, bcpar, hp, pick, sequences)
    place = (tensor_rank * heads_local).astype(jnp.int32)[None]
    back, parts, side_parts = (), [], []
    for sequence in range(sequences):
        d_rest, d_side, *sums_here = ssd_backward(sequence, back, place, rest, d_ssd, *given)
        parts.append(sums_here)
        if sequence == 0:
            d_rest, out_others[0] = early.first((d_rest, out_others[0]))
        else:
            d_rest, side_parts[-1] = tied(d_rest, side_parts[-1])
        side_parts.append((d_side, swap(d_side, "tensor", 1)))
        back = (d_rest,)
    gx, gbc, gh = (sum(terms) for terms in zip(*parts))
    d_rest, out_others[1] = early.second((back[0], out_others[1]))

    split_side = sequences // 2
    side_chips = [
        jnp.concatenate([(own + other).astype(BF16) for own, other in part], axis=0)
        for part in (side_parts[:split_side], side_parts[split_side:])
    ]
    d_rest, side_chips[0] = tied(d_rest, side_chips[0])
    side_others = [swap(side_chips[0], "tensor", 2)]
    d_sent, pre_sent = normed_grad(1 - core_at, 16, d_gate, d_rest, tokens, w_gate, w_rest)
    d_sent, side_chips[1], side_others[0], d_rest = early.third(
        (d_sent, side_chips[1], side_others[0], d_rest)
    )
    side_others.append(swap(side_chips[1], "tensor", 2))
    grad_input = contract_rows(normed, d_rest[:, :di_local]).astype(BF16)
    late_grads = spread(plans[1][0], (grad_gate, grad_input, grad_output), n_dp * plans[1][1])
    early_share, (late_grads, side_others[1], d_rest) = early.total(
        (late_grads, side_others[1], d_rest)
    )
    late = OwnerSum(late_grads, ((0,), (1,), (2,), (3,)))
    d_kept, pre_kept = normed_grad(core_at, 16, d_gate, d_rest, tokens, w_gate, w_rest)
    d_kept, pre_kept = late.first((d_kept, pre_kept))
    grad_pre = jnp.sum(pre_sent + pre_kept, axis=0)
    d_chip = chip_sum(d_kept, d_sent)
    d_others = [swap(part, "tensor", 2) for part in jnp.split(d_chip, 4)]
    d_others[0], side_chips, side_others, out_chip, out_others = late.second(
        (d_others[0], side_chips, side_others, out_chip, out_others)
    )

    side_total = jnp.concatenate(
        [
            (own.astype(F32) + other.astype(F32)).astype(BF16)
            for own, other in zip(side_chips, side_others)
        ],
        axis=0,
    )
    grad_side = lax.dynamic_index_in_dim(
        contract_rows(normed, side_total).reshape(n_dp, n_tensor, -1, side_total.shape[1]),
        tensor_rank,
        1,
        keepdims=False,
    )[:, :, :SIDE]
    gx_sums = jnp.sum(gx.reshape(CONV + 2, 8, di_local), axis=1)
    gbc_sums = jnp.sum(gbc.reshape(CONV + 1, 8, 2 * NS), axis=1)
    gh_sums = jnp.sum(gh.reshape(2, 8, LANES), axis=1)[:, :heads_local]
    own_vector = jnp.concatenate(
        [
            gx_sums[: CONV + 1].reshape(-1),
            jnp.sum(gain_sums, axis=0),
            gh_sums[0],
            jnp.sum(gx_sums[CONV + 1].reshape(heads_local, -1), axis=1),
            gh_sums[1],
        ]
    )
    small_sums = SharedSums(
        grad_side.reshape(n_dp, -1), jnp.concatenate([own_vector, grad_pre, gbc_sums.reshape(-1)])
    )
    d_others[1] = late.third(d_others[1])
    late_share, (d_others[2], misfit, small_sums.owned, small_sums.shared) = late.total(
        (d_others[2], misfit, small_sums.owned, small_sums.shared)
    )

    def repaired(grads):
        again = spread(plans[2][0], grads, n_dp * plans[2][1])
        return lax.psum_scatter(again, "dp", scatter_dimension=0, tiled=True).astype(F32)

    repair_share = lax.cond(
        misfit,
        repaired,
        lambda grads: jnp.zeros((plans[2][1], TILE), F32),
        (grad_gate, grad_input, grad_output),
    )

    tile_share, left_new, right_new, tiles_new, tiles_copy = update_tiles(
        own_rows,
        early_share,
        late_share,
        repair_share,
        matrix_tiles[0],
        left_stats[0],
        right_stats[0],
        left_roots[0],
        right_roots[0],
    )
    arrived, tiles_copy = tied(small_sums.send(), tiles_copy)
    small_sums.add(arrived)
    small_sums.finish()
    split_at = own_vector.shape[0]
    side_own, all_vector = small_sums.owned, small_sums.shared
    quarters = jnp.where(
        (jnp.arange(n_tensor) == tensor_rank)[:, None], side_own, jnp.zeros((), F32)
    )
    common = jnp.concatenate([quarters.reshape(-1), all_vector[split_at:]])[None]
    common = common + swap(common, "tensor", 1)
    common_other = swap(common, "tensor", 2)
    d_half = (d_chip.astype(F32) + jnp.concatenate(d_others).astype(F32)).astype(BF16)
    input_grad = input_grads(
        core_at, d_half, swap(d_half, "tensor", 1), tokens, cotangent, pre_gain[None, :]
    )
    common_other, input_grad = tied(common_other, input_grad)
    common = (common + common_other)[0]
    side_share = common[: side_weight.size].reshape(side_weight.shape)
    common = common[side_weight.size :]
    quarter = half // 2
    mixed_own = [
        (
            lax.dynamic_slice_in_dim(tokens, core * half + i * quarter, quarter, 0).astype(F32)
            + (out_chip[i * quarter : (i + 1) * quarter].astype(F32) + out_others[i].astype(F32))
        ).astype(BF16)
        for i in range(2)
    ]
    mixed_other = [swap(part, "tensor", 1) for part in mixed_own]
    lower_half = core == 0
    mixed = jnp.concatenate(
        [jnp.where(lower_half, own, other) for own, other in zip(mixed_own, mixed_other)]
        + [jnp.where(lower_half, other, own) for own, other in zip(mixed_own, mixed_other)],
        axis=0,
    )

    pre_share = lax.dynamic_slice_in_dim(common[:D], tensor_rank * model_local, model_local, 0)
    bc_share = lax.dynamic_slice_in_dim(
        common[D:].reshape(CONV + 1, 2 * NS), tensor_rank * bc_local, bc_local, 1
    )
    vector_total = jnp.concatenate([all_vector[:split_at], pre_share, bc_share.reshape(-1)])[None]

    side_m, side_v, side_new = adam_update(
        side_weight, side_moment, side_second, side_share, LR_SIDE
    )
    vec_m, vec_v, vec_new = adam_update(
        vector_params, vector_moment, vector_second, vector_total, LR_VEC
    )
    return (
        mixed,
        input_grad,
        tile_share[None],
        left_new[None],
        right_new[None],
        tiles_new[None],
        tiles_copy[None],
        side_m,
        side_v,
        side_new,
        vec_m,
        vec_v,
        vec_new,
    )


def solution(mesh):
    by_dp = P("dp", None)
    by_tensor = P("tensor", None)
    by_tile = P("tensor", "dp", None, None)
    return jax.shard_map(
        on_device,
        mesh=mesh,
        in_specs=(by_dp,) * 3
        + (by_tensor,)
        + (by_tile,) * 5
        + (by_dp,) * 3
        + (by_tensor,) * 3,
        out_specs=(by_dp,) * 2 + (by_tile,) * 5 + (by_dp,) * 3 + (by_tensor,) * 3,
        check_vma=False,
    )
```
